128 devices in a mesh: ctx: 8 (over z_lo, x), head: 16 (over z_hi, y, core).
Axes of the slice: x: 4, y: 4, z: 4 (z_hi: 2, z_lo: 2; z = z_hi * 2 + z_lo), core: 2. Of those that a mesh axis runs over, the one named last changes fastest.
Arguments:
- query_rows: bfloat16 [24576, 5120], P('ctx', 'head'), may hold values from -20 to 20
- key_rows: bfloat16 [24576, 5120], P('ctx', 'head'), may hold values from -20 to 20
- value_rows: bfloat16 [24576, 5120], P('ctx', 'head'), may hold values from -6 to 6
- gate_rows: bfloat16 [24576, 5120], P('ctx', 'head'), may hold values from -6 to 6
- token_rates: float32 [16, 24576], P('head', 'ctx'), may hold values from 0.05 to 1
- step_sizes: float32 [16], P('head'), may hold values from 0.2 to 2
- fast_first: bfloat16 [16, 320, 640], P('head'), may hold values from -0.3125 to 0.3125
- fast_third: bfloat16 [16, 320, 640], P('head'), may hold values from -0.3125 to 0.3125
- fast_second: bfloat16 [16, 640, 320], P('head'), may hold values from -0.25 to 0.25
- norm_gain: float32 [5120], replicated, may hold values from 0.5 to 1.5
Outputs:
- gated_output: bfloat16 [24576, 5120], P(('ctx', 'head'))
The draws below stay inside these ranges and needn't reach their ends.
All inputs are finite; a program needn't handle non-finite values.
Results may differ from the reference program's by a relative error of at most 0.019.
Values may be sent and summed in bfloat16 or wider, within the bound.
No kernel may reach another device: no remote copies, remote signals or barrier semaphores. Data moves between devices by JAX's collectives and lax.ppermute only.
A program may use at most 128 MiB of HBM per device.

```python
import math
import jax
import jax.numpy as jnp
from jax import lax

TOK_DEV = 3072
HD = 320
FH = 640
ATT_DIM = 160
WINDOW = 1024
NS_ITERS = 5
HEADS = 16
D = 5120
SEQ = 24576
GROUP = 12288
N_CTX = 8


def draw_query_rows(key, part):
    key = jax.random.fold_in(key, 1)
    return (1.2 * jnp.clip(jax.random.normal(key, (SEQ, D), jnp.float32), -5.0, 5.0)).astype(jnp.bfloat16)


def draw_key_rows(key, part):
    key = jax.random.fold_in(key, 2)
    return (1.2 * jnp.clip(jax.random.normal(key, (SEQ, D), jnp.float32), -5.0, 5.0)).astype(jnp.bfloat16)


def block_scale(key, dims, cuts, smallest, top_value):
    loudness = 1.0
    for axis_at, shards_of in cuts:
        steps = jax.random.uniform(jax.random.fold_in(jax.random.fold_in(key, 6), axis_at), (shards_of,), jnp.float32, smallest / len(cuts), top_value / len(cuts))
        loudness = loudness * jnp.repeat(jnp.exp(steps), dims[axis_at] // shards_of).reshape((-1,) + (1,) * (len(dims) - 1 - axis_at))
    return loudness


def bell_draw(own_key, extent, scale, limit, cuts=(), dtype=jnp.bfloat16):
    level = block_scale(own_key, extent, cuts, -0.22, 0.18) if cuts else 1.0
    values = jax.random.normal(own_key, extent, jnp.float32) * scale * level
    return jnp.minimum(jnp.maximum(values, -limit), limit).astype(dtype)


def setup_inputs(seed: int = 0) -> dict:
    arg_keys = jax.random.split(jax.random.key(seed), 11)
    return {
        "query_rows": draw_query_rows(jax.random.fold_in(arg_keys[10], 71), 0),
        "key_rows": draw_key_rows(jax.random.fold_in(arg_keys[10], 71), 0),
        "value_rows": bell_draw(arg_keys[2], (SEQ, D), 1.0, 6.0, ((0, 8), (1, 16))),
        "gate_rows": bell_draw(arg_keys[3], (SEQ, D), 1.0, 6.0, ((0, 8), (1, 16))),
        "token_rates": jnp.clip(jnp.exp(math.log(1.0) - 2.9957323 * jax.random.uniform(arg_keys[4], (HEADS, SEQ), jnp.float32) ** block_scale(arg_keys[4], (HEADS, SEQ), ((0, 16), (1, 8)), -0.2, 0.2)), 0.05, 1.0),
        "step_sizes": jnp.clip(jnp.exp(math.log(2.0) - 2.3025851 * jax.random.uniform(arg_keys[5], (HEADS,), jnp.float32) ** block_scale(arg_keys[5], (HEADS,), ((0, 16),), -0.2, 0.2)), 0.2, 2.0),
        "fast_first": bell_draw(arg_keys[6], (HEADS, HD, FH), HD ** -0.5, 0.3125, ((0, 16),)),
        "fast_third": bell_draw(arg_keys[7], (HEADS, HD, FH), HD ** -0.5, 0.3125, ((0, 16),)),
        "fast_second": bell_draw(arg_keys[8], (HEADS, FH, HD), FH ** -0.5, 0.25, ((0, 16),)),
        "norm_gain": jnp.clip(1.0 + 0.1 * jax.random.normal(arg_keys[9], (D,), jnp.float32), 0.5, 1.5),
    }


coef_first = 3.4445
coef_second = -4.775
coef_third = 2.0315
epsilon = 1e-06

def silu_slope(pre):
    sig = jax.nn.sigmoid(pre)
    return sig * (1.0 + pre * (1.0 - sig))

def fast_apply(inputs, first, third, second):
    pre_gate = jnp.dot(inputs, first, preferred_element_type=jnp.float32)
    pre_up = jnp.dot(inputs, third, preferred_element_type=jnp.float32)
    hidden = (jax.nn.silu(pre_gate) * pre_up).astype(jnp.bfloat16)
    return jnp.dot(hidden, second, preferred_element_type=jnp.float32)

def fast_grads(key_block, scaled, first, third, second):
    pre_gate = jnp.dot(key_block, first, preferred_element_type=jnp.float32)
    pre_up = jnp.dot(key_block, third, preferred_element_type=jnp.float32)
    gated = jax.nn.silu(pre_gate)
    hidden = (gated * pre_up).astype(jnp.bfloat16)
    back = jnp.dot(scaled, second.T, preferred_element_type=jnp.float32)
    d_gate = (back * pre_up * silu_slope(pre_gate)).astype(jnp.bfloat16)
    d_up = (back * gated).astype(jnp.bfloat16)
    return (jnp.dot(key_block.T, d_gate, preferred_element_type=jnp.float32), jnp.dot(key_block.T, d_up, preferred_element_type=jnp.float32), jnp.dot(hidden.T, scaled, preferred_element_type=jnp.float32))

def orthogonal(grad):
    high = lax.Precision.HIGHEST
    current = grad * lax.rsqrt(jnp.sum(grad * grad) + epsilon)
    for sweep in range(NS_ITERS):
        gram = jnp.dot(current, current.T, precision=high, preferred_element_type=jnp.float32)
        square = jnp.dot(gram, gram, precision=high, preferred_element_type=jnp.float32)
        mix = coef_second * gram + coef_third * square
        current = coef_first * current + jnp.dot(mix, current, precision=high, preferred_element_type=jnp.float32)
    return current

def attend(queries, keys_ext, values_ext, start):
    count = queries.shape[0]
    block = min(512, count)
    heads = queries.shape[1] // ATT_DIM
    scale = 1.0 / math.sqrt(ATT_DIM)

    def one_block(index):
        begin = index * block
        q_block = lax.dynamic_slice_in_dim(queries, begin, block, 0).reshape(block, heads, ATT_DIM).astype(jnp.float32)
        k_block = lax.dynamic_slice_in_dim(keys_ext, begin, block + WINDOW, 0).reshape(block + WINDOW, heads, ATT_DIM).astype(jnp.float32)
        v_block = lax.dynamic_slice_in_dim(values_ext, begin, block + WINDOW, 0).reshape(block + WINDOW, heads, ATT_DIM).astype(jnp.float32)
        scores = jnp.einsum('qhd,khd->hqk', q_block, k_block) * scale
        q_pos = start + begin + jnp.arange(block)
        k_pos = start + begin - WINDOW + jnp.arange(block + WINDOW)
        valid = (k_pos[None, :] <= q_pos[:, None]) & (k_pos[None, :] > q_pos[:, None] - WINDOW) & (k_pos[None, :] >= 0)
        scores = jnp.where(valid[None], scores, -jnp.inf)
        top = lax.optimization_barrier(jnp.max(scores, -1, keepdims=True))
        expo = jnp.exp(scores - top)
        weights = (expo / lax.optimization_barrier(jnp.sum(expo, -1, keepdims=True))).astype(jnp.bfloat16)
        result = jnp.einsum('hqk,khd->qhd', weights.astype(jnp.float32), v_block)
        return result.reshape(block, heads * ATT_DIM)
    return lax.map(one_block, jnp.arange(count // block)).reshape(count, heads * ATT_DIM)

def one_head(bundle):
    query_head, key_head, value_head, rates, step, first, third, second = bundle
    scaled = (rates[:, None] * value_head).astype(jnp.bfloat16)
    weights = (first, third, second)
    outputs = []
    for part in range(2):
        totals = None
        for block in range(N_CTX // 2):
            begin = part * GROUP + block * TOK_DEV
            pieces = fast_grads(key_head[begin:begin + TOK_DEV], scaled[begin:begin + TOK_DEV], *weights)
            totals = pieces if totals is None else tuple((left + right for left, right in zip(totals, pieces)))
        updates = (orthogonal(totals[0]), orthogonal(totals[1]), orthogonal(totals[2].T).T)
        weights = tuple(((old.astype(jnp.float32) + step * upd).astype(jnp.bfloat16) for old, upd in zip(weights, updates)))
        outputs.append(fast_apply(query_head[part * GROUP:(part + 1) * GROUP], *weights))
    fast_out = jnp.concatenate(outputs, 0)
    padding = jnp.zeros((WINDOW, HD), jnp.bfloat16)
    attn_out = attend(query_head, jnp.concatenate([padding, key_head], 0), jnp.concatenate([padding, value_head], 0), 0)
    return (fast_out + attn_out).astype(jnp.bfloat16)

def reference(query_rows, key_rows, value_rows, gate_rows, token_rates, step_sizes, fast_first, fast_third, fast_second, norm_gain):

    def by_head(array):
        return array.reshape(SEQ, HEADS, HD).transpose(1, 0, 2)
    mixed = lax.map(one_head, (by_head(query_rows), by_head(key_rows), by_head(value_rows), token_rates, step_sizes, fast_first, fast_third, fast_second))
    mixed_full = mixed.transpose(1, 0, 2).reshape(SEQ, D).astype(jnp.float32)
    square_mean = lax.optimization_barrier(jnp.mean(mixed_full * mixed_full, -1, keepdims=True))
    gated = mixed_full * lax.rsqrt(square_mean + epsilon) * norm_gain * jax.nn.silu(gate_rows.astype(jnp.float32))
    return gated.astype(jnp.bfloat16)
```

```python
import functools
import math

import jax
import jax.numpy as jnp
from jax import lax
from jax.experimental import pallas as pl
from jax.experimental.pallas import tpu as pltpu
from jax.sharding import PartitionSpec as P

ATT_DIM = 160
WINDOW = 1024
RING = 4
QB = 256
TB = 512

coef_first = 3.4445
coef_second = -4.775
coef_third = 2.0315
epsilon = 1e-06
LOG2E = 1.4426950408889634
CENTRES = (0.0, 0.0, 0.5, 0.8, 0.8)
F32 = jnp.float32
BF16 = jnp.bfloat16
VMEM_LIMIT = 56 * 1024 * 1024


def params():
    return pltpu.CompilerParams(vmem_limit_bytes=VMEM_LIMIT)


def dot(a, b, dims=((1,), (0,))):
    return lax.dot_general(a, b, (dims, ((), ())), preferred_element_type=F32)


def sigmoid(x):
    return 0.5 * jnp.tanh(0.5 * x) + 0.5


def pick_weights(place, sources, put):
    for j in range(3):
        for s in range(RING):

            @pl.when(lax.rem(place + RING - j, RING) == s)
            def _(j=j, s=s):
                put(j, sources[s][...])


def grads_kernel(static, place_ref, x_ref, v_ref, r_ref, *rest):
    n_src = 3 if static else RING
    sources, (own, s1, s2, s3), (acc, wt) = rest[:n_src], rest[n_src : n_src + 4], rest[n_src + 4 :]
    step = pl.program_id(0)
    place = place_ref[0]

    @pl.when(step == 0)
    def _():
        def put(j, w):
            wt[j] = w.T

        if static:
            for j in range(3):
                put(j, sources[j][...])
        else:
            pick_weights(place, sources, put)
        acc[...] = jnp.zeros_like(acc)

    x = x_ref[...]
    e = (r_ref[...] * v_ref[...].astype(F32)).astype(BF16)
    gate = dot(wt[0], x)
    up = dot(wt[1], x)
    back = dot(wt[2], e)
    sig = sigmoid(gate)
    gated = gate * sig
    hidden = (gated * up).astype(BF16)
    d_gate = (back * up * (sig + gated * (1.0 - sig))).astype(BF16)
    d_up = (back * gated).astype(BF16)
    nt = ((1,), (1,))
    acc[0] += dot(x, d_gate, nt)
    acc[1] += dot(x, d_up, nt)
    acc[2] += dot(e, hidden, nt)

    @pl.when(step == pl.num_programs(0) - 1)
    def _():
        for shift, out in enumerate((own, s1, s2, s3)):
            out[...] = acc[jnp.minimum(lax.rem(place + shift, RING), 2)].astype(BF16)


def grads(place, xt, vt, rates, sources, static):
    width, count = xt.shape
    matrix = sources[0].shape
    whole = pl.BlockSpec(matrix, lambda i, p: (0, 0))
    tokens = pl.BlockSpec((width, TB), lambda i, p: (0, i))
    hidden = matrix[1]
    return pl.pallas_call(
        functools.partial(grads_kernel, static),
        grid_spec=pltpu.PrefetchScalarGridSpec(
            num_scalar_prefetch=1,
            grid=(count // TB,),
            in_specs=[tokens, tokens, pl.BlockSpec((1, TB), lambda i, p: (0, i))]
            + [whole] * len(sources),
            out_specs=[whole] * 4,
            scratch_shapes=[
                pltpu.VMEM((3,) + matrix, F32),
                pltpu.VMEM((3, hidden, width), BF16),
            ],
        ),
        out_shape=[jax.ShapeDtypeStruct(matrix, BF16)] * 4,
        compiler_params=params(),
        cost_estimate=pl.CostEstimate(
            flops=12 * width * hidden * count,
            bytes_accessed=4 * width * count,
            transcendentals=hidden * count,
        ),
    )(place, xt, vt, rates, *sources)


def update_kernel(place_ref, step_ref, own, r1, r2, r3, *rest):
    olds, out = rest[:-1], rest[-1]
    place = place_ref[0]
    if len(olds) == 3:
        old = jnp.where(
            place == 0, olds[0][...], jnp.where(place == 1, olds[1][...], olds[2][...])
        )
    else:
        old = olds[0][...]
    g = own[...].astype(F32) + r1[...].astype(F32) + r2[...].astype(F32) + r3[...].astype(F32)
    x = g * lax.rsqrt(jnp.sum(g * g) + epsilon)
    rows = g.shape[0]
    diagonal = lax.broadcasted_iota(jnp.int32, (rows, rows), 0) == lax.broadcasted_iota(
        jnp.int32, (rows, rows), 1
    )
    for c in CENTRES:
        xb = x.astype(BF16)
        e = dot(xb, xb, ((1,), (1,)))
        if c:
            e = e - jnp.where(diagonal, c, 0.0)
        eb = e.astype(BF16)
        mix = (coef_second + 2.0 * c * coef_third) * e + coef_third * dot(eb, eb)
        k = coef_first + coef_second * c + coef_third * c * c
        x = k * x + dot(mix.astype(BF16), xb)
    out[...] = (old.astype(F32) + step_ref[0] * x).astype(BF16)


def update(place, step, pieces, olds):
    matrix = pieces[0].shape
    smem = pl.BlockSpec(memory_space=pltpu.SMEM)
    vmem = pl.BlockSpec(memory_space=pltpu.VMEM)
    return pl.pallas_call(
        update_kernel,
        in_specs=[smem, smem] + [vmem] * (4 + len(olds)),
        out_specs=vmem,
        out_shape=jax.ShapeDtypeStruct(matrix, BF16),
        compiler_params=params(),
        cost_estimate=pl.CostEstimate(
            flops=5 * 2 * 5 * matrix[0] * matrix[0] * matrix[0],
            bytes_accessed=16 * matrix[0] * matrix[1],
            transcendentals=0,
        ),
    )(place, step, *pieces, *olds)


def attend_kernel(blocks, kb_first, first_ref, q_ref, k_ref, v_ref, *rest):
    if kb_first is None:
        (out, k_nat) = rest
        rims = ()
    else:
        (rim_k, rim_v, _, out, k_nat) = rest
        rims = (rim_k, rim_v)
    step = pl.program_id(0)
    heads = q_ref.shape[0] // ATT_DIM
    chunks = WINDOW // QB + 1
    rim_blocks = WINDOW // QB if rims else 0

    @pl.when(step == 0)
    def _():
        if rims:
            for h in range(heads):
                k_nat[h, :WINDOW, :] = rims[0][pl.ds(h * ATT_DIM, ATT_DIM), :].T
        for h in range(heads):
            k_nat[h, rim_blocks * QB :, :] = k_ref[pl.ds(h * ATT_DIM, ATT_DIM), :].T

    later = lax.broadcasted_iota(jnp.int32, (QB, QB), 0) > lax.broadcasted_iota(
        jnp.int32, (QB, QB), 1
    )
    scale = LOG2E / math.sqrt(ATT_DIM)
    low = -1e30

    def values(h, block):
        return v_ref[pl.ds(h * ATT_DIM, ATT_DIM), pl.ds(pl.multiple_of(block * QB, QB), QB)]

    def body(i, fresh):
        for h in range(heads):
            q = q_ref[pl.ds(h * ATT_DIM, ATT_DIM), :]
            s = []
            for c in range(chunks):
                k = k_nat[h, pl.ds(pl.multiple_of((i + c) * QB, QB), QB), :]
                part = dot(k, q)
                if c == 0:
                    part = jnp.where(later, part, low)
                elif c == chunks - 1:
                    part = jnp.where(later, low, part)
                if c < fresh:
                    part = jnp.where(first_ref[0] == 1, low, part)
                s.append(part)
            top = functools.reduce(
                jnp.maximum, [jnp.max(part, axis=0, keepdims=True) for part in s]
            )
            total = jnp.zeros((1, QB), F32)
            result = jnp.zeros((ATT_DIM, QB), F32)
            for c in range(chunks):
                expo = jnp.exp2((s[c] - top) * scale)
                total += jnp.sum(expo, axis=0, keepdims=True)
                if c < fresh:
                    v = rims[1][pl.ds(h * ATT_DIM, ATT_DIM), pl.ds((i + c) * QB, QB)]
                else:
                    v = values(h, i + c - rim_blocks)
                result += dot(v, expo.astype(BF16))
            out[pl.ds(h * ATT_DIM, ATT_DIM), :] = result / total

    if rims:
        for i in range(blocks):

            @pl.when(step == i)
            def _(i=i):
                body(i, rim_blocks - i)
    else:
        body(step, 0)


def attend_main(qt, kt, vt, first):
    width, count = qt.shape
    skip = WINDOW // QB
    blocks = count // QB - skip
    heads = width // ATT_DIM
    whole = pl.BlockSpec((width, count), lambda i, f: (0, 0))
    return pl.pallas_call(
        functools.partial(attend_kernel, blocks, None),
        grid_spec=pltpu.PrefetchScalarGridSpec(
            num_scalar_prefetch=1,
            grid=(blocks,),
            in_specs=[pl.BlockSpec((width, QB), lambda i, f: (0, i + skip)), whole, whole],
            out_specs=pl.BlockSpec((width, QB), lambda i, f: (0, i + skip)),
            scratch_shapes=[pltpu.VMEM((heads, count, ATT_DIM), BF16)],
        ),
        out_shape=jax.ShapeDtypeStruct((width, count), F32),
        compiler_params=params(),
        cost_estimate=pl.CostEstimate(
            flops=4 * blocks * QB * (WINDOW + QB) * width,
            bytes_accessed=10 * width * count,
            transcendentals=blocks * QB * (WINDOW + QB) * heads,
        ),
    )(first, qt, kt, vt)


def attend_rim(qt, kt, vt, rim_k, rim_v, main, first):
    width = qt.shape[0]
    blocks = WINDOW // QB
    heads = width // ATT_DIM
    whole = pl.BlockSpec((width, WINDOW), lambda i, f: (0, 0))
    return pl.pallas_call(
        functools.partial(attend_kernel, blocks, 0),
        grid_spec=pltpu.PrefetchScalarGridSpec(
            num_scalar_prefetch=1,
            grid=(blocks,),
            in_specs=[pl.BlockSpec((width, QB), lambda i, f: (0, i))] + [whole] * 4
            + [pl.BlockSpec(memory_space=pl.ANY)],
            out_specs=pl.BlockSpec((width, QB), lambda i, f: (0, i)),
            scratch_shapes=[pltpu.VMEM((heads, 2 * WINDOW, ATT_DIM), BF16)],
        ),
        out_shape=jax.ShapeDtypeStruct(main.shape, F32),
        input_output_aliases={6: 0},
        compiler_params=params(),
        cost_estimate=pl.CostEstimate(
            flops=4 * blocks * QB * (WINDOW + QB) * width,
            bytes_accessed=16 * width * WINDOW,
            transcendentals=blocks * QB * (WINDOW + QB) * heads,
        ),
    )(first, qt, kt, vt, rim_k, rim_v, main)


def pack(rows, out, dests):
    n = rows.shape[0] // (2 * dests)
    width = rows.shape[1]
    for d in range(dests):
        begin = 2 * n * d
        out[d] = jnp.concatenate([rows[begin : begin + n], rows[begin + n : begin + 2 * n]], 1)


def apply_kernel(dests, place_ref, part_ref, q_ref, att_ref, *rest):
    sources, out, (wt, w2) = rest[: 2 * RING], rest[2 * RING], rest[2 * RING + 1 :]

    @pl.when(pl.program_id(0) == 0)
    def _():
        def put(j, w):
            if j < 2:
                wt[j] = w.T
            else:
                w2[...] = w

        for part in range(2):

            @pl.when(part_ref[0] == part)
            def _(part=part):
                pick_weights(place_ref[0], sources[part * RING : (part + 1) * RING], put)

    q = q_ref[...]
    gate = dot(wt[0], q)
    up = dot(wt[1], q)
    hidden = (gate * sigmoid(gate) * up).astype(BF16)
    fast = dot(w2[...], hidden)
    pack((fast + att_ref[...]).astype(BF16).T, out, dests)


def apply_mix(place, part, qt, att, early, late, parts_out):
    width, count = qt.shape
    matrix = early[0].shape
    rows = count // parts_out
    dests = 4
    tokens = pl.BlockSpec((width, dests * rows), lambda i, p, g: (0, i))
    return pl.pallas_call(
        functools.partial(apply_kernel, dests),
        grid_spec=pltpu.PrefetchScalarGridSpec(
            num_scalar_prefetch=2,
            grid=(parts_out // dests,),
            in_specs=[tokens, tokens] + [pl.BlockSpec(matrix, lambda i, p, g: (0, 0))] * 8,
            out_specs=pl.BlockSpec((dests, rows // 2, 2 * width), lambda i, p, g: (i, 0, 0)),
            scratch_shapes=[
                pltpu.VMEM((2, matrix[1], width), BF16),
                pltpu.VMEM(matrix, BF16),
            ],
        ),
        out_shape=jax.ShapeDtypeStruct((parts_out, rows // 2, 2 * width), BF16),
        compiler_params=params(),
        cost_estimate=pl.CostEstimate(
            flops=6 * width * matrix[1] * count,
            bytes_accessed=8 * width * count,
            transcendentals=matrix[1] * count,
        ),
    )(place, part, qt, att, *early, *late)


def gate_kernel(dests, g_ref, out):
    pack(g_ref[...].T, out, dests)


def pack_gate(gt, parts_out):
    width, count = gt.shape
    rows = count // parts_out
    dests = 4
    return pl.pallas_call(
        functools.partial(gate_kernel, dests),
        grid=(parts_out // dests,),
        in_specs=[pl.BlockSpec((width, dests * rows), lambda i: (0, i))],
        out_specs=pl.BlockSpec((dests, rows // 2, 2 * width), lambda i: (i, 0, 0)),
        out_shape=jax.ShapeDtypeStruct((parts_out, rows // 2, 2 * width), BF16),
        compiler_params=params(),
        cost_estimate=pl.CostEstimate(
            flops=0, bytes_accessed=8 * width * count, transcendentals=0
        ),
    )(gt)


def final_kernel(m_ref, g_ref, gain_ref, out):
    heads, _, double = m_ref.shape
    width = double // 2
    for half in range(2):
        lanes = slice(half * width, (half + 1) * width)
        total = 0.0
        for h in range(heads):
            m = m_ref[h, :, lanes].astype(F32)
            total += jnp.sum(m * m, axis=1, keepdims=True)
        factor = lax.rsqrt(total / (heads * width) + epsilon)
        for h in range(0, heads, 2):
            cols = slice(h * width, (h + 2) * width)
            m = jnp.concatenate([m_ref[h, :, lanes], m_ref[h + 1, :, lanes]], 1).astype(F32)
            g = jnp.concatenate([g_ref[h, :, lanes], g_ref[h + 1, :, lanes]], 1).astype(F32)
            out[half, :, cols] = (m * factor * gain_ref[:, cols] * (g * sigmoid(g))).astype(BF16)


def final(mixed, gates, gain):
    heads, rows, double = mixed.shape
    block = 32
    wide = heads * double // 2
    tokens = pl.BlockSpec((heads, block, double), lambda i: (0, i, 0))
    result = pl.pallas_call(
        final_kernel,
        grid=(rows // block,),
        in_specs=[tokens, tokens, pl.BlockSpec((1, wide), lambda i: (0, 0))],
        out_specs=pl.BlockSpec((2, block, wide), lambda i: (0, i, 0)),
        out_shape=jax.ShapeDtypeStruct((2, rows, wide), BF16),
        compiler_params=params(),
        cost_estimate=pl.CostEstimate(
            flops=20 * rows * wide, bytes_accessed=12 * rows * wide, transcendentals=2 * rows * wide
        ),
    )(mixed, gates, gain.reshape(1, wide))
    return result.reshape(2 * rows, wide)


def reduce_moves(part):
    base = part * RING
    return [
        [(base + (m - s) % RING, base + m) for m in range(3)] for s in range(1, RING)
    ]


def spread_moves(parts):
    return [
        [(p * RING + m, p * RING + (m + s) % RING) for p in parts for m in range(3)]
        for s in range(1, RING)
    ]


def send(array, pairs):
    return lax.ppermute(array, "ctx", pairs)


def shards(
    query_rows,
    key_rows,
    value_rows,
    gate_rows,
    token_rates,
    step_sizes,
    fast_first,
    fast_third,
    fast_second,
    norm_gain,
):
    ctx = lax.axis_index("ctx")
    heads = lax.axis_size("head")
    place = (ctx % RING).reshape(1).astype(jnp.int32)
    part = (ctx // RING).reshape(1).astype(jnp.int32)
    first = (ctx == 0).reshape(1).astype(jnp.int32)
    qt, kt, vt, gt = query_rows.T, key_rows.T, value_rows.T, gate_rows.T
    count = qt.shape[1]
    start = [fast_first[0], fast_third[0], fast_second[0].T]

    tail_k, tail_v = kt[:, count - WINDOW :], vt[:, count - WINDOW :]
    late_pairs = [(i, i + 1) for i in range(3, 7)]
    early_pairs = [(i, i + 1) for i in range(3)]
    rim_late = (send(tail_k, late_pairs), send(tail_v, late_pairs))

    own, *out = grads(place, kt, vt, token_rates, start, True)
    pieces = [own] + [send(o, p) for o, p in zip(out, reduce_moves(0))]
    att_main = attend_main(qt, kt, vt, first)
    gates = pack_gate(gt, heads)
    pieces, att_main, gates, tails = lax.optimization_barrier(
        (pieces, att_main, gates, (tail_k, tail_v))
    )
    rim_early = (send(tails[0], early_pairs), send(tails[1], early_pairs))
    fresh = update(place, step_sizes, pieces, start)
    crossed = send(fresh, [(m, RING + m) for m in range(3)])
    held = jnp.where(part[0] == 0, fresh, crossed)
    early = [held] + [send(held, p) for p in spread_moves((0, 1))]
    rims = [jnp.where(part[0] == 0, a, b) for a, b in zip(rim_early, rim_late)]
    att = attend_rim(qt, kt, vt, rims[0], rims[1], att_main, first)
    early, att = lax.optimization_barrier((early, att))

    own, *out = grads(place, kt, vt, token_rates, early, False)
    pieces = [own] + [send(o, p) for o, p in zip(out, reduce_moves(1))]
    gate_tokens = lax.all_to_all(gates, "head", split_axis=0, concat_axis=0)
    fresh = update(place, step_sizes, pieces, [early[0]])
    late = [fresh] + [send(fresh, p) for p in spread_moves((1,))]
    mixed = apply_mix(place, part, qt, att, early, late, heads)
    mixed_tokens = lax.all_to_all(mixed, "head", split_axis=0, concat_axis=0)
    return final(mixed_tokens, gate_tokens, norm_gain)


def solution(mesh):
    placed = (
        P("ctx", "head"),
        P("ctx", "head"),
        P("ctx", "head"),
        P("ctx", "head"),
        P("head", "ctx"),
        P("head"),
        P("head", None, None),
        P("head", None, None),
        P("head", None, None),
        P(),
    )
    return jax.shard_map(
        shards, mesh=mesh, in_specs=placed, out_specs=P(("ctx", "head"), None), check_vma=False
    )
```

```python
import functools
import math

import jax
import jax.numpy as jnp
from jax import lax
from jax.experimental import pallas as pl
from jax.experimental.pallas import tpu as pltpu
from jax.sharding import PartitionSpec as P

ATT_DIM = 160
WINDOW = 1024
RING = 4
QB = 256
TB = 512

coef_first = 3.4445
coef_second = -4.775
coef_third = 2.0315
epsilon = 1e-06
LOG2E = 1.4426950408889634
CENTRES = (0.0, 0.0, 0.5, 0.8, 0.8)
F32 = jnp.float32
BF16 = jnp.bfloat16
VMEM_LIMIT = 56 * 1024 * 1024


def params():
    return pltpu.CompilerParams(vmem_limit_bytes=VMEM_LIMIT)


def dot(a, b, dims=((1,), (0,))):
    return lax.dot_general(a, b, (dims, ((), ())), preferred_element_type=F32)


def sigmoid(x):
    return 0.5 * jnp.tanh(0.5 * x) + 0.5


def pick_weights(place, sources, put):
    for j in range(3):
        for s in range(RING):

            @pl.when(lax.rem(place + RING - j, RING) == s)
            def _(j=j, s=s):
                put(j, sources[s][...])


def grads_kernel(static, place_ref, x_ref, v_ref, r_ref, *rest):
    n_src = 3 if static else RING
    sources, (own, s1, s2, s3), (acc, wt) = rest[:n_src], rest[n_src : n_src + 4], rest[n_src + 4 :]
    step = pl.program_id(0)
    place = place_ref[0]

    @pl.when(step == 0)
    def _():
        def put(j, w):
            wt[j] = w.T

        if static:
            for j in range(3):
                put(j, sources[j][...])
        else:
            pick_weights(place, sources, put)
        acc[...] = jnp.zeros_like(acc)

    x = x_ref[...]
    e = (r_ref[...] * v_ref[...].astype(F32)).astype(BF16)
    gate = dot(wt[0], x)
    up = dot(wt[1], x)
    back = dot(wt[2], e)
    sig = sigmoid(gate)
    gated = gate * sig
    hidden = (gated * up).astype(BF16)
    d_gate = (back * up * (sig + gated * (1.0 - sig))).astype(BF16)
    d_up = (back * gated).astype(BF16)
    nt = ((1,), (1,))
    acc[0] += dot(x, d_gate, nt)
    acc[1] += dot(x, d_up, nt)
    acc[2] += dot(e, hidden, nt)

    @pl.when(step == pl.num_programs(0) - 1)
    def _():
        for shift, out in enumerate((own, s1, s2, s3)):
            out[...] = acc[jnp.minimum(lax.rem(place + shift, RING), 2)].astype(BF16)


def grads(place, xt, vt, rates, sources, static):
    width, count = xt.shape
    matrix = sources[0].shape
    whole = pl.BlockSpec(matrix, lambda i, p: (0, 0))
    tokens = pl.BlockSpec((width, TB), lambda i, p: (0, i))
    hidden = matrix[1]
    return pl.pallas_call(
        functools.partial(grads_kernel, static),
        grid_spec=pltpu.PrefetchScalarGridSpec(
            num_scalar_prefetch=1,
            grid=(count // TB,),
            in_specs=[tokens, tokens, pl.BlockSpec((1, TB), lambda i, p: (0, i))]
            + [whole] * len(sources),
            out_specs=[whole] * 4,
            scratch_shapes=[
                pltpu.VMEM((3,) + matrix, F32),
                pltpu.VMEM((3, hidden, width), BF16),
            ],
        ),
        out_shape=[jax.ShapeDtypeStruct(matrix, BF16)] * 4,
        compiler_params=params(),
        cost_estimate=pl.CostEstimate(
            flops=12 * width * hidden * count,
            bytes_accessed=4 * width * count,
            transcendentals=hidden * count,
        ),
    )(place, xt, vt, rates, *sources)


def update_kernel(place_ref, step_ref, own, r1, r2, r3, *rest):
    olds, out = rest[:-1], rest[-1]
    place = place_ref[0]
    if len(olds) == 3:
        old = jnp.where(
            place == 0, olds[0][...], jnp.where(place == 1, olds[1][...], olds[2][...])
        )
    else:
        old = olds[0][...]
    g = own[...].astype(F32) + r1[...].astype(F32) + r2[...].astype(F32) + r3[...].astype(F32)
    x = g * lax.rsqrt(jnp.sum(g * g) + epsilon)
    rows = g.shape[0]
    diagonal = lax.broadcasted_iota(jnp.int32, (rows, rows), 0) == lax.broadcasted_iota(
        jnp.int32, (rows, rows), 1
    )
    for c in CENTRES:
        xb = x.astype(BF16)
        e = dot(xb, xb, ((1,), (1,)))
        if c:
            e = e - jnp.where(diagonal, c, 0.0)
        eb = e.astype(BF16)
        mix = (coef_second + 2.0 * c * coef_third) * e + coef_third * dot(eb, eb)
        k = coef_first + coef_second * c + coef_third * c * c
        x = k * x + dot(mix.astype(BF16), xb)
    out[...] = (old.astype(F32) + step_ref[0] * x).astype(BF16)


def update(place, step, pieces, olds):
    matrix = pieces[0].shape
    smem = pl.BlockSpec(memory_space=pltpu.SMEM)
    vmem = pl.BlockSpec(memory_space=pltpu.VMEM)
    return pl.pallas_call(
        update_kernel,
        in_specs=[smem, smem] + [vmem] * (4 + len(olds)),
        out_specs=vmem,
        out_shape=jax.ShapeDtypeStruct(matrix, BF16),
        compiler_params=params(),
        cost_estimate=pl.CostEstimate(
            flops=5 * 2 * 5 * matrix[0] * matrix[0] * matrix[0],
            bytes_accessed=16 * matrix[0] * matrix[1],
            transcendentals=0,
        ),
    )(place, step, *pieces, *olds)


def attend_kernel(blocks, kb_first, first_ref, q_ref, k_ref, v_ref, *rest):
    if kb_first is None:
        (out, k_nat) = rest
        rims = ()
    else:
        (rim_k, rim_v, _, out, k_nat) = rest
        rims = (rim_k, rim_v)
    step = pl.program_id(0)
    heads = q_ref.shape[0] // ATT_DIM
    chunks = WINDOW // QB + 1
    rim_blocks = WINDOW // QB if rims else 0

    @pl.when(step == 0)
    def _():
        if rims:
            for h in range(heads):
                k_nat[h, :WINDOW, :] = rims[0][pl.ds(h * ATT_DIM, ATT_DIM), :].T
        for h in range(heads):
            k_nat[h, rim_blocks * QB :, :] = k_ref[pl.ds(h * ATT_DIM, ATT_DIM), :].T

    later = lax.broadcasted_iota(jnp.int32, (QB, QB), 0) > lax.broadcasted_iota(
        jnp.int32, (QB, QB), 1
    )
    scale = LOG2E / math.sqrt(ATT_DIM)
    low = -1e30

    def values(h, block):
        return v_ref[pl.ds(h * ATT_DIM, ATT_DIM), pl.ds(pl.multiple_of(block * QB, QB), QB)]

    def body(i, fresh):
        for h in range(heads):
            q = q_ref[pl.ds(h * ATT_DIM, ATT_DIM), :]
            s = []
            for c in range(chunks):
                k = k_nat[h, pl.ds(pl.multiple_of((i + c) * QB, QB), QB), :]
                part = dot(k, q)
                if c == 0:
                    part = jnp.where(later, part, low)
                elif c == chunks - 1:
                    part = jnp.where(later, low, part)
                if c < fresh:
                    part = jnp.where(first_ref[0] == 1, low, part)
                s.append(part)
            top = functools.reduce(
                jnp.maximum, [jnp.max(part, axis=0, keepdims=True) for part in s]
            )
            total = jnp.zeros((1, QB), F32)
            result = jnp.zeros((ATT_DIM, QB), F32)
            for c in range(chunks):
                expo = jnp.exp2((s[c] - top) * scale)
                total += jnp.sum(expo, axis=0, keepdims=True)
                if c < fresh:
                    v = rims[1][pl.ds(h * ATT_DIM, ATT_DIM), pl.ds((i + c) * QB, QB)]
                else:
                    v = values(h, i + c - rim_blocks)
                result += dot(v, expo.astype(BF16))
            out[pl.ds(h * ATT_DIM, ATT_DIM), :] = result / total

    if rims:
        for i in range(blocks):

            @pl.when(step == i)
            def _(i=i):
                body(i, rim_blocks - i)
    else:
        body(step, 0)


def attend_main(qt, kt, vt, first):
    width, count = qt.shape
    skip = WINDOW // QB
    blocks = count // QB - skip
    heads = width // ATT_DIM
    whole = pl.BlockSpec((width, count), lambda i, f: (0, 0))
    return pl.pallas_call(
        functools.partial(attend_kernel, blocks, None),
        grid_spec=pltpu.PrefetchScalarGridSpec(
            num_scalar_prefetch=1,
            grid=(blocks,),
            in_specs=[pl.BlockSpec((width, QB), lambda i, f: (0, i + skip)), whole, whole],
            out_specs=pl.BlockSpec((width, QB), lambda i, f: (0, i + skip)),
            scratch_shapes=[pltpu.VMEM((heads, count, ATT_DIM), BF16)],
        ),
        out_shape=jax.ShapeDtypeStruct((width, count), F32),
        compiler_params=params(),
        cost_estimate=pl.CostEstimate(
            flops=4 * blocks * QB * (WINDOW + QB) * width,
            bytes_accessed=10 * width * count,
            transcendentals=blocks * QB * (WINDOW + QB) * heads,
        ),
    )(first, qt, kt, vt)


def attend_rim(qt, kt, vt, rim_k, rim_v, main, first):
    width = qt.shape[0]
    blocks = WINDOW // QB
    heads = width // ATT_DIM
    whole = pl.BlockSpec((width, WINDOW), lambda i, f: (0, 0))
    return pl.pallas_call(
        functools.partial(attend_kernel, blocks, 0),
        grid_spec=pltpu.PrefetchScalarGridSpec(
            num_scalar_prefetch=1,
            grid=(blocks,),
            in_specs=[pl.BlockSpec((width, QB), lambda i, f: (0, i))] + [whole] * 4
            + [pl.BlockSpec(memory_space=pl.ANY)],
            out_specs=pl.BlockSpec((width, QB), lambda i, f: (0, i)),
            scratch_shapes=[pltpu.VMEM((heads, 2 * WINDOW, ATT_DIM), BF16)],
        ),
        out_shape=jax.ShapeDtypeStruct(main.shape, F32),
        input_output_aliases={6: 0},
        compiler_params=params(),
        cost_estimate=pl.CostEstimate(
            flops=4 * blocks * QB * (WINDOW + QB) * width,
            bytes_accessed=16 * width * WINDOW,
            transcendentals=blocks * QB * (WINDOW + QB) * heads,
        ),
    )(first, qt, kt, vt, rim_k, rim_v, main)


def pack(rows, out, dests):
    n = rows.shape[0] // (2 * dests)
    width = rows.shape[1]
    for d in range(dests):
        begin = 2 * n * d
        out[d] = jnp.concatenate([rows[begin : begin + n], rows[begin + n : begin + 2 * n]], 1)


def apply_kernel(dests, place_ref, part_ref, q_ref, att_ref, *rest):
    sources, out, (wt, w2) = rest[: 2 * RING], rest[2 * RING], rest[2 * RING + 1 :]

    @pl.when(pl.program_id(0) == 0)
    def _():
        def put(j, w):
            if j < 2:
                wt[j] = w.T
            else:
                w2[...] = w

        for part in range(2):

            @pl.when(part_ref[0] == part)
            def _(part=part):
                pick_weights(place_ref[0], sources[part * RING : (part + 1) * RING], put)

    q = q_ref[...]
    gate = dot(wt[0], q)
    up = dot(wt[1], q)
    hidden = (gate * sigmoid(gate) * up).astype(BF16)
    fast = dot(w2[...], hidden)
    pack((fast + att_ref[...]).astype(BF16).T, out, dests)


def apply_mix(place, part, qt, att, early, late, parts_out):
    width, count = qt.shape
    matrix = early[0].shape
    rows = count // parts_out
    dests = 4
    tokens = pl.BlockSpec((width, dests * rows), lambda i, p, g: (0, i))
    return pl.pallas_call(
        functools.partial(apply_kernel, dests),
        grid_spec=pltpu.PrefetchScalarGridSpec(
            num_scalar_prefetch=2,
            grid=(parts_out // dests,),
            in_specs=[tokens, tokens] + [pl.BlockSpec(matrix, lambda i, p, g: (0, 0))] * 8,
            out_specs=pl.BlockSpec((dests, rows // 2, 2 * width), lambda i, p, g: (i, 0, 0)),
            scratch_shapes=[
                pltpu.VMEM((2, matrix[1], width), BF16),
                pltpu.VMEM(matrix, BF16),
            ],
        ),
        out_shape=jax.ShapeDtypeStruct((parts_out, rows // 2, 2 * width), BF16),
        compiler_params=params(),
        cost_estimate=pl.CostEstimate(
            flops=6 * width * matrix[1] * count,
            bytes_accessed=8 * width * count,
            transcendentals=matrix[1] * count,
        ),
    )(place, part, qt, att, *early, *late)


def gate_kernel(dests, g_ref, out):
    pack(g_ref[...].T, out, dests)


def pack_gate(gt, parts_out):
    width, count = gt.shape
    rows = count // parts_out
    dests = 4
    return pl.pallas_call(
        functools.partial(gate_kernel, dests),
        grid=(parts_out // dests,),
        in_specs=[pl.BlockSpec((width, dests * rows), lambda i: (0, i))],
        out_specs=pl.BlockSpec((dests, rows // 2, 2 * width), lambda i: (i, 0, 0)),
        out_shape=jax.ShapeDtypeStruct((parts_out, rows // 2, 2 * width), BF16),
        compiler_params=params(),
        cost_estimate=pl.CostEstimate(
            flops=0, bytes_accessed=8 * width * count, transcendentals=0
        ),
    )(gt)


def final_kernel(m_ref, g_ref, gain_ref, out):
    heads, _, double = m_ref.shape
    width = double // 2
    for half in range(2):
        lanes = slice(half * width, (half + 1) * width)
        total = 0.0
        for h in range(heads):
            m = m_ref[h, :, lanes].astype(F32)
            total += jnp.sum(m * m, axis=1, keepdims=True)
        factor = lax.rsqrt(total / (heads * width) + epsilon)
        for h in range(0, heads, 2):
            cols = slice(h * width, (h + 2) * width)
            m = jnp.concatenate([m_ref[h, :, lanes], m_ref[h + 1, :, lanes]], 1).astype(F32)
            g = jnp.concatenate([g_ref[h, :, lanes], g_ref[h + 1, :, lanes]], 1).astype(F32)
            out[half, :, cols] = (m * factor * gain_ref[:, cols] * (g * sigmoid(g))).astype(BF16)


def final(mixed, gates, gain):
    heads, rows, double = mixed.shape
    block = 32
    wide = heads * double // 2
    tokens = pl.BlockSpec((heads, block, double), lambda i: (0, i, 0))
    result = pl.pallas_call(
        final_kernel,
        grid=(rows // block,),
        in_specs=[tokens, tokens, pl.BlockSpec((1, wide), lambda i: (0, 0))],
        out_specs=pl.BlockSpec((2, block, wide), lambda i: (0, i, 0)),
        out_shape=jax.ShapeDtypeStruct((2, rows, wide), BF16),
        compiler_params=params(),
        cost_estimate=pl.CostEstimate(
            flops=20 * rows * wide, bytes_accessed=12 * rows * wide, transcendentals=2 * rows * wide
        ),
    )(mixed, gates, gain.reshape(1, wide))
    return result.reshape(2 * rows, wide)


def reduce_moves(part):
    return [[(part, (m - s) % RING, part, m) for m in range(3)] for s in range(1, RING)]


def spread_moves(parts):
    return [[(p, m, p, (m + s) % RING) for p in parts for m in range(3)] for s in range(1, RING)]


def ring_send(array, moves):
    heads = lax.axis_size("head")

    def index(part, place, head):
        return (part * RING + (place + 2 * (head % 2)) % RING) * heads + head

    pairs = [(index(a, b, h), index(c, d, h)) for a, b, c, d in moves for h in range(heads)]
    return lax.ppermute(array, ("ctx", "head"), pairs)


def send(array, pairs):
    return lax.ppermute(array, "ctx", pairs)


def shards(
    query_rows,
    key_rows,
    value_rows,
    gate_rows,
    token_rates,
    step_sizes,
    fast_first,
    fast_third,
    fast_second,
    norm_gain,
):
    ctx = lax.axis_index("ctx")
    heads = lax.axis_size("head")
    place = ((ctx + 2 * (lax.axis_index("head") % 2)) % RING).reshape(1).astype(jnp.int32)
    part = (ctx // RING).reshape(1).astype(jnp.int32)
    first = (ctx == 0).reshape(1).astype(jnp.int32)
    qt, kt, vt, gt = query_rows.T, key_rows.T, value_rows.T, gate_rows.T
    count = qt.shape[1]
    start = [fast_first[0], fast_third[0], fast_second[0].T]
    hold = lax.optimization_barrier

    tails = (kt[:, count - WINDOW :], vt[:, count - WINDOW :])
    rim_late = [send(t, [(i, i + 1) for i in range(4, 7)]) for t in tails]
    own, *out = grads(place, kt, vt, token_rates, start, True)
    pieces = [own] + [ring_send(o, p) for o, p in zip(out, reduce_moves(0))]
    q_main, rim_late = hold((qt, rim_late))
    att_main = attend_main(q_main, kt, vt, first)
    pieces, att_main, tails = hold((pieces, att_main, tails))
    fresh = update(place, step_sizes, pieces, start)
    fresh, tails, gt = hold((fresh, tails, gt))
    crossed = ring_send(fresh, [(0, m, 1, m) for m in range(3)])
    rim_early = [send(t, [(i, i + 1) for i in range(4)]) for t in tails]
    gates = pack_gate(gt, heads)
    held = jnp.where(part[0] == 0, fresh, crossed)
    held, gates = hold((held, gates))
    gate_tokens = lax.all_to_all(gates, "head", split_axis=0, concat_axis=0)
    early = [held] + [ring_send(held, p) for p in spread_moves((0, 1))]
    early = hold(early)

    own, *out = grads(place, kt, vt, token_rates, early, False)
    own, out, att_main = hold((own, out, att_main))
    pieces = [own] + [ring_send(o, p) for o, p in zip(out, reduce_moves(1))]
    rims = [jnp.where(ctx <= RING, a, b) for a, b in zip(rim_early, rim_late)]
    att = attend_rim(qt, kt, vt, rims[0], rims[1], att_main, first)
    pieces, att = hold((pieces, att))
    fresh = update(place, step_sizes, pieces, [early[0]])
    late = [fresh] + [ring_send(fresh, p) for p in spread_moves((1,))]
    mixed = apply_mix(place, part, qt, att, early, late, heads)
    mixed_tokens = lax.all_to_all(mixed, "head", split_axis=0, concat_axis=0)
    return final(mixed_tokens, gate_tokens, norm_gain)


def solution(mesh):
    placed = (
        P("ctx", "head"),
        P("ctx", "head"),
        P("ctx", "head"),
        P("ctx", "head"),
        P("head", "ctx"),
        P("head"),
        P("head", None, None),
        P("head", None, None),
        P("head", None, None),
        P(),
    )
    return jax.shard_map(
        shards, mesh=mesh, in_specs=placed, out_specs=P(("ctx", "head"), None), check_vma=False
    )
```

```python
import functools
import math

import jax
import jax.numpy as jnp
from jax import lax
from jax.experimental import pallas as pl
from jax.experimental.pallas import tpu as pltpu
from jax.sharding import PartitionSpec as P

ATT_DIM = 160
WINDOW = 1024
RING = 4
QB = 256
TB = 512
FINAL_ROWS = 32

coef_first = 3.4445
coef_second = -4.775
coef_third = 2.0315
epsilon = 1e-06
LOG2E = 1.4426950408889634
CENTRES = (0.0, 0.0, 0.5, 0.8, 0.8)
F32 = jnp.float32
BF16 = jnp.bfloat16
VMEM_LIMIT = 56 * 1024 * 1024


def params():
    return pltpu.CompilerParams(vmem_limit_bytes=VMEM_LIMIT)


def dot(a, b, dims=((1,), (0,))):
    return lax.dot_general(a, b, (dims, ((), ())), preferred_element_type=F32)


def sigmoid(x):
    return 0.5 * jnp.tanh(0.5 * x) + 0.5


def pick_weights(place, sources, put):
    for j in range(3):
        for s in range(RING):

            @pl.when(lax.rem(place + RING - j, RING) == s)
            def _(j=j, s=s):
                put(j, sources[s][...])


def grads_kernel(static, place_ref, x_ref, v_ref, r_ref, *rest):
    n_src = 3 if static else RING
    sources, (own, s1, s2, s3), (acc, wt) = rest[:n_src], rest[n_src : n_src + 4], rest[-2:]
    step = pl.program_id(0)
    place = place_ref[0]

    @pl.when(step == 0)
    def _():
        def put(j, w):
            wt[j] = w.T

        if static:
            for j in range(3):
                put(j, sources[j][...])
        else:
            pick_weights(place, sources, put)
        acc[...] = jnp.zeros_like(acc)

    x = x_ref[...]
    if static:
        rest[-4][...] = x
        rest[-3][...] = v_ref[...]
    e = (r_ref[...] * v_ref[...].astype(F32)).astype(BF16)
    gate = dot(wt[0], x)
    up = dot(wt[1], x)
    back = dot(wt[2], e)
    sig = sigmoid(gate)
    gated = gate * sig
    hidden = (gated * up).astype(BF16)
    d_gate = (back * up * (sig + gated * (1.0 - sig))).astype(BF16)
    d_up = (back * gated).astype(BF16)
    nt = ((1,), (1,))
    acc[0] += dot(x, d_gate, nt)
    acc[1] += dot(x, d_up, nt)
    acc[2] += dot(e, hidden, nt)

    @pl.when(step == pl.num_programs(0) - 1)
    def _():
        for shift, out in enumerate((own, s1, s2, s3)):
            out[...] = acc[jnp.minimum(lax.rem(place + shift, RING), 2)].astype(BF16)


def grads(place, xt, vt, rates, sources, static):
    width, count = xt.shape
    matrix = sources[0].shape
    whole = pl.BlockSpec(matrix, lambda i, p: (0, 0))
    tokens = pl.BlockSpec((width, TB), lambda i, p: (0, i))
    hidden = matrix[1]
    steps = count // TB
    rim = WINDOW // TB
    tails = [pl.BlockSpec((width, TB), lambda i, p: (0, jnp.maximum(i - (steps - rim), 0)))] * 2
    return pl.pallas_call(
        functools.partial(grads_kernel, static),
        grid_spec=pltpu.PrefetchScalarGridSpec(
            num_scalar_prefetch=1,
            grid=(steps,),
            in_specs=[tokens, tokens, pl.BlockSpec((1, TB), lambda i, p: (0, i))]
            + [whole] * len(sources),
            out_specs=[whole] * 4 + (tails if static else []),
            scratch_shapes=[
                pltpu.VMEM((3,) + matrix, F32),
                pltpu.VMEM((3, hidden, width), BF16),
            ],
        ),
        out_shape=[jax.ShapeDtypeStruct(matrix, BF16)] * 4
        + [jax.ShapeDtypeStruct((width, WINDOW), BF16)] * (2 if static else 0),
        compiler_params=params(),
        cost_estimate=pl.CostEstimate(
            flops=12 * width * hidden * count,
            bytes_accessed=4 * width * count,
            transcendentals=hidden * count,
        ),
    )(place, xt, vt, rates, *sources)


def update_kernel(place_ref, step_ref, own, r1, r2, r3, *rest):
    olds, out = rest[:-1], rest[-1]
    place = place_ref[0]
    if len(olds) == 3:
        old = jnp.where(
            place == 0, olds[0][...], jnp.where(place == 1, olds[1][...], olds[2][...])
        )
    else:
        old = olds[0][...]
    g = own[...].astype(F32) + r1[...].astype(F32) + r2[...].astype(F32) + r3[...].astype(F32)
    x = g * lax.rsqrt(jnp.sum(g * g) + epsilon)
    rows = g.shape[0]
    diagonal = lax.broadcasted_iota(jnp.int32, (rows, rows), 0) == lax.broadcasted_iota(
        jnp.int32, (rows, rows), 1
    )
    for c in CENTRES:
        xb = x.astype(BF16)
        e = dot(xb, xb, ((1,), (1,)))
        if c:
            e = e - jnp.where(diagonal, c, 0.0)
        eb = e.astype(BF16)
        mix = (coef_second + 2.0 * c * coef_third) * e + coef_third * dot(eb, eb)
        k = coef_first + coef_second * c + coef_third * c * c
        x = k * x + dot(mix.astype(BF16), xb)
    out[...] = (old.astype(F32) + step_ref[0] * x).astype(BF16)


def update(place, step, pieces, olds):
    matrix = pieces[0].shape
    smem = pl.BlockSpec(memory_space=pltpu.SMEM)
    vmem = pl.BlockSpec(memory_space=pltpu.VMEM)
    return pl.pallas_call(
        update_kernel,
        in_specs=[smem, smem] + [vmem] * (4 + len(olds)),
        out_specs=vmem,
        out_shape=jax.ShapeDtypeStruct(matrix, BF16),
        compiler_params=params(),
        cost_estimate=pl.CostEstimate(
            flops=5 * 2 * 5 * matrix[0] * matrix[0] * matrix[0],
            bytes_accessed=16 * matrix[0] * matrix[1],
            transcendentals=0,
        ),
    )(place, step, *pieces, *olds)


def attend_kernel(blocks, kb_first, first_ref, q_ref, k_ref, v_ref, *rest):
    if kb_first is None:
        (out, k_nat) = rest
        rims = ()
    else:
        (rim_k, rim_v, _, out, k_nat) = rest
        rims = (rim_k, rim_v)
    step = pl.program_id(0)
    heads = q_ref.shape[0] // ATT_DIM
    chunks = WINDOW // QB + 1
    rim_blocks = WINDOW // QB if rims else 0

    @pl.when(step == 0)
    def _():
        if rims:
            for h in range(heads):
                k_nat[h, :WINDOW, :] = rims[0][pl.ds(h * ATT_DIM, ATT_DIM), :].T
        for h in range(heads):
            k_nat[h, rim_blocks * QB :, :] = k_ref[pl.ds(h * ATT_DIM, ATT_DIM), :].T

    later = lax.broadcasted_iota(jnp.int32, (QB, QB), 0) > lax.broadcasted_iota(
        jnp.int32, (QB, QB), 1
    )
    scale = LOG2E / math.sqrt(ATT_DIM)
    low = -1e30

    def values(h, block):
        return v_ref[pl.ds(h * ATT_DIM, ATT_DIM), pl.ds(pl.multiple_of(block * QB, QB), QB)]

    def body(i, fresh):
        for h in range(heads):
            q = q_ref[pl.ds(h * ATT_DIM, ATT_DIM), :]
            s = []
            for c in range(chunks):
                k = k_nat[h, pl.ds(pl.multiple_of((i + c) * QB, QB), QB), :]
                part = dot(k, q)
                if c == 0:
                    part = jnp.where(later, part, low)
                elif c == chunks - 1:
                    part = jnp.where(later, low, part)
                if c < fresh:
                    part = jnp.where(first_ref[0] == 1, low, part)
                s.append(part)
            top = functools.reduce(
                jnp.maximum, [jnp.max(part, axis=0, keepdims=True) for part in s]
            )
            total = jnp.zeros((1, QB), F32)
            result = jnp.zeros((ATT_DIM, QB), F32)
            for c in range(chunks):
                expo = jnp.exp2((s[c] - top) * scale)
                total += jnp.sum(expo, axis=0, keepdims=True)
                if c < fresh:
                    v = rims[1][pl.ds(h * ATT_DIM, ATT_DIM), pl.ds((i + c) * QB, QB)]
                else:
                    v = values(h, i + c - rim_blocks)
                result += dot(v, expo.astype(BF16))
            out[pl.ds(h * ATT_DIM, ATT_DIM), :] = result / total

    if rims:
        for i in range(blocks):

            @pl.when(step == i)
            def _(i=i):
                body(i, rim_blocks - i)
    else:
        body(step, 0)


def attend_main(qt, kt, vt, first):
    width, count = qt.shape
    skip = WINDOW // QB
    blocks = count // QB - skip
    heads = width // ATT_DIM
    whole = pl.BlockSpec((width, count), lambda i, f: (0, 0))
    return pl.pallas_call(
        functools.partial(attend_kernel, blocks, None),
        grid_spec=pltpu.PrefetchScalarGridSpec(
            num_scalar_prefetch=1,
            grid=(blocks,),
            in_specs=[pl.BlockSpec((width, QB), lambda i, f: (0, i + skip)), whole, whole],
            out_specs=pl.BlockSpec((width, QB), lambda i, f: (0, i + skip)),
            scratch_shapes=[pltpu.VMEM((heads, count, ATT_DIM), BF16)],
        ),
        out_shape=jax.ShapeDtypeStruct((width, count), F32),
        compiler_params=params(),
        cost_estimate=pl.CostEstimate(
            flops=4 * blocks * QB * (WINDOW + QB) * width,
            bytes_accessed=10 * width * count,
            transcendentals=blocks * QB * (WINDOW + QB) * heads,
        ),
    )(first, qt, kt, vt)


def attend_rim(qt, kt, vt, rim_k, rim_v, main, first):
    width = qt.shape[0]
    blocks = WINDOW // QB
    heads = width // ATT_DIM
    whole = pl.BlockSpec((width, WINDOW), lambda i, f: (0, 0))
    return pl.pallas_call(
        functools.partial(attend_kernel, blocks, 0),
        grid_spec=pltpu.PrefetchScalarGridSpec(
            num_scalar_prefetch=1,
            grid=(blocks,),
            in_specs=[pl.BlockSpec((width, QB), lambda i, f: (0, i))] + [whole] * 4
            + [pl.BlockSpec(memory_space=pl.ANY)],
            out_specs=pl.BlockSpec((width, QB), lambda i, f: (0, i)),
            scratch_shapes=[pltpu.VMEM((heads, 2 * WINDOW, ATT_DIM), BF16)],
        ),
        out_shape=jax.ShapeDtypeStruct(main.shape, F32),
        input_output_aliases={6: 0},
        compiler_params=params(),
        cost_estimate=pl.CostEstimate(
            flops=4 * blocks * QB * (WINDOW + QB) * width,
            bytes_accessed=16 * width * WINDOW,
            transcendentals=blocks * QB * (WINDOW + QB) * heads,
        ),
    )(first, qt, kt, vt, rim_k, rim_v, main)


def pack(rows, out, dests):
    n = rows.shape[0] // (2 * dests)
    width = rows.shape[1]
    for d in range(dests):
        begin = 2 * n * d
        out[d] = jnp.concatenate([rows[begin : begin + n], rows[begin + n : begin + 2 * n]], 1)


def apply_kernel(dests, place_ref, part_ref, q_ref, att_ref, *rest):
    sources, out, (wt, w2) = rest[: 2 * RING], rest[2 * RING], rest[2 * RING + 1 :]

    @pl.when(pl.program_id(0) == 0)
    def _():
        def put(j, w):
            if j < 2:
                wt[j] = w.T
            else:
                w2[...] = w

        for part in range(2):

            @pl.when(part_ref[0] == part)
            def _(part=part):
                pick_weights(place_ref[0], sources[part * RING : (part + 1) * RING], put)

    q = q_ref[...]
    gate = dot(wt[0], q)
    up = dot(wt[1], q)
    hidden = (gate * sigmoid(gate) * up).astype(BF16)
    fast = dot(w2[...], hidden)
    pack((fast + att_ref[...]).astype(BF16).T, out, dests)


def apply_mix(place, part, qt, att, early, late, parts_out):
    width, count = qt.shape
    matrix = early[0].shape
    rows = count // parts_out
    dests = 4
    tokens = pl.BlockSpec((width, dests * rows), lambda i, p, g: (0, i))
    return pl.pallas_call(
        functools.partial(apply_kernel, dests),
        grid_spec=pltpu.PrefetchScalarGridSpec(
            num_scalar_prefetch=2,
            grid=(parts_out // dests,),
            in_specs=[tokens, tokens] + [pl.BlockSpec(matrix, lambda i, p, g: (0, 0))] * 8,
            out_specs=pl.BlockSpec((dests, rows // 2, 2 * width), lambda i, p, g: (i, 0, 0)),
            scratch_shapes=[
                pltpu.VMEM((2, matrix[1], width), BF16),
                pltpu.VMEM(matrix, BF16),
            ],
        ),
        out_shape=jax.ShapeDtypeStruct((parts_out, rows // 2, 2 * width), BF16),
        compiler_params=params(),
        cost_estimate=pl.CostEstimate(
            flops=6 * width * matrix[1] * count,
            bytes_accessed=8 * width * count,
            transcendentals=matrix[1] * count,
        ),
    )(place, part, qt, att, *early, *late)


def gate_kernel(dests, g_ref, out):
    pack(g_ref[...].T, out, dests)


def pack_gate(gt, parts_out):
    width, count = gt.shape
    rows = count // parts_out
    dests = 4
    return pl.pallas_call(
        functools.partial(gate_kernel, dests),
        grid=(parts_out // dests,),
        in_specs=[pl.BlockSpec((width, dests * rows), lambda i: (0, i))],
        out_specs=pl.BlockSpec((dests, rows // 2, 2 * width), lambda i: (i, 0, 0)),
        out_shape=jax.ShapeDtypeStruct((parts_out, rows // 2, 2 * width), BF16),
        compiler_params=params(),
        cost_estimate=pl.CostEstimate(
            flops=0, bytes_accessed=8 * width * count, transcendentals=0
        ),
    )(gt)


def final_kernel(m_ref, g_ref, gain_ref, out):
    heads, rows, double = m_ref.shape
    width = double // 2
    squares = jnp.zeros((rows, double), F32)
    for h in range(heads):
        m = m_ref[h].astype(F32)
        squares += m * m
    left = lax.broadcasted_iota(jnp.int32, (1, double), 1) < width
    mean = 1.0 / (heads * width)
    early = lax.rsqrt(jnp.sum(squares[:, :width], 1, keepdims=True) * mean + epsilon)
    late = lax.rsqrt(jnp.sum(squares[:, width:], 1, keepdims=True) * mean + epsilon)
    factor = jnp.where(left, early, late)
    for h in range(0, heads, 2):
        pair = []
        for j in (h, h + 1):
            g = g_ref[j].astype(F32)
            scale = factor * gain_ref[j : j + 1]
            pair.append((m_ref[j].astype(F32) * scale * (g * sigmoid(g))).astype(BF16))
        cols = slice(h * width, (h + 2) * width)
        out[0, :, cols] = jnp.concatenate([y[:, :width] for y in pair], 1)
        out[1, :, cols] = jnp.concatenate([y[:, width:] for y in pair], 1)


def final(mixed, gates, gain):
    heads, rows, double = mixed.shape
    block = FINAL_ROWS
    wide = heads * double // 2
    gain = gain.reshape(heads, double // 2)
    tokens = pl.BlockSpec((heads, block, double), lambda i: (0, i, 0))
    result = pl.pallas_call(
        final_kernel,
        grid=(rows // block,),
        in_specs=[tokens, tokens, pl.BlockSpec((heads, double), lambda i: (0, 0))],
        out_specs=pl.BlockSpec((2, block, wide), lambda i: (0, i, 0)),
        out_shape=jax.ShapeDtypeStruct((2, rows, wide), BF16),
        compiler_params=params(),
        cost_estimate=pl.CostEstimate(
            flops=20 * rows * wide, bytes_accessed=12 * rows * wide, transcendentals=2 * rows * wide
        ),
    )(mixed, gates, jnp.concatenate([gain, gain], 1))
    return result.reshape(2 * rows, wide)


def reduce_moves(part):
    return [[(part, (m - s) % RING, part, m) for m in range(3)] for s in range(1, RING)]


def spread_moves(parts):
    return [[(p, m, p, (m + s) % RING) for p in parts for m in range(3)] for s in range(1, RING)]


def ring_send(array, moves):
    heads = lax.axis_size("head")

    def index(part, place, head):
        return (part * RING + (place + 2 * (head % 2)) % RING) * heads + head

    pairs = [(index(a, b, h), index(c, d, h)) for a, b, c, d in moves for h in range(heads)]
    return lax.ppermute(array, ("ctx", "head"), pairs)


def send(array, pairs):
    return lax.ppermute(array, "ctx", pairs)


def shards(
    query_rows,
    key_rows,
    value_rows,
    gate_rows,
    token_rates,
    step_sizes,
    fast_first,
    fast_third,
    fast_second,
    norm_gain,
):
    ctx = lax.axis_index("ctx")
    heads = lax.axis_size("head")
    place = ((ctx + 2 * (lax.axis_index("head") % 2)) % RING).reshape(1).astype(jnp.int32)
    part = (ctx // RING).reshape(1).astype(jnp.int32)
    first = (ctx == 0).reshape(1).astype(jnp.int32)
    qt, kt, vt, gt = query_rows.T, key_rows.T, value_rows.T, gate_rows.T
    start = [fast_first[0], fast_third[0], fast_second[0].T]
    hold = lax.optimization_barrier

    own, *out = grads(place, kt, vt, token_rates, start, True)
    out, tails = out[:3], out[3:]
    pieces = [own] + [ring_send(o, p) for o, p in zip(out, reduce_moves(0))]
    rim_late = [send(t, [(i, i + 1) for i in range(4, 7)]) for t in tails]
    att_main = attend_main(qt, kt, vt, first)
    pieces, att_main = hold((pieces, att_main))
    fresh = update(place, step_sizes, pieces, start)
    fresh, gt, rim_late = hold((fresh, gt, rim_late))
    crossed = ring_send(fresh, [(0, m, 1, m) for m in range(3)])
    gates = pack_gate(gt, heads)
    held = jnp.where(part[0] == 0, fresh, crossed)
    held, gates = hold((held, gates))
    gate_tokens = lax.all_to_all(gates, "head", split_axis=0, concat_axis=0)
    early = [held] + [ring_send(held, p) for p in spread_moves((0, 1))]
    early, tails = hold((early, tails))
    rim_early = [send(t, [(i, i + 1) for i in range(4)]) for t in tails]

    own, *out = grads(place, kt, vt, token_rates, early, False)
    own, out, att_main = hold((own, out, att_main))
    pieces = [own] + [ring_send(o, p) for o, p in zip(out, reduce_moves(1))]
    rims = [jnp.where(ctx <= RING, a, b) for a, b in zip(rim_early, rim_late)]
    att = attend_rim(qt, kt, vt, rims[0], rims[1], att_main, first)
    pieces, att = hold((pieces, att))
    fresh = update(place, step_sizes, pieces, [early[0]])
    late = [fresh] + [ring_send(fresh, p) for p in spread_moves((1,))]
    mixed = apply_mix(place, part, qt, att, early, late, heads)
    mixed_tokens = lax.all_to_all(mixed, "head", split_axis=0, concat_axis=0)
    return final(mixed_tokens, gate_tokens, norm_gain)


def solution(mesh):
    placed = (
        P("ctx", "head"),
        P("ctx", "head"),
        P("ctx", "head"),
        P("ctx", "head"),
        P("head", "ctx"),
        P("head"),
        P("head", None, None),
        P("head", None, None),
        P("head", None, None),
        P(),
    )
    return jax.shard_map(
        shards, mesh=mesh, in_specs=placed, out_specs=P(("ctx", "head"), None), check_vma=False
    )
```

```python
import functools
import math

import jax
import jax.numpy as jnp
from jax import lax
from jax.experimental import pallas as pl
from jax.experimental.pallas import tpu as pltpu
from jax.sharding import PartitionSpec as P

ATT_DIM = 160
WINDOW = 1024
RING = 4
QB = 256
TB = 512
FINAL_ROWS = 32
CUT = 256

coef_first = 3.4445
coef_second = -4.775
coef_third = 2.0315
epsilon = 1e-06
LOG2E = 1.4426950408889634
CENTRES = (0.0, 0.0, 0.5, 0.8, 0.8)
F32 = jnp.float32
BF16 = jnp.bfloat16
VMEM_LIMIT = 56 * 1024 * 1024


def params():
    return pltpu.CompilerParams(vmem_limit_bytes=VMEM_LIMIT)


def dot(a, b, dims=((1,), (0,))):
    return lax.dot_general(a, b, (dims, ((), ())), preferred_element_type=F32)


def sigmoid(x):
    return 0.5 * jnp.tanh(0.5 * x) + 0.5


def pick_weights(place, sources, put):
    for j in range(3):
        for s in range(RING):

            @pl.when(lax.rem(place + RING - j, RING) == s)
            def _(j=j, s=s):
                put(j, sources[s][...])


def grads_kernel(span, tails, place_ref, x_ref, v_ref, r_ref, *rest):
    static = span is not None
    n_src = 3 if static else RING
    sources, (own, s1, s2, s3), (acc, wt) = rest[:n_src], rest[n_src : n_src + 4], rest[-2:]
    step = pl.program_id(0)
    place = place_ref[0]

    @pl.when(step == 0)
    def _():
        def put(j, w):
            wt[j] = w.T

        if static:
            for j in range(3):
                put(j, sources[j][:, span])
        else:
            pick_weights(place, sources, put)
        acc[...] = jnp.zeros_like(acc)

    x = x_ref[...]
    if tails:
        rest[-4][...] = x
        rest[-3][...] = v_ref[...]
    e = (r_ref[...] * v_ref[...].astype(F32)).astype(BF16)
    gate = dot(wt[0], x)
    up = dot(wt[1], x)
    back = dot(wt[2], e)
    sig = sigmoid(gate)
    gated = gate * sig
    hidden = (gated * up).astype(BF16)
    d_gate = (back * up * (sig + gated * (1.0 - sig))).astype(BF16)
    d_up = (back * gated).astype(BF16)
    nt = ((1,), (1,))
    acc[0] += dot(x, d_gate, nt)
    acc[1] += dot(x, d_up, nt)
    acc[2] += dot(e, hidden, nt)

    @pl.when(step == pl.num_programs(0) - 1)
    def _():
        for shift, out in enumerate((own, s1, s2, s3)):
            out[...] = acc[jnp.minimum(lax.rem(place + shift, RING), 2)].astype(BF16)


def grads(place, xt, vt, rates, sources, span=None, tails=False):
    width, count = xt.shape
    matrix = sources[0].shape
    hidden = matrix[1] if span is None else span.stop - span.start
    part = (width, hidden)
    tokens = pl.BlockSpec((width, TB), lambda i, p: (0, i))
    steps = count // TB
    rim = WINDOW // TB
    rims = [pl.BlockSpec((width, TB), lambda i, p: (0, jnp.maximum(i - (steps - rim), 0)))] * 2
    return pl.pallas_call(
        functools.partial(grads_kernel, span, tails),
        grid_spec=pltpu.PrefetchScalarGridSpec(
            num_scalar_prefetch=1,
            grid=(steps,),
            in_specs=[tokens, tokens, pl.BlockSpec((1, TB), lambda i, p: (0, i))]
            + [pl.BlockSpec(matrix, lambda i, p: (0, 0))] * len(sources),
            out_specs=[pl.BlockSpec(part, lambda i, p: (0, 0))] * 4 + (rims if tails else []),
            scratch_shapes=[
                pltpu.VMEM((3,) + part, F32),
                pltpu.VMEM((3, hidden, width), BF16),
            ],
        ),
        out_shape=[jax.ShapeDtypeStruct(part, BF16)] * 4
        + [jax.ShapeDtypeStruct((width, WINDOW), BF16)] * (2 if tails else 0),
        compiler_params=params(),
        cost_estimate=pl.CostEstimate(
            flops=12 * width * hidden * count,
            bytes_accessed=4 * width * count,
            transcendentals=hidden * count,
        ),
    )(place, xt, vt, rates, *sources)


def update_kernel(place_ref, step_ref, *refs):
    pieces, olds, outs = refs[: 2 * RING], refs[2 * RING : -2], refs[-2:]
    place = place_ref[0]
    if len(olds) == 3:
        old = jnp.where(
            place == 0, olds[0][...], jnp.where(place == 1, olds[1][...], olds[2][...])
        )
    else:
        old = jnp.concatenate([olds[0][...], olds[1][...]], 1)
    sums = [sum(p[...].astype(F32) for p in pieces[i * RING : (i + 1) * RING]) for i in range(2)]
    g = jnp.concatenate(sums, 1)
    x = g * lax.rsqrt(jnp.sum(g * g) + epsilon)
    rows = g.shape[0]
    diagonal = lax.broadcasted_iota(jnp.int32, (rows, rows), 0) == lax.broadcasted_iota(
        jnp.int32, (rows, rows), 1
    )
    for c in CENTRES:
        xb = x.astype(BF16)
        e = dot(xb, xb, ((1,), (1,)))
        if c:
            e = e - jnp.where(diagonal, c, 0.0)
        eb = e.astype(BF16)
        mix = (coef_second + 2.0 * c * coef_third) * e + coef_third * dot(eb, eb)
        k = coef_first + coef_second * c + coef_third * c * c
        x = k * x + dot(mix.astype(BF16), xb)
    new = (old.astype(F32) + step_ref[0] * x).astype(BF16)
    outs[0][...] = new[:, :CUT]
    outs[1][...] = new[:, CUT:]


def update(place, step, pieces, olds):
    rows = pieces[0].shape[0]
    widths = (CUT, pieces[-1].shape[1])
    smem = pl.BlockSpec(memory_space=pltpu.SMEM)
    vmem = pl.BlockSpec(memory_space=pltpu.VMEM)
    return pl.pallas_call(
        update_kernel,
        in_specs=[smem, smem] + [vmem] * (len(pieces) + len(olds)),
        out_specs=[vmem] * 2,
        out_shape=[jax.ShapeDtypeStruct((rows, w), BF16) for w in widths],
        compiler_params=params(),
        cost_estimate=pl.CostEstimate(
            flops=5 * 2 * 5 * rows * rows * rows,
            bytes_accessed=16 * rows * sum(widths),
            transcendentals=0,
        ),
    )(place, step, *pieces, *olds)


def attend_kernel(blocks, kb_first, first_ref, q_ref, k_ref, v_ref, *rest):
    if kb_first is None:
        (out, k_nat) = rest
        rims = ()
    else:
        (rim_k, rim_v, _, out, k_nat) = rest
        rims = (rim_k, rim_v)
    step = pl.program_id(0)
    heads = q_ref.shape[0] // ATT_DIM
    chunks = WINDOW // QB + 1
    rim_blocks = WINDOW // QB if rims else 0

    @pl.when(step == 0)
    def _():
        if rims:
            for h in range(heads):
                k_nat[h, :WINDOW, :] = rims[0][pl.ds(h * ATT_DIM, ATT_DIM), :].T
        for h in range(heads):
            k_nat[h, rim_blocks * QB :, :] = k_ref[pl.ds(h * ATT_DIM, ATT_DIM), :].T

    later = lax.broadcasted_iota(jnp.int32, (QB, QB), 0) > lax.broadcasted_iota(
        jnp.int32, (QB, QB), 1
    )
    scale = LOG2E / math.sqrt(ATT_DIM)
    low = -1e30

    def values(h, block):
        return v_ref[pl.ds(h * ATT_DIM, ATT_DIM), pl.ds(pl.multiple_of(block * QB, QB), QB)]

    def body(i, fresh):
        for h in range(heads):
            q = q_ref[pl.ds(h * ATT_DIM, ATT_DIM), :]
            s = []
            for c in range(chunks):
                k = k_nat[h, pl.ds(pl.multiple_of((i + c) * QB, QB), QB), :]
                part = dot(k, q)
                if c == 0:
                    part = jnp.where(later, part, low)
                elif c == chunks - 1:
                    part = jnp.where(later, low, part)
                if c < fresh:
                    part = jnp.where(first_ref[0] == 1, low, part)
                s.append(part)
            top = functools.reduce(
                jnp.maximum, [jnp.max(part, axis=0, keepdims=True) for part in s]
            )
            total = jnp.zeros((1, QB), F32)
            result = jnp.zeros((ATT_DIM, QB), F32)
            for c in range(chunks):
                expo = jnp.exp2((s[c] - top) * scale)
                total += jnp.sum(expo, axis=0, keepdims=True)
                if c < fresh:
                    v = rims[1][pl.ds(h * ATT_DIM, ATT_DIM), pl.ds((i + c) * QB, QB)]
                else:
                    v = values(h, i + c - rim_blocks)
                result += dot(v, expo.astype(BF16))
            out[pl.ds(h * ATT_DIM, ATT_DIM), :] = result / total

    if rims:
        for i in range(blocks):

            @pl.when(step == i)
            def _(i=i):
                body(i, rim_blocks - i)
    else:
        body(step, 0)


def attend_main(qt, kt, vt, first):
    width, count = qt.shape
    skip = WINDOW // QB
    blocks = count // QB - skip
    heads = width // ATT_DIM
    whole = pl.BlockSpec((width, count), lambda i, f: (0, 0))
    return pl.pallas_call(
        functools.partial(attend_kernel, blocks, None),
        grid_spec=pltpu.PrefetchScalarGridSpec(
            num_scalar_prefetch=1,
            grid=(blocks,),
            in_specs=[pl.BlockSpec((width, QB), lambda i, f: (0, i + skip)), whole, whole],
            out_specs=pl.BlockSpec((width, QB), lambda i, f: (0, i + skip)),
            scratch_shapes=[pltpu.VMEM((heads, count, ATT_DIM), BF16)],
        ),
        out_shape=jax.ShapeDtypeStruct((width, count), F32),
        compiler_params=params(),
        cost_estimate=pl.CostEstimate(
            flops=4 * blocks * QB * (WINDOW + QB) * width,
            bytes_accessed=10 * width * count,
            transcendentals=blocks * QB * (WINDOW + QB) * heads,
        ),
    )(first, qt, kt, vt)


def attend_rim(qt, kt, vt, rim_k, rim_v, main, first):
    width = qt.shape[0]
    blocks = WINDOW // QB
    heads = width // ATT_DIM
    whole = pl.BlockSpec((width, WINDOW), lambda i, f: (0, 0))
    return pl.pallas_call(
        functools.partial(attend_kernel, blocks, 0),
        grid_spec=pltpu.PrefetchScalarGridSpec(
            num_scalar_prefetch=1,
            grid=(blocks,),
            in_specs=[pl.BlockSpec((width, QB), lambda i, f: (0, i))] + [whole] * 4
            + [pl.BlockSpec(memory_space=pl.ANY)],
            out_specs=pl.BlockSpec((width, QB), lambda i, f: (0, i)),
            scratch_shapes=[pltpu.VMEM((heads, 2 * WINDOW, ATT_DIM), BF16)],
        ),
        out_shape=jax.ShapeDtypeStruct(main.shape, F32),
        input_output_aliases={6: 0},
        compiler_params=params(),
        cost_estimate=pl.CostEstimate(
            flops=4 * blocks * QB * (WINDOW + QB) * width,
            bytes_accessed=16 * width * WINDOW,
            transcendentals=blocks * QB * (WINDOW + QB) * heads,
        ),
    )(first, qt, kt, vt, rim_k, rim_v, main)


def pack(rows, out, dests):
    n = rows.shape[0] // (2 * dests)
    width = rows.shape[1]
    for d in range(dests):
        begin = 2 * n * d
        out[d] = jnp.concatenate([rows[begin : begin + n], rows[begin + n : begin + 2 * n]], 1)


def apply_kernel(dests, place_ref, part_ref, q_ref, att_ref, *rest):
    sources, out, (wt, w2) = rest[: 4 * RING], rest[4 * RING], rest[4 * RING + 1 :]
    spans = (slice(0, CUT), slice(CUT, w2.shape[1]))

    @pl.when(pl.program_id(0) == 0)
    def _():
        for part in range(2):
            for half, span in enumerate(spans):

                def put(j, w, span=span):
                    if j < 2:
                        wt[j, span, :] = w.T
                    else:
                        w2[:, span] = w

                @pl.when(part_ref[0] == part)
                def _(begin=(2 * part + half) * RING, put=put):
                    pick_weights(place_ref[0], sources[begin : begin + RING], put)

    q = q_ref[...]
    gate = dot(wt[0], q)
    up = dot(wt[1], q)
    hidden = (gate * sigmoid(gate) * up).astype(BF16)
    fast = dot(w2[...], hidden)
    pack((fast + att_ref[...]).astype(BF16).T, out, dests)


def apply_mix(place, part, qt, att, sources, parts_out):
    width, count = qt.shape
    matrix = (width, sources[0].shape[1] + sources[RING].shape[1])
    rows = count // parts_out
    dests = 4
    tokens = pl.BlockSpec((width, dests * rows), lambda i, p, g: (0, i))
    return pl.pallas_call(
        functools.partial(apply_kernel, dests),
        grid_spec=pltpu.PrefetchScalarGridSpec(
            num_scalar_prefetch=2,
            grid=(parts_out // dests,),
            in_specs=[tokens, tokens]
            + [pl.BlockSpec(w.shape, lambda i, p, g: (0, 0)) for w in sources],
            out_specs=pl.BlockSpec((dests, rows // 2, 2 * width), lambda i, p, g: (i, 0, 0)),
            scratch_shapes=[
                pltpu.VMEM((2, matrix[1], width), BF16),
                pltpu.VMEM(matrix, BF16),
            ],
        ),
        out_shape=jax.ShapeDtypeStruct((parts_out, rows // 2, 2 * width), BF16),
        compiler_params=params(),
        cost_estimate=pl.CostEstimate(
            flops=6 * width * matrix[1] * count,
            bytes_accessed=8 * width * count,
            transcendentals=matrix[1] * count,
        ),
    )(place, part, qt, att, *sources)


def gate_kernel(dests, g_ref, out):
    pack(g_ref[...].T, out, dests)


def pack_gate(gt, parts_out):
    width, count = gt.shape
    rows = count // parts_out
    dests = 4
    return pl.pallas_call(
        functools.partial(gate_kernel, dests),
        grid=(parts_out // dests,),
        in_specs=[pl.BlockSpec((width, dests * rows), lambda i: (0, i))],
        out_specs=pl.BlockSpec((dests, rows // 2, 2 * width), lambda i: (i, 0, 0)),
        out_shape=jax.ShapeDtypeStruct((parts_out, rows // 2, 2 * width), BF16),
        compiler_params=params(),
        cost_estimate=pl.CostEstimate(
            flops=0, bytes_accessed=8 * width * count, transcendentals=0
        ),
    )(gt)


def final_kernel(m_ref, g_ref, gain_ref, out):
    heads, rows, double = m_ref.shape
    width = double // 2
    squares = jnp.zeros((rows, double), F32)
    for h in range(heads):
        m = m_ref[h].astype(F32)
        squares += m * m
    left = lax.broadcasted_iota(jnp.int32, (1, double), 1) < width
    mean = 1.0 / (heads * width)
    early = lax.rsqrt(jnp.sum(squares[:, :width], 1, keepdims=True) * mean + epsilon)
    late = lax.rsqrt(jnp.sum(squares[:, width:], 1, keepdims=True) * mean + epsilon)
    factor = jnp.where(left, early, late)
    for h in range(0, heads, 2):
        pair = []
        for j in (h, h + 1):
            g = g_ref[j].astype(F32)
            scale = factor * gain_ref[j : j + 1]
            pair.append((m_ref[j].astype(F32) * scale * (g * sigmoid(g))).astype(BF16))
        cols = slice(h * width, (h + 2) * width)
        out[0, :, cols] = jnp.concatenate([y[:, :width] for y in pair], 1)
        out[1, :, cols] = jnp.concatenate([y[:, width:] for y in pair], 1)


def final(mixed, gates, gain):
    heads, rows, double = mixed.shape
    block = FINAL_ROWS
    wide = heads * double // 2
    gain = gain.reshape(heads, double // 2)
    tokens = pl.BlockSpec((heads, block, double), lambda i: (0, i, 0))
    result = pl.pallas_call(
        final_kernel,
        grid=(rows // block,),
        in_specs=[tokens, tokens, pl.BlockSpec((heads, double), lambda i: (0, 0))],
        out_specs=pl.BlockSpec((2, block, wide), lambda i: (0, i, 0)),
        out_shape=jax.ShapeDtypeStruct((2, rows, wide), BF16),
        compiler_params=params(),
        cost_estimate=pl.CostEstimate(
            flops=20 * rows * wide, bytes_accessed=12 * rows * wide, transcendentals=2 * rows * wide
        ),
    )(mixed, gates, jnp.concatenate([gain, gain], 1))
    return result.reshape(2 * rows, wide)


def reduce_moves(part):
    return [[(part, (m - s) % RING, part, m) for m in range(3)] for s in range(1, RING)]


def spread_moves(parts):
    return [[(p, m, p, (m + s) % RING) for p in parts for m in range(3)] for s in range(1, RING)]


def ring_send(array, moves):
    heads = lax.axis_size("head")

    def index(part, place, head):
        return (part * RING + (place + 2 * (head % 2)) % RING) * heads + head

    pairs = [(index(a, b, h), index(c, d, h)) for a, b, c, d in moves for h in range(heads)]
    return lax.ppermute(array, ("ctx", "head"), pairs)


def send(array, pairs):
    return lax.ppermute(array, "ctx", pairs)


def shards(
    query_rows,
    key_rows,
    value_rows,
    gate_rows,
    token_rates,
    step_sizes,
    fast_first,
    fast_third,
    fast_second,
    norm_gain,
):
    ctx = lax.axis_index("ctx")
    heads = lax.axis_size("head")
    place = ((ctx + 2 * (lax.axis_index("head") % 2)) % RING).reshape(1).astype(jnp.int32)
    part = (ctx // RING).reshape(1).astype(jnp.int32)
    first = (ctx == 0).reshape(1).astype(jnp.int32)
    qt, kt, vt, gt = query_rows.T, key_rows.T, value_rows.T, gate_rows.T
    start = [fast_first[0], fast_third[0], fast_second[0].T]
    hold = lax.optimization_barrier

    hidden = start[0].shape[1]

    own_a, *out_a = grads(place, kt, vt, token_rates, start, slice(0, CUT), True)
    out_a, tails = out_a[:3], out_a[3:]
    pieces_a = [own_a] + [ring_send(o, p) for o, p in zip(out_a, reduce_moves(0))]
    own_a, v_next = hold((own_a, vt))
    own_b, *out_b = grads(place, kt, v_next, token_rates, start, slice(CUT, hidden))
    pieces_b = [own_b] + [ring_send(o, p) for o, p in zip(out_b, reduce_moves(0))]
    rim_late = [send(t, [(i, i + 1) for i in range(4, 7)]) for t in tails]
    q_main, own_b = hold((qt, own_b))
    att_main = attend_main(q_main, kt, vt, first)
    pieces_a, pieces_b, att_main = hold((pieces_a, pieces_b, att_main))
    fresh = update(place, step_sizes, pieces_a + pieces_b, start)
    fresh, gt, rim_late = hold((fresh, gt, rim_late))
    gates = pack_gate(gt, heads)
    crossed = [ring_send(f, [(0, m, 1, m) for m in range(3)]) for f in fresh]
    held = [jnp.where(part[0] == 0, f, c) for f, c in zip(fresh, crossed)]
    moves = spread_moves((0, 1))
    early_a = [held[0]] + [ring_send(held[0], p) for p in moves]
    early_b = [held[1]] + [ring_send(held[1], p) for p in moves]
    early_b[0], gates = hold((early_b[0], gates))
    gate_tokens = lax.all_to_all(gates, "head", split_axis=0, concat_axis=0)

    own_a, *out_a = grads(place, kt, vt, token_rates, early_a)
    pieces_a = [own_a] + [ring_send(o, p) for o, p in zip(out_a, reduce_moves(1))]
    own_a, early_b, tails = hold((own_a, early_b, tails))
    rim_early = [send(t, [(i, i + 1) for i in range(4)]) for t in tails]
    own_b, *out_b = grads(place, kt, vt, token_rates, early_b)
    pieces_b = [own_b] + [ring_send(o, p) for o, p in zip(out_b, reduce_moves(1))]
    fresh = update(place, step_sizes, pieces_a + pieces_b, [early_a[0], early_b[0]])
    fresh, att_main = hold((fresh, att_main))
    late = [[f] + [ring_send(f, p) for p in spread_moves((1,))] for f in fresh]
    rims = [jnp.where(ctx <= RING, a, b) for a, b in zip(rim_early, rim_late)]
    att = attend_rim(qt, kt, vt, rims[0], rims[1], att_main, first)
    mixed = apply_mix(place, part, qt, att, early_a + early_b + late[0] + late[1], heads)
    mixed_tokens = lax.all_to_all(mixed, "head", split_axis=0, concat_axis=0)
    return final(mixed_tokens, gate_tokens, norm_gain)


def solution(mesh):
    placed = (
        P("ctx", "head"),
        P("ctx", "head"),
        P("ctx", "head"),
        P("ctx", "head"),
        P("head", "ctx"),
        P("head"),
        P("head", None, None),
        P("head", None, None),
        P("head", None, None),
        P(),
    )
    return jax.shard_map(
        shards, mesh=mesh, in_specs=placed, out_specs=P(("ctx", "head"), None), check_vma=False
    )
```

```python
import functools
import math

import jax
import jax.numpy as jnp
from jax import lax
from jax.experimental import pallas as pl
from jax.experimental.pallas import tpu as pltpu
from jax.sharding import PartitionSpec as P

ATT_DIM = 160
WINDOW = 1024
RING = 4
QB = 256
TB = 1536
SB = 512
FINAL_ROWS = 32

coef_first = 3.4445
coef_second = -4.775
coef_third = 2.0315
epsilon = 1e-06
LOG2E = 1.4426950408889634
CENTRES = (0.0, 0.0, 0.5, 0.8, 0.8)
F32 = jnp.float32
BF16 = jnp.bfloat16
VMEM_LIMIT = 56 * 1024 * 1024


def params():
    return pltpu.CompilerParams(vmem_limit_bytes=VMEM_LIMIT)


def dot(a, b, dims=((1,), (0,))):
    return lax.dot_general(a, b, (dims, ((), ())), preferred_element_type=F32)


def sigmoid(x):
    return 0.5 * jnp.tanh(0.5 * x) + 0.5


def pick_weights(place, sources, put):
    for j in range(3):
        for s in range(RING):

            @pl.when(lax.rem(place + RING - j, RING) == s)
            def _(j=j, s=s):
                put(j, sources[s][...])


def grads_kernel(static, place_ref, x_ref, v_ref, r_ref, *rest):
    n_src = 3 if static else RING
    sources, outs, rest = rest[:n_src], rest[n_src : n_src + 4], rest[n_src + 4 :]
    acc, wt, d_gate, d_up, hidden, scaled = rest[-6:]
    step = pl.program_id(0)
    last = pl.num_programs(0) - 1
    place = place_ref[0]
    width, count = x_ref.shape

    @pl.when(step == 0)
    def _():
        def put(j, w):
            wt[j] = (w * 0.5 if j == 0 else w).T

        if static:
            for j in range(3):
                put(j, sources[j][...])
        else:
            pick_weights(place, sources, put)
        acc[...] = jnp.zeros_like(acc)

    def forward(span):
        x = x_ref[:, span]
        e = (r_ref[:, span] * v_ref[:, span].astype(F32)).astype(BF16)
        scaled[:, span] = e
        half = dot(wt[0], x)
        up = dot(wt[1], x)
        back = dot(wt[2], e)
        both = 1.0 + jnp.tanh(half)
        gated = half * both
        slope = both * (half + half + 1.0 - gated)
        hidden[:, span] = (gated * up).astype(BF16)
        d_up[:, span] = (back * gated).astype(BF16)
        d_gate[:, span] = (back * up * slope).astype(BF16)

    def backward(span):
        nt = ((1,), (1,))
        x = x_ref[:, span]
        acc[0] += dot(x, d_gate[:, span], nt)
        acc[1] += dot(x, d_up[:, span], nt)
        acc[2] += dot(scaled[:, span], hidden[:, span], nt)

    spans = [slice(b, b + SB) for b in range(0, count, SB)]
    for i, span in enumerate(spans):
        forward(span)
        if i:
            backward(spans[i - 1])
    backward(spans[-1])

    @pl.when(step == last)
    def _():
        if static:
            rim = slice(count - WINDOW, count)
            rest[0][:width] = x_ref[:, rim]
            rest[0][width:] = v_ref[:, rim]
        for shift, out in enumerate(outs):
            j = jnp.minimum(lax.rem(place + shift, RING), 2)
            out[...] = (acc[j] * jnp.where(j == 0, 0.5, 1.0)).astype(BF16)


def grads(place, xt, vt, rates, sources, static):
    width, count = xt.shape
    matrix = sources[0].shape
    whole = pl.BlockSpec(matrix, lambda i, p: (0, 0))
    tokens = pl.BlockSpec((width, TB), lambda i, p: (0, i))
    hidden = matrix[1]
    rim = (2 * width, WINDOW)
    return pl.pallas_call(
        functools.partial(grads_kernel, static),
        grid_spec=pltpu.PrefetchScalarGridSpec(
            num_scalar_prefetch=1,
            grid=(count // TB,),
            in_specs=[tokens, tokens, pl.BlockSpec((1, TB), lambda i, p: (0, i))]
            + [whole] * len(sources),
            out_specs=[whole] * 4 + ([pl.BlockSpec(rim, lambda i, p: (0, 0))] if static else []),
            scratch_shapes=[
                pltpu.VMEM((3,) + matrix, F32),
                pltpu.VMEM((3, hidden, width), BF16),
            ]
            + [pltpu.VMEM((hidden, TB), BF16)] * 3
            + [pltpu.VMEM((width, TB), BF16)],
        ),
        out_shape=[jax.ShapeDtypeStruct(matrix, BF16)] * 4
        + ([jax.ShapeDtypeStruct(rim, BF16)] if static else []),
        compiler_params=params(),
        cost_estimate=pl.CostEstimate(
            flops=12 * width * hidden * count,
            bytes_accessed=4 * width * count,
            transcendentals=hidden * count,
        ),
    )(place, xt, vt, rates, *sources)


def update_kernel(place_ref, step_ref, own, r1, r2, r3, *rest):
    olds, out = rest[:-1], rest[-1]
    place = place_ref[0]
    if len(olds) == 3:
        old = jnp.where(
            place == 0, olds[0][...], jnp.where(place == 1, olds[1][...], olds[2][...])
        )
    else:
        old = olds[0][...]
    g = own[...].astype(F32) + r1[...].astype(F32) + r2[...].astype(F32) + r3[...].astype(F32)
    x = g * lax.rsqrt(jnp.sum(g * g) + epsilon)
    rows = g.shape[0]
    diagonal = lax.broadcasted_iota(jnp.int32, (rows, rows), 0) == lax.broadcasted_iota(
        jnp.int32, (rows, rows), 1
    )
    for c in CENTRES:
        xb = x.astype(BF16)
        e = dot(xb, xb, ((1,), (1,)))
        if c:
            e = e - jnp.where(diagonal, c, 0.0)
        eb = e.astype(BF16)
        mix = (coef_second + 2.0 * c * coef_third) * e + coef_third * dot(eb, eb)
        k = coef_first + coef_second * c + coef_third * c * c
        x = k * x + dot(mix.astype(BF16), xb)
    out[...] = (old.astype(F32) + step_ref[0] * x).astype(BF16)


def update(place, step, pieces, olds):
    matrix = pieces[0].shape
    smem = pl.BlockSpec(memory_space=pltpu.SMEM)
    vmem = pl.BlockSpec(memory_space=pltpu.VMEM)
    return pl.pallas_call(
        update_kernel,
        in_specs=[smem, smem] + [vmem] * (4 + len(olds)),
        out_specs=vmem,
        out_shape=jax.ShapeDtypeStruct(matrix, BF16),
        compiler_params=params(),
        cost_estimate=pl.CostEstimate(
            flops=5 * 2 * 5 * matrix[0] * matrix[0] * matrix[0],
            bytes_accessed=16 * matrix[0] * matrix[1],
            transcendentals=0,
        ),
    )(place, step, *pieces, *olds)


def attend_kernel(blocks, kb_first, first_ref, q_ref, k_ref, v_ref, *rest):
    if kb_first is None:
        (out, k_nat) = rest
        rims = ()
    else:
        (rim, _, out, k_nat) = rest
        width = q_ref.shape[0]
        rims = (rim.at[:width], rim.at[width:])
    step = pl.program_id(0)
    heads = q_ref.shape[0] // ATT_DIM
    chunks = WINDOW // QB + 1
    rim_blocks = WINDOW // QB if rims else 0

    @pl.when(step == 0)
    def _():
        if rims:
            for h in range(heads):
                k_nat[h, :WINDOW, :] = rims[0][pl.ds(h * ATT_DIM, ATT_DIM), :].T
        for h in range(heads):
            k_nat[h, rim_blocks * QB :, :] = k_ref[pl.ds(h * ATT_DIM, ATT_DIM), :].T

    later = lax.broadcasted_iota(jnp.int32, (QB, QB), 0) > lax.broadcasted_iota(
        jnp.int32, (QB, QB), 1
    )
    scale = LOG2E / math.sqrt(ATT_DIM)
    low = -1e30

    def values(h, block):
        return v_ref[pl.ds(h * ATT_DIM, ATT_DIM), pl.ds(pl.multiple_of(block * QB, QB), QB)]

    def body(i, fresh):
        for h in range(heads):
            q = q_ref[pl.ds(h * ATT_DIM, ATT_DIM), :]
            s = []
            for c in range(chunks):
                k = k_nat[h, pl.ds(pl.multiple_of((i + c) * QB, QB), QB), :]
                part = dot(k, q)
                if c == 0:
                    part = jnp.where(later, part, low)
                elif c == chunks - 1:
                    part = jnp.where(later, low, part)
                if c < fresh:
                    part = jnp.where(first_ref[0] == 1, low, part)
                s.append(part)
            top = functools.reduce(
                jnp.maximum, [jnp.max(part, axis=0, keepdims=True) for part in s]
            )
            total = jnp.zeros((1, QB), F32)
            result = jnp.zeros((ATT_DIM, QB), F32)
            for c in range(chunks):
                expo = jnp.exp2((s[c] - top) * scale)
                total += jnp.sum(expo, axis=0, keepdims=True)
                if c < fresh:
                    v = rims[1][pl.ds(h * ATT_DIM, ATT_DIM), pl.ds((i + c) * QB, QB)]
                else:
                    v = values(h, i + c - rim_blocks)
                result += dot(v, expo.astype(BF16))
            out[pl.ds(h * ATT_DIM, ATT_DIM), :] = result / total

    if rims:
        for i in range(blocks):

            @pl.when(step == i)
            def _(i=i):
                body(i, rim_blocks - i)
    else:
        body(step, 0)


def attend_main(qt, kt, vt, first):
    width, count = qt.shape
    skip = WINDOW // QB
    blocks = count // QB - skip
    heads = width // ATT_DIM
    whole = pl.BlockSpec((width, count), lambda i, f: (0, 0))
    return pl.pallas_call(
        functools.partial(attend_kernel, blocks, None),
        grid_spec=pltpu.PrefetchScalarGridSpec(
            num_scalar_prefetch=1,
            grid=(blocks,),
            in_specs=[pl.BlockSpec((width, QB), lambda i, f: (0, i + skip)), whole, whole],
            out_specs=pl.BlockSpec((width, QB), lambda i, f: (0, i + skip)),
            scratch_shapes=[pltpu.VMEM((heads, count, ATT_DIM), BF16)],
        ),
        out_shape=jax.ShapeDtypeStruct((width, count), F32),
        compiler_params=params(),
        cost_estimate=pl.CostEstimate(
            flops=4 * blocks * QB * (WINDOW + QB) * width,
            bytes_accessed=10 * width * count,
            transcendentals=blocks * QB * (WINDOW + QB) * heads,
        ),
    )(first, qt, kt, vt)


def attend_rim(qt, kt, vt, rim, main, first):
    width = qt.shape[0]
    blocks = WINDOW // QB
    heads = width // ATT_DIM
    whole = pl.BlockSpec((width, WINDOW), lambda i, f: (0, 0))
    return pl.pallas_call(
        functools.partial(attend_kernel, blocks, 0),
        grid_spec=pltpu.PrefetchScalarGridSpec(
            num_scalar_prefetch=1,
            grid=(blocks,),
            in_specs=[pl.BlockSpec((width, QB), lambda i, f: (0, i))] + [whole] * 2
            + [
                pl.BlockSpec(rim.shape, lambda i, f: (0, 0)),
                pl.BlockSpec(memory_space=pl.ANY),
            ],
            out_specs=pl.BlockSpec((width, QB), lambda i, f: (0, i)),
            scratch_shapes=[pltpu.VMEM((heads, 2 * WINDOW, ATT_DIM), BF16)],
        ),
        out_shape=jax.ShapeDtypeStruct(main.shape, F32),
        input_output_aliases={5: 0},
        compiler_params=params(),
        cost_estimate=pl.CostEstimate(
            flops=4 * blocks * QB * (WINDOW + QB) * width,
            bytes_accessed=16 * width * WINDOW,
            transcendentals=blocks * QB * (WINDOW + QB) * heads,
        ),
    )(first, qt, kt, vt, rim, main)


def pack(rows, out, dests):
    n = rows.shape[0] // (2 * dests)
    width = rows.shape[1]
    for d in range(dests):
        begin = 2 * n * d
        out[d] = jnp.concatenate([rows[begin : begin + n], rows[begin + n : begin + 2 * n]], 1)


def apply_kernel(dests, place_ref, part_ref, q_ref, att_ref, *rest):
    sources, out, (wt, w2) = rest[: 2 * RING], rest[2 * RING], rest[2 * RING + 1 :]

    @pl.when(pl.program_id(0) == 0)
    def _():
        def put(j, w):
            if j < 2:
                wt[j] = (w * 0.5 if j == 0 else w).T
            else:
                w2[...] = w

        for part in range(2):

            @pl.when(part_ref[0] == part)
            def _(part=part):
                pick_weights(place_ref[0], sources[part * RING : (part + 1) * RING], put)

    q = q_ref[...]
    half = dot(wt[0], q)
    up = dot(wt[1], q)
    hidden = (half * (1.0 + jnp.tanh(half)) * up).astype(BF16)
    fast = dot(w2[...], hidden)
    pack((fast + att_ref[...]).astype(BF16).T, out, dests)


def apply_mix(place, part, qt, att, early, late, parts_out):
    width, count = qt.shape
    matrix = early[0].shape
    rows = count // parts_out
    dests = 4
    tokens = pl.BlockSpec((width, dests * rows), lambda i, p, g: (0, i))
    return pl.pallas_call(
        functools.partial(apply_kernel, dests),
        grid_spec=pltpu.PrefetchScalarGridSpec(
            num_scalar_prefetch=2,
            grid=(parts_out // dests,),
            in_specs=[tokens, tokens] + [pl.BlockSpec(matrix, lambda i, p, g: (0, 0))] * 8,
            out_specs=pl.BlockSpec((dests, rows // 2, 2 * width), lambda i, p, g: (i, 0, 0)),
            scratch_shapes=[
                pltpu.VMEM((2, matrix[1], width), BF16),
                pltpu.VMEM(matrix, BF16),
            ],
        ),
        out_shape=jax.ShapeDtypeStruct((parts_out, rows // 2, 2 * width), BF16),
        compiler_params=params(),
        cost_estimate=pl.CostEstimate(
            flops=6 * width * matrix[1] * count,
            bytes_accessed=8 * width * count,
            transcendentals=matrix[1] * count,
        ),
    )(place, part, qt, att, *early, *late)


def gate_kernel(dests, g_ref, out):
    pack(g_ref[...].T, out, dests)


def pack_gate(gt, parts_out):
    width, count = gt.shape
    rows = count // parts_out
    dests = 4
    return pl.pallas_call(
        functools.partial(gate_kernel, dests),
        grid=(parts_out // dests,),
        in_specs=[pl.BlockSpec((width, dests * rows), lambda i: (0, i))],
        out_specs=pl.BlockSpec((dests, rows // 2, 2 * width), lambda i: (i, 0, 0)),
        out_shape=jax.ShapeDtypeStruct((parts_out, rows // 2, 2 * width), BF16),
        compiler_params=params(),
        cost_estimate=pl.CostEstimate(
            flops=0, bytes_accessed=8 * width * count, transcendentals=0
        ),
    )(gt)


def final_kernel(m_ref, g_ref, gain_ref, out):
    heads, rows, double = m_ref.shape
    width = double // 2
    squares = jnp.zeros((rows, double), F32)
    for h in range(heads):
        m = m_ref[h].astype(F32)
        squares += m * m
    left = lax.broadcasted_iota(jnp.int32, (1, double), 1) < width
    mean = 1.0 / (heads * width)
    early = lax.rsqrt(jnp.sum(squares[:, :width], 1, keepdims=True) * mean + epsilon)
    late = lax.rsqrt(jnp.sum(squares[:, width:], 1, keepdims=True) * mean + epsilon)
    factor = jnp.where(left, early, late)
    for h in range(0, heads, 2):
        pair = []
        for j in (h, h + 1):
            g = g_ref[j].astype(F32)
            scale = factor * gain_ref[j : j + 1]
            pair.append((m_ref[j].astype(F32) * scale * (g * sigmoid(g))).astype(BF16))
        cols = slice(h * width, (h + 2) * width)
        out[0, :, cols] = jnp.concatenate([y[:, :width] for y in pair], 1)
        out[1, :, cols] = jnp.concatenate([y[:, width:] for y in pair], 1)


def final(mixed, gates, gain):
    heads, rows, double = mixed.shape
    block = FINAL_ROWS
    wide = heads * double // 2
    gain = gain.reshape(heads, double // 2)
    tokens = pl.BlockSpec((heads, block, double), lambda i: (0, i, 0))
    result = pl.pallas_call(
        final_kernel,
        grid=(rows // block,),
        in_specs=[tokens, tokens, pl.BlockSpec((heads, double), lambda i: (0, 0))],
        out_specs=pl.BlockSpec((2, block, wide), lambda i: (0, i, 0)),
        out_shape=jax.ShapeDtypeStruct((2, rows, wide), BF16),
        compiler_params=params(),
        cost_estimate=pl.CostEstimate(
            flops=20 * rows * wide, bytes_accessed=12 * rows * wide, transcendentals=2 * rows * wide
        ),
    )(mixed, gates, jnp.concatenate([gain, gain], 1))
    return result.reshape(2 * rows, wide)


def reduce_moves(part):
    return [[(part, (m - s) % RING, part, m) for m in range(3)] for s in range(1, RING)]


def spread_moves(parts):
    return [[(p, m, p, (m + s) % RING) for p in parts for m in range(3)] for s in range(1, RING)]


def ring_send(array, moves):
    heads = lax.axis_size("head")

    def index(part, place, head):
        return (part * RING + (place + 2 * (head % 2)) % RING) * heads + head

    pairs = [(index(a, b, h), index(c, d, h)) for a, b, c, d in moves for h in range(heads)]
    return lax.ppermute(array, ("ctx", "head"), pairs)


def send(array, pairs):
    return lax.ppermute(array, "ctx", pairs)


def shards(
    query_rows,
    key_rows,
    value_rows,
    gate_rows,
    token_rates,
    step_sizes,
    fast_first,
    fast_third,
    fast_second,
    norm_gain,
):
    ctx = lax.axis_index("ctx")
    heads = lax.axis_size("head")
    place = ((ctx + 2 * (lax.axis_index("head") % 2)) % RING).reshape(1).astype(jnp.int32)
    part = (ctx // RING).reshape(1).astype(jnp.int32)
    first = (ctx == 0).reshape(1).astype(jnp.int32)
    qt, kt, vt, gt = query_rows.T, key_rows.T, value_rows.T, gate_rows.T
    start = [fast_first[0], fast_third[0], fast_second[0].T]
    hold = lax.optimization_barrier

    own, *out = grads(place, kt, vt, token_rates, start, True)
    out, tail = out[:3], out[3]
    pieces = [own] + [ring_send(o, p) for o, p in zip(out, reduce_moves(0))]
    rim_late = send(tail, [(i, i + 1) for i in range(4, 7)])
    att_main = attend_main(qt, kt, vt, first)
    pieces, att_main = hold((pieces, att_main))
    fresh = update(place, step_sizes, pieces, start)
    fresh, gt, rim_late = hold((fresh, gt, rim_late))
    crossed = ring_send(fresh, [(0, m, 1, m) for m in range(3)])
    gates = pack_gate(gt, heads)
    held = jnp.where(part[0] == 0, fresh, crossed)
    held, gates = hold((held, gates))
    gate_tokens = lax.all_to_all(gates, "head", split_axis=0, concat_axis=0)
    early = [held] + [ring_send(held, p) for p in spread_moves((0, 1))]
    early[1], tail = hold((early[1], tail))
    rim_early = send(tail, [(i, i + 1) for i in range(4)])

    own, *out = grads(place, kt, vt, token_rates, early, False)
    pieces = [own] + [ring_send(o, p) for o, p in zip(out, reduce_moves(1))]
    fresh = update(place, step_sizes, pieces, [early[0]])
    fresh, att_main = hold((fresh, att_main))
    late = [fresh] + [ring_send(fresh, p) for p in spread_moves((1,))]
    att = attend_rim(qt, kt, vt, jnp.where(ctx <= RING, rim_early, rim_late), att_main, first)
    mixed = apply_mix(place, part, qt, att, early, late, heads)
    mixed_tokens = lax.all_to_all(mixed, "head", split_axis=0, concat_axis=0)
    return final(mixed_tokens, gate_tokens, norm_gain)


def solution(mesh):
    placed = (
        P("ctx", "head"),
        P("ctx", "head"),
        P("ctx", "head"),
        P("ctx", "head"),
        P("head", "ctx"),
        P("head"),
        P("head", None, None),
        P("head", None, None),
        P("head", None, None),
        P(),
    )
    return jax.shard_map(
        shards, mesh=mesh, in_specs=placed, out_specs=P(("ctx", "head"), None), check_vma=False
    )
```

```python
import functools
import math

import jax
import jax.numpy as jnp
from jax import lax
from jax.experimental import pallas as pl
from jax.experimental.pallas import tpu as pltpu
from jax.sharding import PartitionSpec as P

ATT_DIM = 160
WINDOW = 1024
RING = 4
QB = 256
TB = 1536
SB = 512
FINAL_ROWS = 32

coef_first = 3.4445
coef_second = -4.775
coef_third = 2.0315
epsilon = 1e-06
LOG2E = 1.4426950408889634
CENTRES = (0.0, 0.0, 0.5, 0.8, 0.8)
F32 = jnp.float32
BF16 = jnp.bfloat16
VMEM_LIMIT = 56 * 1024 * 1024


def params():
    return pltpu.CompilerParams(vmem_limit_bytes=VMEM_LIMIT)


def dot(a, b, dims=((1,), (0,))):
    return lax.dot_general(a, b, (dims, ((), ())), preferred_element_type=F32)


def sigmoid(x):
    return 0.5 * jnp.tanh(0.5 * x) + 0.5


def pick_weights(place, sources, put):
    for j in range(3):
        for s in range(RING):

            @pl.when(lax.rem(place + RING - j, RING) == s)
            def _(j=j, s=s):
                put(j, sources[s][...])


def grads_kernel(static, place_ref, x_ref, v_ref, r_ref, *rest):
    n_src = 3 if static else RING
    sources, outs, rest = rest[:n_src], rest[n_src : n_src + 4], rest[n_src + 4 :]
    acc, wt, d_gate, d_up, hidden, scaled = rest[-6:]
    step = pl.program_id(0)
    last = pl.num_programs(0) - 1
    place = place_ref[0]
    width, count = x_ref.shape

    @pl.when(step == 0)
    def _():
        def put(j, w):
            wt[j] = (w * 0.5 if j == 0 else w).T

        if static:
            for j in range(3):
                put(j, sources[j][...])
        else:
            pick_weights(place, sources, put)
        acc[...] = jnp.zeros_like(acc)

    def forward(span):
        x = x_ref[:, span]
        e = (r_ref[:, span] * v_ref[:, span].astype(F32)).astype(BF16)
        scaled[:, span] = e
        half = dot(wt[0], x)
        up = dot(wt[1], x)
        back = dot(wt[2], e)
        both = 1.0 + jnp.tanh(half)
        gated = half * both
        slope = both * (half + half + 1.0 - gated)
        hidden[:, span] = (gated * up).astype(BF16)
        d_up[:, span] = (back * gated).astype(BF16)
        d_gate[:, span] = (back * up * slope).astype(BF16)

    def backward(span):
        nt = ((1,), (1,))
        x = x_ref[:, span]
        acc[0] += dot(x, d_gate[:, span], nt)
        acc[1] += dot(x, d_up[:, span], nt)
        acc[2] += dot(scaled[:, span], hidden[:, span], nt)

    spans = [slice(b, b + SB) for b in range(0, count, SB)]
    for i, span in enumerate(spans):
        forward(span)
        if i:
            backward(spans[i - 1])
    backward(spans[-1])

    @pl.when(step == last)
    def _():
        if static:
            rim = slice(count - WINDOW, count)
            rest[0][:width] = x_ref[:, rim]
            rest[0][width:] = v_ref[:, rim]
        for shift, out in enumerate(outs):
            j = jnp.minimum(lax.rem(place + shift, RING), 2)
            out[...] = (acc[j] * jnp.where(j == 0, 0.5, 1.0)).astype(BF16)


def grads(place, xt, vt, rates, sources, static):
    width, count = xt.shape
    matrix = sources[0].shape
    whole = pl.BlockSpec(matrix, lambda i, p: (0, 0))
    tokens = pl.BlockSpec((width, TB), lambda i, p: (0, i))
    hidden = matrix[1]
    rim = (2 * width, WINDOW)
    return pl.pallas_call(
        functools.partial(grads_kernel, static),
        grid_spec=pltpu.PrefetchScalarGridSpec(
            num_scalar_prefetch=1,
            grid=(count // TB,),
            in_specs=[tokens, tokens, pl.BlockSpec((1, TB), lambda i, p: (0, i))]
            + [whole] * len(sources),
            out_specs=[whole] * 4 + ([pl.BlockSpec(rim, lambda i, p: (0, 0))] if static else []),
            scratch_shapes=[
                pltpu.VMEM((3,) + matrix, F32),
                pltpu.VMEM((3, hidden, width), BF16),
            ]
            + [pltpu.VMEM((hidden, TB), BF16)] * 3
            + [pltpu.VMEM((width, TB), BF16)],
        ),
        out_shape=[jax.ShapeDtypeStruct(matrix, BF16)] * 4
        + ([jax.ShapeDtypeStruct(rim, BF16)] if static else []),
        compiler_params=params(),
        cost_estimate=pl.CostEstimate(
            flops=12 * width * hidden * count,
            bytes_accessed=4 * width * count,
            transcendentals=hidden * count,
        ),
    )(place, xt, vt, rates, *sources)


def update_kernel(place_ref, step_ref, own, r1, r2, r3, *rest):
    olds, out = rest[:-1], rest[-1]
    place = place_ref[0]
    if len(olds) == 3:
        old = jnp.where(
            place == 0, olds[0][...], jnp.where(place == 1, olds[1][...], olds[2][...])
        )
    else:
        old = olds[0][...]
    g = own[...].astype(F32) + r1[...].astype(F32) + r2[...].astype(F32) + r3[...].astype(F32)
    x = g * lax.rsqrt(jnp.sum(g * g) + epsilon)
    rows = g.shape[0]
    diagonal = lax.broadcasted_iota(jnp.int32, (rows, rows), 0) == lax.broadcasted_iota(
        jnp.int32, (rows, rows), 1
    )
    for c in CENTRES:
        xb = x.astype(BF16)
        e = dot(xb, xb, ((1,), (1,)))
        if c:
            e = e - jnp.where(diagonal, c, 0.0)
        eb = e.astype(BF16)
        mix = (coef_second + 2.0 * c * coef_third) * e + coef_third * dot(eb, eb)
        k = coef_first + coef_second * c + coef_third * c * c
        x = k * x + dot(mix.astype(BF16), xb)
    out[...] = (old.astype(F32) + step_ref[0] * x).astype(BF16)


def update(place, step, pieces, olds):
    matrix = pieces[0].shape
    smem = pl.BlockSpec(memory_space=pltpu.SMEM)
    vmem = pl.BlockSpec(memory_space=pltpu.VMEM)
    return pl.pallas_call(
        update_kernel,
        in_specs=[smem, smem] + [vmem] * (4 + len(olds)),
        out_specs=vmem,
        out_shape=jax.ShapeDtypeStruct(matrix, BF16),
        compiler_params=params(),
        cost_estimate=pl.CostEstimate(
            flops=5 * 2 * 5 * matrix[0] * matrix[0] * matrix[0],
            bytes_accessed=16 * matrix[0] * matrix[1],
            transcendentals=0,
        ),
    )(place, step, *pieces, *olds)


def attend_kernel(blocks, kb_first, first_ref, q_ref, k_ref, v_ref, *rest):
    if kb_first is None:
        (out, k_nat) = rest
        rims = ()
    else:
        (rim, _, out, k_nat) = rest
        width = q_ref.shape[0]
        rims = (rim.at[:width], rim.at[width:])
    step = pl.program_id(0)
    heads = q_ref.shape[0] // ATT_DIM
    chunks = WINDOW // QB + 1
    rim_blocks = WINDOW // QB if rims else 0

    @pl.when(step == 0)
    def _():
        if rims:
            for h in range(heads):
                k_nat[h, :WINDOW, :] = rims[0][pl.ds(h * ATT_DIM, ATT_DIM), :].T
        for h in range(heads):
            k_nat[h, rim_blocks * QB :, :] = k_ref[pl.ds(h * ATT_DIM, ATT_DIM), :].T

    later = lax.broadcasted_iota(jnp.int32, (QB, QB), 0) > lax.broadcasted_iota(
        jnp.int32, (QB, QB), 1
    )
    scale = LOG2E / math.sqrt(ATT_DIM)
    low = -1e30

    def values(h, block):
        return v_ref[pl.ds(h * ATT_DIM, ATT_DIM), pl.ds(pl.multiple_of(block * QB, QB), QB)]

    def body(i, fresh):
        for h in range(heads):
            q = q_ref[pl.ds(h * ATT_DIM, ATT_DIM), :]
            s = []
            for c in range(chunks):
                k = k_nat[h, pl.ds(pl.multiple_of((i + c) * QB, QB), QB), :]
                part = dot(k, q)
                if c == 0:
                    part = jnp.where(later, part, low)
                elif c == chunks - 1:
                    part = jnp.where(later, low, part)
                if c < fresh:
                    part = jnp.where(first_ref[0] == 1, low, part)
                s.append(part)
            top = functools.reduce(
                jnp.maximum, [jnp.max(part, axis=0, keepdims=True) for part in s]
            )
            total = jnp.zeros((1, QB), F32)
            result = jnp.zeros((ATT_DIM, QB), F32)
            for c in range(chunks):
                expo = jnp.exp2((s[c] - top) * scale)
                total += jnp.sum(expo, axis=0, keepdims=True)
                if c < fresh:
                    v = rims[1][pl.ds(h * ATT_DIM, ATT_DIM), pl.ds((i + c) * QB, QB)]
                else:
                    v = values(h, i + c - rim_blocks)
                result += dot(v, expo.astype(BF16))
            out[pl.ds(h * ATT_DIM, ATT_DIM), :] = result / total

    if rims:
        for i in range(blocks):

            @pl.when(step == i)
            def _(i=i):
                body(i, rim_blocks - i)
    else:
        body(step, 0)


def attend_main(qt, kt, vt, first):
    width, count = qt.shape
    skip = WINDOW // QB
    blocks = count // QB - skip
    heads = width // ATT_DIM
    whole = pl.BlockSpec((width, count), lambda i, f: (0, 0))
    return pl.pallas_call(
        functools.partial(attend_kernel, blocks, None),
        grid_spec=pltpu.PrefetchScalarGridSpec(
            num_scalar_prefetch=1,
            grid=(blocks,),
            in_specs=[pl.BlockSpec((width, QB), lambda i, f: (0, i + skip)), whole, whole],
            out_specs=pl.BlockSpec((width, QB), lambda i, f: (0, i + skip)),
            scratch_shapes=[pltpu.VMEM((heads, count, ATT_DIM), BF16)],
        ),
        out_shape=jax.ShapeDtypeStruct((width, count), F32),
        compiler_params=params(),
        cost_estimate=pl.CostEstimate(
            flops=4 * blocks * QB * (WINDOW + QB) * width,
            bytes_accessed=10 * width * count,
            transcendentals=blocks * QB * (WINDOW + QB) * heads,
        ),
    )(first, qt, kt, vt)


def attend_rim(qt, kt, vt, rim, main, first):
    width = qt.shape[0]
    blocks = WINDOW // QB
    heads = width // ATT_DIM
    whole = pl.BlockSpec((width, WINDOW), lambda i, f: (0, 0))
    return pl.pallas_call(
        functools.partial(attend_kernel, blocks, 0),
        grid_spec=pltpu.PrefetchScalarGridSpec(
            num_scalar_prefetch=1,
            grid=(blocks,),
            in_specs=[pl.BlockSpec((width, QB), lambda i, f: (0, i))] + [whole] * 2
            + [
                pl.BlockSpec(rim.shape, lambda i, f: (0, 0)),
                pl.BlockSpec(memory_space=pl.ANY),
            ],
            out_specs=pl.BlockSpec((width, QB), lambda i, f: (0, i)),
            scratch_shapes=[pltpu.VMEM((heads, 2 * WINDOW, ATT_DIM), BF16)],
        ),
        out_shape=jax.ShapeDtypeStruct(main.shape, F32),
        input_output_aliases={5: 0},
        compiler_params=params(),
        cost_estimate=pl.CostEstimate(
            flops=4 * blocks * QB * (WINDOW + QB) * width,
            bytes_accessed=16 * width * WINDOW,
            transcendentals=blocks * QB * (WINDOW + QB) * heads,
        ),
    )(first, qt, kt, vt, rim, main)


def pack(rows, out, dests):
    n = rows.shape[0] // (2 * dests)
    width = rows.shape[1]
    for d in range(dests):
        begin = 2 * n * d
        out[d] = jnp.concatenate([rows[begin : begin + n], rows[begin + n : begin + 2 * n]], 1)


def apply_kernel(dests, place_ref, part_ref, q_ref, att_ref, *rest):
    sources, out, (wt, w2) = rest[: 2 * RING], rest[2 * RING], rest[2 * RING + 1 :]

    @pl.when(pl.program_id(0) == 0)
    def _():
        def put(j, w):
            if j < 2:
                wt[j] = (w * 0.5 if j == 0 else w).T
            else:
                w2[...] = w

        for part in range(2):

            @pl.when(part_ref[0] == part)
            def _(part=part):
                pick_weights(place_ref[0], sources[part * RING : (part + 1) * RING], put)

    q = q_ref[...]
    half = dot(wt[0], q)
    up = dot(wt[1], q)
    hidden = (half * (1.0 + jnp.tanh(half)) * up).astype(BF16)
    fast = dot(w2[...], hidden)
    pack((fast + att_ref[...]).astype(BF16).T, out, dests)


def apply_mix(place, part, qt, att, early, late, parts_out):
    width, count = qt.shape
    matrix = early[0].shape
    rows = count // parts_out
    dests = 4
    tokens = pl.BlockSpec((width, dests * rows), lambda i, p, g: (0, i))
    return pl.pallas_call(
        functools.partial(apply_kernel, dests),
        grid_spec=pltpu.PrefetchScalarGridSpec(
            num_scalar_prefetch=2,
            grid=(parts_out // dests,),
            in_specs=[tokens, tokens] + [pl.BlockSpec(matrix, lambda i, p, g: (0, 0))] * 8,
            out_specs=pl.BlockSpec((dests, rows // 2, 2 * width), lambda i, p, g: (i, 0, 0)),
            scratch_shapes=[
                pltpu.VMEM((2, matrix[1], width), BF16),
                pltpu.VMEM(matrix, BF16),
            ],
        ),
        out_shape=jax.ShapeDtypeStruct((parts_out, rows // 2, 2 * width), BF16),
        compiler_params=params(),
        cost_estimate=pl.CostEstimate(
            flops=6 * width * matrix[1] * count,
            bytes_accessed=8 * width * count,
            transcendentals=matrix[1] * count,
        ),
    )(place, part, qt, att, *early, *late)


def gate_kernel(dests, g_ref, out):
    pack(g_ref[...].T, out, dests)


def pack_gate(gt, parts_out):
    width, count = gt.shape
    rows = count // parts_out
    dests = 4
    return pl.pallas_call(
        functools.partial(gate_kernel, dests),
        grid=(parts_out // dests,),
        in_specs=[pl.BlockSpec((width, dests * rows), lambda i: (0, i))],
        out_specs=pl.BlockSpec((dests, rows // 2, 2 * width), lambda i: (i, 0, 0)),
        out_shape=jax.ShapeDtypeStruct((parts_out, rows // 2, 2 * width), BF16),
        compiler_params=params(),
        cost_estimate=pl.CostEstimate(
            flops=0, bytes_accessed=8 * width * count, transcendentals=0
        ),
    )(gt)


def final_kernel(m_ref, g_ref, gain_ref, out):
    heads, rows, double = m_ref.shape
    width = double // 2
    squares = jnp.zeros((rows, double), F32)
    for h in range(heads):
        m = m_ref[h].astype(F32)
        squares += m * m
    left = lax.broadcasted_iota(jnp.int32, (1, double), 1) < width
    mean = 1.0 / (heads * width)
    early = lax.rsqrt(jnp.sum(squares[:, :width], 1, keepdims=True) * mean + epsilon)
    late = lax.rsqrt(jnp.sum(squares[:, width:], 1, keepdims=True) * mean + epsilon)
    factor = jnp.where(left, early, late)
    for h in range(0, heads, 2):
        pair = []
        for j in (h, h + 1):
            g = g_ref[j].astype(F32)
            scale = factor * gain_ref[j : j + 1]
            pair.append((m_ref[j].astype(F32) * scale * (g * sigmoid(g))).astype(BF16))
        cols = slice(h * width, (h + 2) * width)
        out[0, :, cols] = jnp.concatenate([y[:, :width] for y in pair], 1)
        out[1, :, cols] = jnp.concatenate([y[:, width:] for y in pair], 1)


def final(mixed, gates, gain):
    heads, rows, double = mixed.shape
    block = FINAL_ROWS
    wide = heads * double // 2
    gain = gain.reshape(heads, double // 2)
    tokens = pl.BlockSpec((heads, block, double), lambda i: (0, i, 0))
    result = pl.pallas_call(
        final_kernel,
        grid=(rows // block,),
        in_specs=[tokens, tokens, pl.BlockSpec((heads, double), lambda i: (0, 0))],
        out_specs=pl.BlockSpec((2, block, wide), lambda i: (0, i, 0)),
        out_shape=jax.ShapeDtypeStruct((2, rows, wide), BF16),
        compiler_params=params(),
        cost_estimate=pl.CostEstimate(
            flops=20 * rows * wide, bytes_accessed=12 * rows * wide, transcendentals=2 * rows * wide
        ),
    )(mixed, gates, jnp.concatenate([gain, gain], 1))
    return result.reshape(2 * rows, wide)


def reduce_moves(part):
    return [[(part, (m - s) % RING, part, m) for m in range(3)] for s in range(1, RING)]


def spread_moves(parts):
    return [[(p, m, p, (m + s) % RING) for p in parts for m in range(3)] for s in range(1, RING)]


def ring_send(array, moves):
    heads = lax.axis_size("head")

    def index(part, place, head):
        return (part * RING + (place + 2 * (head % 2)) % RING) * heads + head

    pairs = [(index(a, b, h), index(c, d, h)) for a, b, c, d in moves for h in range(heads)]
    return lax.ppermute(array, ("ctx", "head"), pairs)


def send(array, pairs):
    return lax.ppermute(array, "ctx", pairs)


def shards(
    query_rows,
    key_rows,
    value_rows,
    gate_rows,
    token_rates,
    step_sizes,
    fast_first,
    fast_third,
    fast_second,
    norm_gain,
):
    ctx = lax.axis_index("ctx")
    heads = lax.axis_size("head")
    place = ((ctx + 2 * (lax.axis_index("head") % 2)) % RING).reshape(1).astype(jnp.int32)
    part = (ctx // RING).reshape(1).astype(jnp.int32)
    first = (ctx == 0).reshape(1).astype(jnp.int32)
    qt, kt, vt, gt = query_rows.T, key_rows.T, value_rows.T, gate_rows.T
    start = [fast_first[0], fast_third[0], fast_second[0].T]
    hold = lax.optimization_barrier

    own, *out = grads(place, kt, vt, token_rates, start, True)
    out, tail = out[:3], out[3]
    pieces = [own] + [ring_send(o, p) for o, p in zip(out, reduce_moves(0))]
    rim_late = send(tail, [(i, i + 1) for i in range(4, 7)])
    fresh = update(place, step_sizes, pieces, start)
    fresh, gt, rim_late, q_main = hold((fresh, gt, rim_late, qt))
    crossed = ring_send(fresh, [(0, m, 1, m) for m in range(3)])
    gates = pack_gate(gt, heads)
    att_main = attend_main(q_main, kt, vt, first)
    held = jnp.where(part[0] == 0, fresh, crossed)
    held, gates = hold((held, gates))
    gate_tokens = lax.all_to_all(gates, "head", split_axis=0, concat_axis=0)
    early = [held] + [ring_send(held, p) for p in spread_moves((0, 1))]
    early[1], tail = hold((early[1], tail))
    rim_early = send(tail, [(i, i + 1) for i in range(4)])

    own, *out = grads(place, kt, vt, token_rates, early, False)
    pieces = [own] + [ring_send(o, p) for o, p in zip(out, reduce_moves(1))]
    fresh = update(place, step_sizes, pieces, [early[0]])
    fresh, att_main = hold((fresh, att_main))
    late = [fresh] + [ring_send(fresh, p) for p in spread_moves((1,))]
    att = attend_rim(qt, kt, vt, jnp.where(ctx <= RING, rim_early, rim_late), att_main, first)
    mixed = apply_mix(place, part, qt, att, early, late, heads)
    mixed_tokens = lax.all_to_all(mixed, "head", split_axis=0, concat_axis=0)
    return final(mixed_tokens, gate_tokens, norm_gain)


def solution(mesh):
    placed = (
        P("ctx", "head"),
        P("ctx", "head"),
        P("ctx", "head"),
        P("ctx", "head"),
        P("head", "ctx"),
        P("head"),
        P("head", None, None),
        P("head", None, None),
        P("head", None, None),
        P(),
    )
    return jax.shard_map(
        shards, mesh=mesh, in_specs=placed, out_specs=P(("ctx", "head"), None), check_vma=False
    )
```

```python
import functools
import math

import jax
import jax.numpy as jnp
from jax import lax
from jax.experimental import pallas as pl
from jax.experimental.pallas import tpu as pltpu
from jax.sharding import PartitionSpec as P

ATT_DIM = 160
WINDOW = 1024
RING = 4
QB = 256
TB = 1536
SB = 512
FINAL_ROWS = 32

coef_first = 3.4445
coef_second = -4.775
coef_third = 2.0315
epsilon = 1e-06
LOG2E = 1.4426950408889634
CENTRES = (0.0, 0.0, 0.5, 0.8, 0.8)
F32 = jnp.float32
BF16 = jnp.bfloat16
MIB = 1024 * 1024


def params(mib):
    return pltpu.CompilerParams(vmem_limit_bytes=mib * MIB)


def dot(a, b, dims=((1,), (0,))):
    return lax.dot_general(a, b, (dims, ((), ())), preferred_element_type=F32)


def sigmoid(x):
    return 0.5 * jnp.tanh(0.5 * x) + 0.5


def pick_weights(place, sources, put):
    for j in range(3):
        for s in range(RING):

            @pl.when(lax.rem(place + RING - j, RING) == s)
            def _(j=j, s=s):
                put(j, sources[s][...])


def grads_kernel(static, place_ref, x_ref, v_ref, r_ref, *rest):
    n_src = 3 if static else RING
    sources, outs, rest = rest[:n_src], rest[n_src : n_src + 4], rest[n_src + 4 :]
    acc, wt, d_gate, d_up, hidden, scaled = rest[-6:]
    step = pl.program_id(0)
    last = pl.num_programs(0) - 1
    place = place_ref[0]
    width, count = x_ref.shape

    @pl.when(step == 0)
    def _():
        def put(j, w):
            wt[j] = (w * 0.5 if j == 0 else w).T

        if static:
            for j in range(3):
                put(j, sources[j][...])
        else:
            pick_weights(place, sources, put)
        acc[...] = jnp.zeros_like(acc)

    def forward(span):
        x = x_ref[:, span]
        e = (r_ref[:, span] * v_ref[:, span].astype(F32)).astype(BF16)
        scaled[:, span] = e
        half = dot(wt[0], x)
        up = dot(wt[1], x)
        back = dot(wt[2], e)
        both = 1.0 + jnp.tanh(half)
        gated = half * both
        slope = both * (half + half + 1.0 - gated)
        hidden[:, span] = (gated * up).astype(BF16)
        d_up[:, span] = (back * gated).astype(BF16)
        d_gate[:, span] = (back * up * slope).astype(BF16)

    def backward(span):
        nt = ((1,), (1,))
        x = x_ref[:, span]
        acc[0] += dot(x, d_gate[:, span], nt)
        acc[1] += dot(x, d_up[:, span], nt)
        acc[2] += dot(scaled[:, span], hidden[:, span], nt)

    spans = [slice(b, b + SB) for b in range(0, count, SB)]
    for i, span in enumerate(spans):
        forward(span)
        if i:
            backward(spans[i - 1])
    backward(spans[-1])

    @pl.when(step == last)
    def _():
        if static:
            rim = slice(count - WINDOW, count)
            rest[0][:width] = x_ref[:, rim]
            rest[0][width:] = v_ref[:, rim]
        for shift, out in enumerate(outs):
            j = jnp.minimum(lax.rem(place + shift, RING), 2)
            out[...] = (acc[j] * jnp.where(j == 0, 0.5, 1.0)).astype(BF16)


def grads(place, xt, vt, rates, sources, static):
    width, count = xt.shape
    matrix = sources[0].shape
    whole = pl.BlockSpec(matrix, lambda i, p: (0, 0))
    tokens = pl.BlockSpec((width, TB), lambda i, p: (0, i))
    hidden = matrix[1]
    rim = (2 * width, WINDOW)
    return pl.pallas_call(
        functools.partial(grads_kernel, static),
        grid_spec=pltpu.PrefetchScalarGridSpec(
            num_scalar_prefetch=1,
            grid=(count // TB,),
            in_specs=[tokens, tokens, pl.BlockSpec((1, TB), lambda i, p: (0, i))]
            + [whole] * len(sources),
            out_specs=[whole] * 4 + ([pl.BlockSpec(rim, lambda i, p: (0, 0))] if static else []),
            scratch_shapes=[
                pltpu.VMEM((3,) + matrix, F32),
                pltpu.VMEM((3, hidden, width), BF16),
            ]
            + [pltpu.VMEM((hidden, TB), BF16)] * 3
            + [pltpu.VMEM((width, TB), BF16)],
        ),
        out_shape=[jax.ShapeDtypeStruct(matrix, BF16)] * 4
        + ([jax.ShapeDtypeStruct(rim, BF16)] if static else []),
        compiler_params=params(56),
        cost_estimate=pl.CostEstimate(
            flops=12 * width * hidden * count,
            bytes_accessed=4 * width * count,
            transcendentals=hidden * count,
        ),
    )(place, xt, vt, rates, *sources)


def update_kernel(place_ref, step_ref, own, r1, r2, r3, *rest):
    olds, out = rest[:-1], rest[-1]
    place = place_ref[0]
    if len(olds) == 3:
        old = jnp.where(
            place == 0, olds[0][...], jnp.where(place == 1, olds[1][...], olds[2][...])
        )
    else:
        old = olds[0][...]
    g = own[...].astype(F32) + r1[...].astype(F32) + r2[...].astype(F32) + r3[...].astype(F32)
    x = g * lax.rsqrt(jnp.sum(g * g) + epsilon)
    rows = g.shape[0]
    diagonal = lax.broadcasted_iota(jnp.int32, (rows, rows), 0) == lax.broadcasted_iota(
        jnp.int32, (rows, rows), 1
    )
    for c in CENTRES:
        xb = x.astype(BF16)
        e = dot(xb, xb, ((1,), (1,)))
        if c:
            e = e - jnp.where(diagonal, c, 0.0)
        eb = e.astype(BF16)
        mix = (coef_second + 2.0 * c * coef_third) * e + coef_third * dot(eb, eb)
        k = coef_first + coef_second * c + coef_third * c * c
        x = k * x + dot(mix.astype(BF16), xb)
    out[...] = (old.astype(F32) + step_ref[0] * x).astype(BF16)


def update(place, step, pieces, olds, mib):
    matrix = pieces[0].shape
    smem = pl.BlockSpec(memory_space=pltpu.SMEM)
    vmem = pl.BlockSpec(memory_space=pltpu.VMEM)
    return pl.pallas_call(
        update_kernel,
        in_specs=[smem, smem] + [vmem] * (4 + len(olds)),
        out_specs=vmem,
        out_shape=jax.ShapeDtypeStruct(matrix, BF16),
        compiler_params=params(mib),
        cost_estimate=pl.CostEstimate(
            flops=5 * 2 * 5 * matrix[0] * matrix[0] * matrix[0],
            bytes_accessed=16 * matrix[0] * matrix[1],
            transcendentals=0,
        ),
    )(place, step, *pieces, *olds)


def attend_kernel(blocks, kb_first, first_ref, q_ref, k_ref, v_ref, *rest):
    if kb_first is None:
        (out, k_nat) = rest
        rims = ()
    else:
        (rim, _, out, k_nat) = rest
        width = q_ref.shape[0]
        rims = (rim.at[:width], rim.at[width:])
    step = pl.program_id(0)
    heads = q_ref.shape[0] // ATT_DIM
    chunks = WINDOW // QB + 1
    rim_blocks = WINDOW // QB if rims else 0

    @pl.when(step == 0)
    def _():
        if rims:
            for h in range(heads):
                k_nat[h, :WINDOW, :] = rims[0][pl.ds(h * ATT_DIM, ATT_DIM), :].T
        for h in range(heads):
            k_nat[h, rim_blocks * QB :, :] = k_ref[pl.ds(h * ATT_DIM, ATT_DIM), :].T

    later = lax.broadcasted_iota(jnp.int32, (QB, QB), 0) > lax.broadcasted_iota(
        jnp.int32, (QB, QB), 1
    )
    scale = LOG2E / math.sqrt(ATT_DIM)
    low = -1e30

    def values(h, block):
        return v_ref[pl.ds(h * ATT_DIM, ATT_DIM), pl.ds(pl.multiple_of(block * QB, QB), QB)]

    def body(i, fresh):
        for h in range(heads):
            q = q_ref[pl.ds(h * ATT_DIM, ATT_DIM), :]
            s = []
            for c in range(chunks):
                k = k_nat[h, pl.ds(pl.multiple_of((i + c) * QB, QB), QB), :]
                part = dot(k, q)
                if c == 0:
                    part = jnp.where(later, part, low)
                elif c == chunks - 1:
                    part = jnp.where(later, low, part)
                if c < fresh:
                    part = jnp.where(first_ref[0] == 1, low, part)
                s.append(part)
            top = functools.reduce(
                jnp.maximum, [jnp.max(part, axis=0, keepdims=True) for part in s]
            )
            total = jnp.zeros((1, QB), F32)
            result = jnp.zeros((ATT_DIM, QB), F32)
            for c in range(chunks):
                expo = jnp.exp2((s[c] - top) * scale)
                total += jnp.sum(expo, axis=0, keepdims=True)
                if c < fresh:
                    v = rims[1][pl.ds(h * ATT_DIM, ATT_DIM), pl.ds((i + c) * QB, QB)]
                else:
                    v = values(h, i + c - rim_blocks)
                result += dot(v, expo.astype(BF16))
            out[pl.ds(h * ATT_DIM, ATT_DIM), :] = result / total

    if rims:
        for i in range(blocks):

            @pl.when(step == i)
            def _(i=i):
                body(i, rim_blocks - i)
    else:
        body(step, 0)


def attend_main(qt, kt, vt, first):
    width, count = qt.shape
    skip = WINDOW // QB
    blocks = count // QB - skip
    heads = width // ATT_DIM
    whole = pl.BlockSpec((width, count), lambda i, f: (0, 0))
    return pl.pallas_call(
        functools.partial(attend_kernel, blocks, None),
        grid_spec=pltpu.PrefetchScalarGridSpec(
            num_scalar_prefetch=1,
            grid=(blocks,),
            in_specs=[pl.BlockSpec((width, QB), lambda i, f: (0, i + skip)), whole, whole],
            out_specs=pl.BlockSpec((width, QB), lambda i, f: (0, i + skip)),
            scratch_shapes=[pltpu.VMEM((heads, count, ATT_DIM), BF16)],
        ),
        out_shape=jax.ShapeDtypeStruct((width, count), F32),
        compiler_params=params(56),
        cost_estimate=pl.CostEstimate(
            flops=4 * blocks * QB * (WINDOW + QB) * width,
            bytes_accessed=10 * width * count,
            transcendentals=blocks * QB * (WINDOW + QB) * heads,
        ),
    )(first, qt, kt, vt)


def attend_rim(qt, kt, vt, rim, main, first):
    width = qt.shape[0]
    blocks = WINDOW // QB
    heads = width // ATT_DIM
    whole = pl.BlockSpec((width, WINDOW), lambda i, f: (0, 0))
    return pl.pallas_call(
        functools.partial(attend_kernel, blocks, 0),
        grid_spec=pltpu.PrefetchScalarGridSpec(
            num_scalar_prefetch=1,
            grid=(blocks,),
            in_specs=[pl.BlockSpec((width, QB), lambda i, f: (0, i))] + [whole] * 2
            + [
                pl.BlockSpec(rim.shape, lambda i, f: (0, 0)),
                pl.BlockSpec(memory_space=pl.ANY),
            ],
            out_specs=pl.BlockSpec((width, QB), lambda i, f: (0, i)),
            scratch_shapes=[pltpu.VMEM((heads, 2 * WINDOW, ATT_DIM), BF16)],
        ),
        out_shape=jax.ShapeDtypeStruct(main.shape, F32),
        input_output_aliases={5: 0},
        compiler_params=params(56),
        cost_estimate=pl.CostEstimate(
            flops=4 * blocks * QB * (WINDOW + QB) * width,
            bytes_accessed=16 * width * WINDOW,
            transcendentals=blocks * QB * (WINDOW + QB) * heads,
        ),
    )(first, qt, kt, vt, rim, main)


def pack(rows, out, dests):
    n = rows.shape[0] // (2 * dests)
    width = rows.shape[1]
    for d in range(dests):
        begin = 2 * n * d
        out[d] = jnp.concatenate([rows[begin : begin + n], rows[begin + n : begin + 2 * n]], 1)


def apply_kernel(dests, place_ref, part_ref, q_ref, att_ref, *rest):
    sources, out, (wt, w2) = rest[: 2 * RING], rest[2 * RING], rest[2 * RING + 1 :]

    @pl.when(pl.program_id(0) == 0)
    def _():
        def put(j, w):
            if j < 2:
                wt[j] = (w * 0.5 if j == 0 else w).T
            else:
                w2[...] = w

        for part in range(2):

            @pl.when(part_ref[0] == part)
            def _(part=part):
                pick_weights(place_ref[0], sources[part * RING : (part + 1) * RING], put)

    q = q_ref[...]
    half = dot(wt[0], q)
    up = dot(wt[1], q)
    hidden = (half * (1.0 + jnp.tanh(half)) * up).astype(BF16)
    fast = dot(w2[...], hidden)
    pack((fast + att_ref[...]).astype(BF16).T, out, dests)


def apply_mix(place, part, qt, att, early, late, parts_out):
    width, count = qt.shape
    matrix = early[0].shape
    rows = count // parts_out
    dests = 4
    tokens = pl.BlockSpec((width, dests * rows), lambda i, p, g: (0, i))
    return pl.pallas_call(
        functools.partial(apply_kernel, dests),
        grid_spec=pltpu.PrefetchScalarGridSpec(
            num_scalar_prefetch=2,
            grid=(parts_out // dests,),
            in_specs=[tokens, tokens] + [pl.BlockSpec(matrix, lambda i, p, g: (0, 0))] * 8,
            out_specs=pl.BlockSpec((dests, rows // 2, 2 * width), lambda i, p, g: (i, 0, 0)),
            scratch_shapes=[
                pltpu.VMEM((2, matrix[1], width), BF16),
                pltpu.VMEM(matrix, BF16),
            ],
        ),
        out_shape=jax.ShapeDtypeStruct((parts_out, rows // 2, 2 * width), BF16),
        compiler_params=params(56),
        cost_estimate=pl.CostEstimate(
            flops=6 * width * matrix[1] * count,
            bytes_accessed=8 * width * count,
            transcendentals=matrix[1] * count,
        ),
    )(place, part, qt, att, *early, *late)


def gate_kernel(dests, g_ref, out):
    pack(g_ref[...].T, out, dests)


def pack_gate(gt, parts_out):
    width, count = gt.shape
    rows = count // parts_out
    dests = 4
    return pl.pallas_call(
        functools.partial(gate_kernel, dests),
        grid=(parts_out // dests,),
        in_specs=[pl.BlockSpec((width, dests * rows), lambda i: (0, i))],
        out_specs=pl.BlockSpec((dests, rows // 2, 2 * width), lambda i: (i, 0, 0)),
        out_shape=jax.ShapeDtypeStruct((parts_out, rows // 2, 2 * width), BF16),
        compiler_params=params(56),
        cost_estimate=pl.CostEstimate(
            flops=0, bytes_accessed=8 * width * count, transcendentals=0
        ),
    )(gt)


def final_kernel(m_ref, g_ref, gain_ref, out):
    heads, rows, double = m_ref.shape
    width = double // 2
    squares = jnp.zeros((rows, double), F32)
    for h in range(heads):
        m = m_ref[h].astype(F32)
        squares += m * m
    left = lax.broadcasted_iota(jnp.int32, (1, double), 1) < width
    mean = 1.0 / (heads * width)
    early = lax.rsqrt(jnp.sum(squares[:, :width], 1, keepdims=True) * mean + epsilon)
    late = lax.rsqrt(jnp.sum(squares[:, width:], 1, keepdims=True) * mean + epsilon)
    factor = jnp.where(left, early, late)
    for h in range(0, heads, 2):
        pair = []
        for j in (h, h + 1):
            g = g_ref[j].astype(F32)
            scale = factor * gain_ref[j : j + 1]
            pair.append((m_ref[j].astype(F32) * scale * (g * sigmoid(g))).astype(BF16))
        cols = slice(h * width, (h + 2) * width)
        out[0, :, cols] = jnp.concatenate([y[:, :width] for y in pair], 1)
        out[1, :, cols] = jnp.concatenate([y[:, width:] for y in pair], 1)


def final(mixed, gates, gain):
    heads, rows, double = mixed.shape
    block = FINAL_ROWS
    wide = heads * double // 2
    gain = gain.reshape(heads, double // 2)
    tokens = pl.BlockSpec((heads, block, double), lambda i: (0, i, 0))
    result = pl.pallas_call(
        final_kernel,
        grid=(rows // block,),
        in_specs=[tokens, tokens, pl.BlockSpec((heads, double), lambda i: (0, 0))],
        out_specs=pl.BlockSpec((2, block, wide), lambda i: (0, i, 0)),
        out_shape=jax.ShapeDtypeStruct((2, rows, wide), BF16),
        compiler_params=params(16),
        cost_estimate=pl.CostEstimate(
            flops=20 * rows * wide, bytes_accessed=12 * rows * wide, transcendentals=2 * rows * wide
        ),
    )(mixed, gates, jnp.concatenate([gain, gain], 1))
    return result.reshape(2 * rows, wide)


def reduce_moves(part):
    return [[(part, (m - s) % RING, part, m) for m in range(3)] for s in range(1, RING)]


def spread_moves(parts):
    return [[(p, m, p, (m + s) % RING) for p in parts for m in range(3)] for s in range(1, RING)]


def ring_send(array, moves):
    heads = lax.axis_size("head")

    def index(part, place, head):
        return (part * RING + (place + 2 * (head % 2)) % RING) * heads + head

    pairs = [(index(a, b, h), index(c, d, h)) for a, b, c, d in moves for h in range(heads)]
    return lax.ppermute(array, ("ctx", "head"), pairs)


def send(array, pairs):
    return lax.ppermute(array, "ctx", pairs)


def shards(
    query_rows,
    key_rows,
    value_rows,
    gate_rows,
    token_rates,
    step_sizes,
    fast_first,
    fast_third,
    fast_second,
    norm_gain,
):
    ctx = lax.axis_index("ctx")
    heads = lax.axis_size("head")
    place = ((ctx + 2 * (lax.axis_index("head") % 2)) % RING).reshape(1).astype(jnp.int32)
    part = (ctx // RING).reshape(1).astype(jnp.int32)
    first = (ctx == 0).reshape(1).astype(jnp.int32)
    qt, kt, vt, gt = query_rows.T, key_rows.T, value_rows.T, gate_rows.T
    start = [fast_first[0], fast_third[0], fast_second[0].T]
    hold = lax.optimization_barrier

    own, *out = grads(place, kt, vt, token_rates, start, True)
    out, tail = out[:3], out[3]
    pieces = [own] + [ring_send(o, p) for o, p in zip(out, reduce_moves(0))]
    rim_late = send(tail, [(i, i + 1) for i in range(4, 7)])
    att_main = attend_main(qt, kt, vt, first)
    pieces, att_main = hold((pieces, att_main))
    fresh = update(place, step_sizes, pieces, start, 12)
    fresh, gt, rim_late = hold((fresh, gt, rim_late))
    crossed = ring_send(fresh, [(0, m, 1, m) for m in range(3)])
    gates = pack_gate(gt, heads)
    held = jnp.where(part[0] == 0, fresh, crossed)
    held, gates = hold((held, gates))
    gate_tokens = lax.all_to_all(gates, "head", split_axis=0, concat_axis=0)
    early = [held] + [ring_send(held, p) for p in spread_moves((0, 1))]
    early[1], tail = hold((early[1], tail))
    rim_early = send(tail, [(i, i + 1) for i in range(4)])

    own, *out = grads(place, kt, vt, token_rates, early, False)
    pieces = [own] + [ring_send(o, p) for o, p in zip(out, reduce_moves(1))]
    fresh = update(place, step_sizes, pieces, [early[0]], 56)
    fresh, att_main = hold((fresh, att_main))
    late = [fresh] + [ring_send(fresh, p) for p in spread_moves((1,))]
    att = attend_rim(qt, kt, vt, jnp.where(ctx <= RING, rim_early, rim_late), att_main, first)
    att, gate_tokens = hold((att, gate_tokens))
    mixed = apply_mix(place, part, qt, att, early, late, heads)
    mixed_tokens = lax.all_to_all(mixed, "head", split_axis=0, concat_axis=0)
    return final(mixed_tokens, gate_tokens, norm_gain)


def solution(mesh):
    placed = (
        P("ctx", "head"),
        P("ctx", "head"),
        P("ctx", "head"),
        P("ctx", "head"),
        P("head", "ctx"),
        P("head"),
        P("head", None, None),
        P("head", None, None),
        P("head", None, None),
        P(),
    )
    return jax.shard_map(
        shards, mesh=mesh, in_specs=placed, out_specs=P(("ctx", "head"), None), check_vma=False
    )
```

```python
import functools
import math

import jax
import jax.numpy as jnp
from jax import lax
from jax.experimental import pallas as pl
from jax.experimental.pallas import tpu as pltpu
from jax.sharding import PartitionSpec as P

ATT_DIM = 160
WINDOW = 1024
RING = 4
QB = 256
TB = 1536
SB = 512
LED = WINDOW // QB + 1
FINAL_ROWS = 32

coef_first = 3.4445
coef_second = -4.775
coef_third = 2.0315
epsilon = 1e-06
LOG2E = 1.4426950408889634
CENTRES = (0.0, 0.0, 0.5, 0.8, 0.8)
F32 = jnp.float32
BF16 = jnp.bfloat16
MIB = 1024 * 1024


def params(mib):
    return pltpu.CompilerParams(vmem_limit_bytes=mib * MIB)


def dot(a, b, dims=((1,), (0,))):
    return lax.dot_general(a, b, (dims, ((), ())), preferred_element_type=F32)


def sigmoid(x):
    return 0.5 * jnp.tanh(0.5 * x) + 0.5


def pick_weights(place, sources, put):
    for j in range(3):
        for s in range(RING):

            @pl.when(lax.rem(place + RING - j, RING) == s)
            def _(j=j, s=s):
                put(j, sources[s][...])


def grads_kernel(static, place_ref, x_ref, v_ref, r_ref, *rest):
    n_src = 3 if static else RING
    sources, outs, rest = rest[:n_src], rest[n_src : n_src + 4], rest[n_src + 4 :]
    acc, wt, d_gate, d_up, hidden, scaled = rest[-6:]
    step = pl.program_id(0)
    last = pl.num_programs(0) - 1
    place = place_ref[0]
    width, count = x_ref.shape

    @pl.when(step == 0)
    def _():
        def put(j, w):
            wt[j] = (w * 0.5 if j == 0 else w).T

        if static:
            for j in range(3):
                put(j, sources[j][...])
        else:
            pick_weights(place, sources, put)
        acc[...] = jnp.zeros_like(acc)

    def forward(span):
        x = x_ref[:, span]
        e = (r_ref[:, span] * v_ref[:, span].astype(F32)).astype(BF16)
        scaled[:, span] = e
        half = dot(wt[0], x)
        up = dot(wt[1], x)
        back = dot(wt[2], e)
        both = 1.0 + jnp.tanh(half)
        gated = half * both
        slope = both * (half + half + 1.0 - gated)
        hidden[:, span] = (gated * up).astype(BF16)
        d_up[:, span] = (back * gated).astype(BF16)
        d_gate[:, span] = (back * up * slope).astype(BF16)

    def backward(span):
        nt = ((1,), (1,))
        x = x_ref[:, span]
        acc[0] += dot(x, d_gate[:, span], nt)
        acc[1] += dot(x, d_up[:, span], nt)
        acc[2] += dot(scaled[:, span], hidden[:, span], nt)

    spans = [slice(b, b + SB) for b in range(0, count, SB)]
    for i, span in enumerate(spans):
        forward(span)
        if i:
            backward(spans[i - 1])
    backward(spans[-1])

    @pl.when(step == last)
    def _():
        if static:
            rim = slice(count - WINDOW, count)
            rest[0][:width] = x_ref[:, rim]
            rest[0][width:] = v_ref[:, rim]
        for shift, out in enumerate(outs):
            j = jnp.minimum(lax.rem(place + shift, RING), 2)
            out[...] = (acc[j] * jnp.where(j == 0, 0.5, 1.0)).astype(BF16)


def grads(place, xt, vt, rates, sources, static):
    width, count = xt.shape
    matrix = sources[0].shape
    whole = pl.BlockSpec(matrix, lambda i, p: (0, 0))
    tokens = pl.BlockSpec((width, TB), lambda i, p: (0, i))
    hidden = matrix[1]
    rim = (2 * width, WINDOW)
    return pl.pallas_call(
        functools.partial(grads_kernel, static),
        grid_spec=pltpu.PrefetchScalarGridSpec(
            num_scalar_prefetch=1,
            grid=(count // TB,),
            in_specs=[tokens, tokens, pl.BlockSpec((1, TB), lambda i, p: (0, i))]
            + [whole] * len(sources),
            out_specs=[whole] * 4 + ([pl.BlockSpec(rim, lambda i, p: (0, 0))] if static else []),
            scratch_shapes=[
                pltpu.VMEM((3,) + matrix, F32),
                pltpu.VMEM((3, hidden, width), BF16),
            ]
            + [pltpu.VMEM((hidden, TB), BF16)] * 3
            + [pltpu.VMEM((width, TB), BF16)],
        ),
        out_shape=[jax.ShapeDtypeStruct(matrix, BF16)] * 4
        + ([jax.ShapeDtypeStruct(rim, BF16)] if static else []),
        compiler_params=params(56),
        cost_estimate=pl.CostEstimate(
            flops=12 * width * hidden * count,
            bytes_accessed=4 * width * count,
            transcendentals=hidden * count,
        ),
    )(place, xt, vt, rates, *sources)


def update_kernel(place_ref, step_ref, own, r1, r2, r3, *rest):
    olds, out = rest[:-1], rest[-1]
    place = place_ref[0]
    if len(olds) == 3:
        old = jnp.where(
            place == 0, olds[0][...], jnp.where(place == 1, olds[1][...], olds[2][...])
        )
    else:
        old = olds[0][...]
    g = own[...].astype(F32) + r1[...].astype(F32) + r2[...].astype(F32) + r3[...].astype(F32)
    x = g * lax.rsqrt(jnp.sum(g * g) + epsilon)
    rows = g.shape[0]
    diagonal = lax.broadcasted_iota(jnp.int32, (rows, rows), 0) == lax.broadcasted_iota(
        jnp.int32, (rows, rows), 1
    )
    for c in CENTRES:
        xb = x.astype(BF16)
        e = dot(xb, xb, ((1,), (1,)))
        if c:
            e = e - jnp.where(diagonal, c, 0.0)
        eb = e.astype(BF16)
        mix = (coef_second + 2.0 * c * coef_third) * e + coef_third * dot(eb, eb)
        k = coef_first + coef_second * c + coef_third * c * c
        x = k * x + dot(mix.astype(BF16), xb)
    out[...] = (old.astype(F32) + step_ref[0] * x).astype(BF16)


def update(place, step, pieces, olds, mib):
    matrix = pieces[0].shape
    smem = pl.BlockSpec(memory_space=pltpu.SMEM)
    vmem = pl.BlockSpec(memory_space=pltpu.VMEM)
    return pl.pallas_call(
        update_kernel,
        in_specs=[smem, smem] + [vmem] * (4 + len(olds)),
        out_specs=vmem,
        out_shape=jax.ShapeDtypeStruct(matrix, BF16),
        compiler_params=params(mib),
        cost_estimate=pl.CostEstimate(
            flops=5 * 2 * 5 * matrix[0] * matrix[0] * matrix[0],
            bytes_accessed=16 * matrix[0] * matrix[1],
            transcendentals=0,
        ),
    )(place, step, *pieces, *olds)


def attend_kernel(blocks, kb_first, first_ref, q_ref, k_ref, v_ref, *rest):
    if kb_first is None:
        (out, k_nat) = rest
        rims = ()
    else:
        (rim, _, out, k_nat) = rest
        width = q_ref.shape[0]
        rims = (rim.at[:width], rim.at[width:])
    step = pl.program_id(0)
    heads = q_ref.shape[0] // ATT_DIM
    chunks = WINDOW // QB + 1
    rim_blocks = WINDOW // QB if rims else 0

    @pl.when(step == 0)
    def _():
        if rims:
            for h in range(heads):
                k_nat[h, :WINDOW, :] = rims[0][pl.ds(h * ATT_DIM, ATT_DIM), :].T
        for h in range(heads):
            k_nat[h, rim_blocks * QB :, :] = k_ref[pl.ds(h * ATT_DIM, ATT_DIM), :].T

    later = lax.broadcasted_iota(jnp.int32, (QB, QB), 0) > lax.broadcasted_iota(
        jnp.int32, (QB, QB), 1
    )
    scale = LOG2E / math.sqrt(ATT_DIM)
    low = -1e30

    def values(h, block):
        return v_ref[pl.ds(h * ATT_DIM, ATT_DIM), pl.ds(pl.multiple_of(block * QB, QB), QB)]

    def body(i, fresh):
        for h in range(heads):
            q = q_ref[pl.ds(h * ATT_DIM, ATT_DIM), :]
            s = []
            for c in range(chunks):
                k = k_nat[h, pl.ds(pl.multiple_of((i + c) * QB, QB), QB), :]
                part = dot(k, q)
                if c == 0:
                    part = jnp.where(later, part, low)
                elif c == chunks - 1:
                    part = jnp.where(later, low, part)
                if c < fresh:
                    part = jnp.where(first_ref[0] == 1, low, part)
                s.append(part)
            top = functools.reduce(
                jnp.maximum, [jnp.max(part, axis=0, keepdims=True) for part in s]
            )
            total = jnp.zeros((1, QB), F32)
            result = jnp.zeros((ATT_DIM, QB), F32)
            for c in range(chunks):
                expo = jnp.exp2((s[c] - top) * scale)
                total += jnp.sum(expo, axis=0, keepdims=True)
                if c < fresh:
                    v = rims[1][pl.ds(h * ATT_DIM, ATT_DIM), pl.ds((i + c) * QB, QB)]
                else:
                    v = values(h, i + c - rim_blocks)
                result += dot(v, expo.astype(BF16))
            out[pl.ds(h * ATT_DIM, ATT_DIM), :] = result / total

    if rims:
        for i in range(blocks):

            @pl.when(step == i)
            def _(i=i):
                body(i, max(rim_blocks - i, 0))
    else:
        body(step + LED - (chunks - 1), 0)


def attend_main(qt, kt, vt, first):
    width, count = qt.shape
    skip = LED
    blocks = count // QB - skip
    heads = width // ATT_DIM
    whole = pl.BlockSpec((width, count), lambda i, f: (0, 0))
    return pl.pallas_call(
        functools.partial(attend_kernel, blocks, None),
        grid_spec=pltpu.PrefetchScalarGridSpec(
            num_scalar_prefetch=1,
            grid=(blocks,),
            in_specs=[pl.BlockSpec((width, QB), lambda i, f: (0, i + skip)), whole, whole],
            out_specs=pl.BlockSpec((width, QB), lambda i, f: (0, i + skip)),
            scratch_shapes=[pltpu.VMEM((heads, count, ATT_DIM), BF16)],
        ),
        out_shape=jax.ShapeDtypeStruct((width, count), F32),
        compiler_params=params(56),
        cost_estimate=pl.CostEstimate(
            flops=4 * blocks * QB * (WINDOW + QB) * width,
            bytes_accessed=10 * width * count,
            transcendentals=blocks * QB * (WINDOW + QB) * heads,
        ),
    )(first, qt, kt, vt)


def attend_rim(qt, kt, vt, rim, main, first):
    width = qt.shape[0]
    blocks = LED
    heads = width // ATT_DIM
    whole = pl.BlockSpec((width, LED * QB), lambda i, f: (0, 0))
    return pl.pallas_call(
        functools.partial(attend_kernel, blocks, 0),
        grid_spec=pltpu.PrefetchScalarGridSpec(
            num_scalar_prefetch=1,
            grid=(blocks,),
            in_specs=[pl.BlockSpec((width, QB), lambda i, f: (0, i))] + [whole] * 2
            + [
                pl.BlockSpec(rim.shape, lambda i, f: (0, 0)),
                pl.BlockSpec(memory_space=pl.ANY),
            ],
            out_specs=pl.BlockSpec((width, QB), lambda i, f: (0, i)),
            scratch_shapes=[pltpu.VMEM((heads, WINDOW + LED * QB, ATT_DIM), BF16)],
        ),
        out_shape=jax.ShapeDtypeStruct(main.shape, F32),
        input_output_aliases={5: 0},
        compiler_params=params(56),
        cost_estimate=pl.CostEstimate(
            flops=4 * blocks * QB * (WINDOW + QB) * width,
            bytes_accessed=16 * width * WINDOW,
            transcendentals=blocks * QB * (WINDOW + QB) * heads,
        ),
    )(first, qt, kt, vt, rim, main)


def pack(rows, out, dests):
    n = rows.shape[0] // (2 * dests)
    width = rows.shape[1]
    for d in range(dests):
        begin = 2 * n * d
        out[d] = jnp.concatenate([rows[begin : begin + n], rows[begin + n : begin + 2 * n]], 1)


def apply_kernel(dests, place_ref, part_ref, q_ref, att_ref, *rest):
    sources, out, (wt, w2) = rest[: 2 * RING], rest[2 * RING], rest[2 * RING + 1 :]

    @pl.when(pl.program_id(0) == 0)
    def _():
        def put(j, w):
            if j < 2:
                wt[j] = (w * 0.5 if j == 0 else w).T
            else:
                w2[...] = w

        for part in range(2):

            @pl.when(part_ref[0] == part)
            def _(part=part):
                pick_weights(place_ref[0], sources[part * RING : (part + 1) * RING], put)

    q = q_ref[...]
    half = dot(wt[0], q)
    up = dot(wt[1], q)
    hidden = (half * (1.0 + jnp.tanh(half)) * up).astype(BF16)
    fast = dot(w2[...], hidden)
    pack((fast + att_ref[...]).astype(BF16).T, out, dests)


def apply_mix(place, part, qt, att, early, late, parts_out):
    width, count = qt.shape
    matrix = early[0].shape
    rows = count // parts_out
    dests = 4
    tokens = pl.BlockSpec((width, dests * rows), lambda i, p, g: (0, i))
    return pl.pallas_call(
        functools.partial(apply_kernel, dests),
        grid_spec=pltpu.PrefetchScalarGridSpec(
            num_scalar_prefetch=2,
            grid=(parts_out // dests,),
            in_specs=[tokens, tokens] + [pl.BlockSpec(matrix, lambda i, p, g: (0, 0))] * 8,
            out_specs=pl.BlockSpec((dests, rows // 2, 2 * width), lambda i, p, g: (i, 0, 0)),
            scratch_shapes=[
                pltpu.VMEM((2, matrix[1], width), BF16),
                pltpu.VMEM(matrix, BF16),
            ],
        ),
        out_shape=jax.ShapeDtypeStruct((parts_out, rows // 2, 2 * width), BF16),
        compiler_params=params(56),
        cost_estimate=pl.CostEstimate(
            flops=6 * width * matrix[1] * count,
            bytes_accessed=8 * width * count,
            transcendentals=matrix[1] * count,
        ),
    )(place, part, qt, att, *early, *late)


def gate_kernel(dests, g_ref, out):
    pack(g_ref[...].T, out, dests)


def pack_gate(gt, parts_out):
    width, count = gt.shape
    rows = count // parts_out
    dests = 4
    return pl.pallas_call(
        functools.partial(gate_kernel, dests),
        grid=(parts_out // dests,),
        in_specs=[pl.BlockSpec((width, dests * rows), lambda i: (0, i))],
        out_specs=pl.BlockSpec((dests, rows // 2, 2 * width), lambda i: (i, 0, 0)),
        out_shape=jax.ShapeDtypeStruct((parts_out, rows // 2, 2 * width), BF16),
        compiler_params=params(56),
        cost_estimate=pl.CostEstimate(
            flops=0, bytes_accessed=8 * width * count, transcendentals=0
        ),
    )(gt)


def final_kernel(m_ref, g_ref, gain_ref, out):
    heads, rows, double = m_ref.shape
    width = double // 2
    squares = jnp.zeros((rows, double), F32)
    for h in range(heads):
        m = m_ref[h].astype(F32)
        squares += m * m
    left = lax.broadcasted_iota(jnp.int32, (1, double), 1) < width
    mean = 1.0 / (heads * width)
    early = lax.rsqrt(jnp.sum(squares[:, :width], 1, keepdims=True) * mean + epsilon)
    late = lax.rsqrt(jnp.sum(squares[:, width:], 1, keepdims=True) * mean + epsilon)
    factor = jnp.where(left, early, late)
    for h in range(0, heads, 2):
        pair = []
        for j in (h, h + 1):
            g = g_ref[j].astype(F32)
            scale = factor * gain_ref[j : j + 1]
            pair.append((m_ref[j].astype(F32) * scale * (g * sigmoid(g))).astype(BF16))
        cols = slice(h * width, (h + 2) * width)
        out[0, :, cols] = jnp.concatenate([y[:, :width] for y in pair], 1)
        out[1, :, cols] = jnp.concatenate([y[:, width:] for y in pair], 1)


def final(mixed, gates, gain):
    heads, rows, double = mixed.shape
    block = FINAL_ROWS
    wide = heads * double // 2
    gain = gain.reshape(heads, double // 2)
    tokens = pl.BlockSpec((heads, block, double), lambda i: (0, i, 0))
    result = pl.pallas_call(
        final_kernel,
        grid=(rows // block,),
        in_specs=[tokens, tokens, pl.BlockSpec((heads, double), lambda i: (0, 0))],
        out_specs=pl.BlockSpec((2, block, wide), lambda i: (0, i, 0)),
        out_shape=jax.ShapeDtypeStruct((2, rows, wide), BF16),
        compiler_params=params(16),
        cost_estimate=pl.CostEstimate(
            flops=20 * rows * wide, bytes_accessed=12 * rows * wide, transcendentals=2 * rows * wide
        ),
    )(mixed, gates, jnp.concatenate([gain, gain], 1))
    return result.reshape(2 * rows, wide)


def reduce_moves(part):
    return [[(part, (m - s) % RING, part, m) for m in range(3)] for s in range(1, RING)]


def spread_moves(parts):
    return [[(p, m, p, (m + s) % RING) for p in parts for m in range(3)] for s in range(1, RING)]


def ring_send(array, moves):
    heads = lax.axis_size("head")

    def index(part, place, head):
        return (part * RING + (place + 2 * (head % 2)) % RING) * heads + head

    pairs = [(index(a, b, h), index(c, d, h)) for a, b, c, d in moves for h in range(heads)]
    return lax.ppermute(array, ("ctx", "head"), pairs)


def send(array, pairs):
    return lax.ppermute(array, "ctx", pairs)


def shards(
    query_rows,
    key_rows,
    value_rows,
    gate_rows,
    token_rates,
    step_sizes,
    fast_first,
    fast_third,
    fast_second,
    norm_gain,
):
    ctx = lax.axis_index("ctx")
    heads = lax.axis_size("head")
    place = ((ctx + 2 * (lax.axis_index("head") % 2)) % RING).reshape(1).astype(jnp.int32)
    part = (ctx // RING).reshape(1).astype(jnp.int32)
    first = (ctx == 0).reshape(1).astype(jnp.int32)
    qt, kt, vt, gt = query_rows.T, key_rows.T, value_rows.T, gate_rows.T
    start = [fast_first[0], fast_third[0], fast_second[0].T]
    hold = lax.optimization_barrier

    own, *out = grads(place, kt, vt, token_rates, start, True)
    out, tail = out[:3], out[3]
    pieces = [own] + [ring_send(o, p) for o, p in zip(out, reduce_moves(0))]
    rim_late = send(tail, [(i, i + 1) for i in range(4, 7)])
    att_main = attend_main(qt, kt, vt, first)
    pieces, att_main = hold((pieces, att_main))
    fresh = update(place, step_sizes, pieces, start, 12)
    fresh, gt = hold((fresh, gt))
    crossed = ring_send(fresh, [(0, m, 1, m) for m in range(3)])
    gates = pack_gate(gt, heads)
    held = jnp.where(part[0] == 0, fresh, crossed)
    held, gates, rim_late = hold((held, gates, rim_late))
    gate_tokens = lax.all_to_all(gates, "head", split_axis=0, concat_axis=0)
    early = [held] + [ring_send(held, p) for p in spread_moves((0, 1))]
    early[1], tail = hold((early[1], tail))
    rim_early = send(tail, [(i, i + 1) for i in range(4)])

    own, *out = grads(place, kt, vt, token_rates, early, False)
    pieces = [own] + [ring_send(o, p) for o, p in zip(out, reduce_moves(1))]
    fresh = update(place, step_sizes, pieces, [early[0]], 56)
    fresh, att_main = hold((fresh, att_main))
    late = [fresh] + [ring_send(fresh, p) for p in spread_moves((1,))]
    att = attend_rim(qt, kt, vt, jnp.where(ctx <= RING, rim_early, rim_late), att_main, first)
    att, gate_tokens = hold((att, gate_tokens))
    mixed = apply_mix(place, part, qt, att, early, late, heads)
    mixed_tokens = lax.all_to_all(mixed, "head", split_axis=0, concat_axis=0)
    return final(mixed_tokens, gate_tokens, norm_gain)


def solution(mesh):
    placed = (
        P("ctx", "head"),
        P("ctx", "head"),
        P("ctx", "head"),
        P("ctx", "head"),
        P("head", "ctx"),
        P("head"),
        P("head", None, None),
        P("head", None, None),
        P("head", None, None),
        P(),
    )
    return jax.shard_map(
        shards, mesh=mesh, in_specs=placed, out_specs=P(("ctx", "head"), None), check_vma=False
    )
```

```python
import functools
import math

import jax
import jax.numpy as jnp
from jax import lax
from jax.experimental import pallas as pl
from jax.experimental.pallas import tpu as pltpu
from jax.sharding import PartitionSpec as P

ATT_DIM = 160
WINDOW = 1024
RING = 4
QB = 256
TB = 1536
SB = 512
LED = WINDOW // QB + 1
FINAL_ROWS = 32

coef_first = 3.4445
coef_second = -4.775
coef_third = 2.0315
epsilon = 1e-06
LOG2E = 1.4426950408889634
CENTRES = (0.0, 0.0, 0.5, 0.8, 0.8)
F32 = jnp.float32
BF16 = jnp.bfloat16
MIB = 1024 * 1024


def params(mib):
    return pltpu.CompilerParams(vmem_limit_bytes=mib * MIB)


def dot(a, b, dims=((1,), (0,))):
    return lax.dot_general(a, b, (dims, ((), ())), preferred_element_type=F32)


def sigmoid(x):
    return 0.5 * jnp.tanh(0.5 * x) + 0.5


def pick_weights(place, sources, put):
    for j in range(3):
        for s in range(RING):

            @pl.when(lax.rem(place + RING - j, RING) == s)
            def _(j=j, s=s):
                put(j, sources[s][...])


def grads_kernel(static, place_ref, x_ref, v_ref, r_ref, *rest):
    n_src = 3 if static else RING
    sources, outs, rest = rest[:n_src], rest[n_src : n_src + 4], rest[n_src + 4 :]
    acc, wt, d_gate, d_up, hidden, scaled = rest[-6:]
    step = pl.program_id(0)
    last = pl.num_programs(0) - 1
    place = place_ref[0]
    width, count = x_ref.shape

    @pl.when(step == 0)
    def _():
        def put(j, w):
            wt[j] = (w * 0.5 if j == 0 else w).T

        if static:
            for j in range(3):
                put(j, sources[j][...])
        else:
            pick_weights(place, sources, put)
        acc[...] = jnp.zeros_like(acc)

    def forward(span):
        x = x_ref[:, span]
        e = (r_ref[:, span] * v_ref[:, span].astype(F32)).astype(BF16)
        scaled[:, span] = e
        half = dot(wt[0], x)
        up = dot(wt[1], x)
        back = dot(wt[2], e)
        both = 1.0 + jnp.tanh(half)
        gated = half * both
        slope = both * (half + half + 1.0 - gated)
        hidden[:, span] = (gated * up).astype(BF16)
        d_up[:, span] = (back * gated).astype(BF16)
        d_gate[:, span] = (back * up * slope).astype(BF16)

    def backward(span):
        nt = ((1,), (1,))
        x = x_ref[:, span]
        acc[0] += dot(x, d_gate[:, span], nt)
        acc[1] += dot(x, d_up[:, span], nt)
        acc[2] += dot(scaled[:, span], hidden[:, span], nt)

    spans = [slice(b, b + SB) for b in range(0, count, SB)]
    for i, span in enumerate(spans):
        forward(span)
        if i:
            backward(spans[i - 1])
    backward(spans[-1])

    @pl.when(step == last)
    def _():
        if static:
            rim = slice(count - WINDOW, count)
            rest[0][:width] = x_ref[:, rim]
            rest[0][width:] = v_ref[:, rim]
        for shift, out in enumerate(outs):
            j = jnp.minimum(lax.rem(place + shift, RING), 2)
            out[...] = (acc[j] * jnp.where(j == 0, 0.5, 1.0)).astype(BF16)


def grads(place, xt, vt, rates, sources, static):
    width, count = xt.shape
    matrix = sources[0].shape
    whole = pl.BlockSpec(matrix, lambda i, p: (0, 0))
    tokens = pl.BlockSpec((width, TB), lambda i, p: (0, i))
    hidden = matrix[1]
    rim = (2 * width, WINDOW)
    return pl.pallas_call(
        functools.partial(grads_kernel, static),
        grid_spec=pltpu.PrefetchScalarGridSpec(
            num_scalar_prefetch=1,
            grid=(count // TB,),
            in_specs=[tokens, tokens, pl.BlockSpec((1, TB), lambda i, p: (0, i))]
            + [whole] * len(sources),
            out_specs=[whole] * 4 + ([pl.BlockSpec(rim, lambda i, p: (0, 0))] if static else []),
            scratch_shapes=[
                pltpu.VMEM((3,) + matrix, F32),
                pltpu.VMEM((3, hidden, width), BF16),
            ]
            + [pltpu.VMEM((hidden, TB), BF16)] * 3
            + [pltpu.VMEM((width, TB), BF16)],
        ),
        out_shape=[jax.ShapeDtypeStruct(matrix, BF16)] * 4
        + ([jax.ShapeDtypeStruct(rim, BF16)] if static else []),
        compiler_params=params(56),
        cost_estimate=pl.CostEstimate(
            flops=12 * width * hidden * count,
            bytes_accessed=4 * width * count,
            transcendentals=hidden * count,
        ),
    )(place, xt, vt, rates, *sources)


def update_kernel(place_ref, step_ref, own, r1, r2, r3, *rest):
    olds, out = rest[:-1], rest[-1]
    place = place_ref[0]
    if len(olds) == 3:
        old = jnp.where(
            place == 0, olds[0][...], jnp.where(place == 1, olds[1][...], olds[2][...])
        )
    else:
        old = olds[0][...]
    g = own[...].astype(F32) + r1[...].astype(F32) + r2[...].astype(F32) + r3[...].astype(F32)
    x = g * lax.rsqrt(jnp.sum(g * g) + epsilon)
    rows = g.shape[0]
    diagonal = lax.broadcasted_iota(jnp.int32, (rows, rows), 0) == lax.broadcasted_iota(
        jnp.int32, (rows, rows), 1
    )
    for c in CENTRES:
        xb = x.astype(BF16)
        e = dot(xb, xb, ((1,), (1,)))
        if c:
            e = e - jnp.where(diagonal, c, 0.0)
        eb = e.astype(BF16)
        mix = (coef_second + 2.0 * c * coef_third) * e + coef_third * dot(eb, eb)
        k = coef_first + coef_second * c + coef_third * c * c
        x = k * x + dot(mix.astype(BF16), xb)
    out[...] = (old.astype(F32) + step_ref[0] * x).astype(BF16)


def update(place, step, pieces, olds, mib):
    matrix = pieces[0].shape
    smem = pl.BlockSpec(memory_space=pltpu.SMEM)
    vmem = pl.BlockSpec(memory_space=pltpu.VMEM)
    return pl.pallas_call(
        update_kernel,
        in_specs=[smem, smem] + [vmem] * (4 + len(olds)),
        out_specs=vmem,
        out_shape=jax.ShapeDtypeStruct(matrix, BF16),
        compiler_params=params(mib),
        cost_estimate=pl.CostEstimate(
            flops=5 * 2 * 5 * matrix[0] * matrix[0] * matrix[0],
            bytes_accessed=16 * matrix[0] * matrix[1],
            transcendentals=0,
        ),
    )(place, step, *pieces, *olds)


def attend_kernel(blocks, kb_first, first_ref, q_ref, k_ref, v_ref, *rest):
    if kb_first is None:
        (out, k_nat) = rest
        rims = ()
    else:
        (rim, _, out, k_nat) = rest
        width = q_ref.shape[0]
        rims = (rim.at[:width], rim.at[width:])
    step = pl.program_id(0)
    heads = q_ref.shape[0] // ATT_DIM
    chunks = WINDOW // QB + 1
    rim_blocks = WINDOW // QB if rims else 0

    @pl.when(step == 0)
    def _():
        if rims:
            for h in range(heads):
                k_nat[h, :WINDOW, :] = rims[0][pl.ds(h * ATT_DIM, ATT_DIM), :].T
        for h in range(heads):
            k_nat[h, rim_blocks * QB :, :] = k_ref[pl.ds(h * ATT_DIM, ATT_DIM), :].T

    later = lax.broadcasted_iota(jnp.int32, (QB, QB), 0) > lax.broadcasted_iota(
        jnp.int32, (QB, QB), 1
    )
    scale = LOG2E / math.sqrt(ATT_DIM)
    low = -1e30

    def values(h, block):
        return v_ref[pl.ds(h * ATT_DIM, ATT_DIM), pl.ds(pl.multiple_of(block * QB, QB), QB)]

    def body(i, fresh):
        for h in range(heads):
            q = q_ref[pl.ds(h * ATT_DIM, ATT_DIM), :]
            s = []
            for c in range(chunks):
                k = k_nat[h, pl.ds(pl.multiple_of((i + c) * QB, QB), QB), :]
                part = dot(k, q)
                if c == 0:
                    part = jnp.where(later, part, low)
                elif c == chunks - 1:
                    part = jnp.where(later, low, part)
                if c < fresh:
                    part = jnp.where(first_ref[0] == 1, low, part)
                s.append(part)
            top = functools.reduce(
                jnp.maximum, [jnp.max(part, axis=0, keepdims=True) for part in s]
            )
            total = jnp.zeros((1, QB), F32)
            result = jnp.zeros((ATT_DIM, QB), F32)
            for c in range(chunks):
                expo = jnp.exp2((s[c] - top) * scale)
                total += jnp.sum(expo, axis=0, keepdims=True)
                if c < fresh:
                    v = rims[1][pl.ds(h * ATT_DIM, ATT_DIM), pl.ds((i + c) * QB, QB)]
                else:
                    v = values(h, i + c - rim_blocks)
                result += dot(v, expo.astype(BF16))
            out[pl.ds(h * ATT_DIM, ATT_DIM), :] = result / total

    if rims:
        for i in range(blocks):

            @pl.when(step == i)
            def _(i=i):
                body(i, max(rim_blocks - i, 0))
    else:
        body(step + LED - (chunks - 1), 0)


def attend_main(qt, kt, vt, first):
    width, count = qt.shape
    skip = LED
    blocks = count // QB - skip
    heads = width // ATT_DIM
    whole = pl.BlockSpec((width, count), lambda i, f: (0, 0))
    return pl.pallas_call(
        functools.partial(attend_kernel, blocks, None),
        grid_spec=pltpu.PrefetchScalarGridSpec(
            num_scalar_prefetch=1,
            grid=(blocks,),
            in_specs=[pl.BlockSpec((width, QB), lambda i, f: (0, i + skip)), whole, whole],
            out_specs=pl.BlockSpec((width, QB), lambda i, f: (0, i + skip)),
            scratch_shapes=[pltpu.VMEM((heads, count, ATT_DIM), BF16)],
        ),
        out_shape=jax.ShapeDtypeStruct((width, count), F32),
        compiler_params=params(56),
        cost_estimate=pl.CostEstimate(
            flops=4 * blocks * QB * (WINDOW + QB) * width,
            bytes_accessed=10 * width * count,
            transcendentals=blocks * QB * (WINDOW + QB) * heads,
        ),
    )(first, qt, kt, vt)


def attend_rim(qt, kt, vt, rim, main, first):
    width = qt.shape[0]
    blocks = LED
    heads = width // ATT_DIM
    whole = pl.BlockSpec((width, LED * QB), lambda i, f: (0, 0))
    return pl.pallas_call(
        functools.partial(attend_kernel, blocks, 0),
        grid_spec=pltpu.PrefetchScalarGridSpec(
            num_scalar_prefetch=1,
            grid=(blocks,),
            in_specs=[pl.BlockSpec((width, QB), lambda i, f: (0, i))] + [whole] * 2
            + [
                pl.BlockSpec(rim.shape, lambda i, f: (0, 0)),
                pl.BlockSpec(memory_space=pl.ANY),
            ],
            out_specs=pl.BlockSpec((width, QB), lambda i, f: (0, i)),
            scratch_shapes=[pltpu.VMEM((heads, WINDOW + LED * QB, ATT_DIM), BF16)],
        ),
        out_shape=jax.ShapeDtypeStruct(main.shape, F32),
        input_output_aliases={5: 0},
        compiler_params=params(56),
        cost_estimate=pl.CostEstimate(
            flops=4 * blocks * QB * (WINDOW + QB) * width,
            bytes_accessed=16 * width * WINDOW,
            transcendentals=blocks * QB * (WINDOW + QB) * heads,
        ),
    )(first, qt, kt, vt, rim, main)


def pack(rows, out, dests):
    n = rows.shape[0] // (2 * dests)
    width = rows.shape[1]
    for d in range(dests):
        begin = 2 * n * d
        out[d] = jnp.concatenate([rows[begin : begin + n], rows[begin + n : begin + 2 * n]], 1)


def apply_kernel(dests, place_ref, part_ref, q_ref, att_ref, *rest):
    sources, out, (wt, w2) = rest[: 2 * RING], rest[2 * RING], rest[2 * RING + 1 :]

    @pl.when(pl.program_id(0) == 0)
    def _():
        def put(j, w):
            if j < 2:
                wt[j] = (w * 0.5 if j == 0 else w).T
            else:
                w2[...] = w

        for part in range(2):

            @pl.when(part_ref[0] == part)
            def _(part=part):
                pick_weights(place_ref[0], sources[part * RING : (part + 1) * RING], put)

    q = q_ref[...]
    half = dot(wt[0], q)
    up = dot(wt[1], q)
    hidden = (half * (1.0 + jnp.tanh(half)) * up).astype(BF16)
    fast = dot(w2[...], hidden)
    pack((fast + att_ref[...]).astype(BF16).T, out, dests)


def apply_mix(place, part, qt, att, early, late, parts_out):
    width, count = qt.shape
    matrix = early[0].shape
    rows = count // parts_out
    dests = 4
    tokens = pl.BlockSpec((width, dests * rows), lambda i, p, g: (0, i))
    return pl.pallas_call(
        functools.partial(apply_kernel, dests),
        grid_spec=pltpu.PrefetchScalarGridSpec(
            num_scalar_prefetch=2,
            grid=(parts_out // dests,),
            in_specs=[tokens, tokens] + [pl.BlockSpec(matrix, lambda i, p, g: (0, 0))] * 8,
            out_specs=pl.BlockSpec((dests, rows // 2, 2 * width), lambda i, p, g: (i, 0, 0)),
            scratch_shapes=[
                pltpu.VMEM((2, matrix[1], width), BF16),
                pltpu.VMEM(matrix, BF16),
            ],
        ),
        out_shape=jax.ShapeDtypeStruct((parts_out, rows // 2, 2 * width), BF16),
        compiler_params=params(56),
        cost_estimate=pl.CostEstimate(
            flops=6 * width * matrix[1] * count,
            bytes_accessed=8 * width * count,
            transcendentals=matrix[1] * count,
        ),
    )(place, part, qt, att, *early, *late)


def gate_kernel(dests, g_ref, out):
    pack(g_ref[...].T, out, dests)


def pack_gate(gt, parts_out):
    width, count = gt.shape
    rows = count // parts_out
    dests = 4
    return pl.pallas_call(
        functools.partial(gate_kernel, dests),
        grid=(parts_out // dests,),
        in_specs=[pl.BlockSpec((width, dests * rows), lambda i: (0, i))],
        out_specs=pl.BlockSpec((dests, rows // 2, 2 * width), lambda i: (i, 0, 0)),
        out_shape=jax.ShapeDtypeStruct((parts_out, rows // 2, 2 * width), BF16),
        compiler_params=params(56),
        cost_estimate=pl.CostEstimate(
            flops=0, bytes_accessed=8 * width * count, transcendentals=0
        ),
    )(gt)


def final_kernel(m_ref, g_ref, gain_ref, out):
    heads, rows, double = m_ref.shape
    width = double // 2
    squares = jnp.zeros((rows, double), F32)
    for h in range(heads):
        m = m_ref[h].astype(F32)
        squares += m * m
    left = lax.broadcasted_iota(jnp.int32, (1, double), 1) < width
    mean = 1.0 / (heads * width)
    early = lax.rsqrt(jnp.sum(squares[:, :width], 1, keepdims=True) * mean + epsilon)
    late = lax.rsqrt(jnp.sum(squares[:, width:], 1, keepdims=True) * mean + epsilon)
    factor = jnp.where(left, early, late)
    for h in range(0, heads, 2):
        pair = []
        for j in (h, h + 1):
            g = g_ref[j].astype(F32)
            scale = factor * gain_ref[j : j + 1]
            pair.append((m_ref[j].astype(F32) * scale * (g * sigmoid(g))).astype(BF16))
        cols = slice(h * width, (h + 2) * width)
        out[0, :, cols] = jnp.concatenate([y[:, :width] for y in pair], 1)
        out[1, :, cols] = jnp.concatenate([y[:, width:] for y in pair], 1)


def final(mixed, gates, gain):
    heads, rows, double = mixed.shape
    block = FINAL_ROWS
    wide = heads * double // 2
    gain = gain.reshape(heads, double // 2)
    tokens = pl.BlockSpec((heads, block, double), lambda i: (0, i, 0))
    result = pl.pallas_call(
        final_kernel,
        grid=(rows // block,),
        in_specs=[tokens, tokens, pl.BlockSpec((heads, double), lambda i: (0, 0))],
        out_specs=pl.BlockSpec((2, block, wide), lambda i: (0, i, 0)),
        out_shape=jax.ShapeDtypeStruct((2, rows, wide), BF16),
        compiler_params=params(48),
        cost_estimate=pl.CostEstimate(
            flops=20 * rows * wide, bytes_accessed=12 * rows * wide, transcendentals=2 * rows * wide
        ),
    )(mixed, gates, jnp.concatenate([gain, gain], 1))
    return result.reshape(2 * rows, wide)


def reduce_moves(part):
    return [[(part, (m - s) % RING, part, m) for m in range(3)] for s in range(1, RING)]


def spread_moves(parts):
    return [[(p, m, p, (m + s) % RING) for p in parts for m in range(3)] for s in range(1, RING)]


def ring_send(array, moves):
    heads = lax.axis_size("head")

    def index(part, place, head):
        return (part * RING + (place + 2 * (head % 2)) % RING) * heads + head

    pairs = [(index(a, b, h), index(c, d, h)) for a, b, c, d in moves for h in range(heads)]
    return lax.ppermute(array, ("ctx", "head"), pairs)


def send(array, pairs):
    return lax.ppermute(array, "ctx", pairs)


def shards(
    query_rows,
    key_rows,
    value_rows,
    gate_rows,
    token_rates,
    step_sizes,
    fast_first,
    fast_third,
    fast_second,
    norm_gain,
):
    ctx = lax.axis_index("ctx")
    heads = lax.axis_size("head")
    place = ((ctx + 2 * (lax.axis_index("head") % 2)) % RING).reshape(1).astype(jnp.int32)
    part = (ctx // RING).reshape(1).astype(jnp.int32)
    first = (ctx == 0).reshape(1).astype(jnp.int32)
    qt, kt, vt, gt = query_rows.T, key_rows.T, value_rows.T, gate_rows.T
    start = [fast_first[0], fast_third[0], fast_second[0].T]
    hold = lax.optimization_barrier

    own, *out = grads(place, kt, vt, token_rates, start, True)
    out, tail = out[:3], out[3]
    pieces = [own] + [ring_send(o, p) for o, p in zip(out, reduce_moves(0))]
    rim_late = send(tail, [(i, i + 1) for i in range(4, 7)])
    att_main = attend_main(qt, kt, vt, first)
    pieces, att_main = hold((pieces, att_main))
    fresh = update(place, step_sizes, pieces, start, 12)
    fresh, gt = hold((fresh, gt))
    crossed = ring_send(fresh, [(0, m, 1, m) for m in range(3)])
    gates = pack_gate(gt, heads)
    held = jnp.where(part[0] == 0, fresh, crossed)
    held, gates, rim_late = hold((held, gates, rim_late))
    gate_tokens = lax.all_to_all(gates, "head", split_axis=0, concat_axis=0)
    early = [held] + [ring_send(held, p) for p in spread_moves((0, 1))]
    early[1], tail = hold((early[1], tail))
    rim_early = send(tail, [(i, i + 1) for i in range(4)])

    own, *out = grads(place, kt, vt, token_rates, early, False)
    pieces = [own] + [ring_send(o, p) for o, p in zip(out, reduce_moves(1))]
    fresh = update(place, step_sizes, pieces, [early[0]], 56)
    fresh, att_main = hold((fresh, att_main))
    late = [fresh] + [ring_send(fresh, p) for p in spread_moves((1,))]
    att = attend_rim(qt, kt, vt, jnp.where(ctx <= RING, rim_early, rim_late), att_main, first)
    att, gate_tokens = hold((att, gate_tokens))
    mixed = apply_mix(place, part, qt, att, early, late, heads)
    mixed_tokens = lax.all_to_all(mixed, "head", split_axis=0, concat_axis=0)
    return final(mixed_tokens, gate_tokens, norm_gain)


def solution(mesh):
    placed = (
        P("ctx", "head"),
        P("ctx", "head"),
        P("ctx", "head"),
        P("ctx", "head"),
        P("head", "ctx"),
        P("head"),
        P("head", None, None),
        P("head", None, None),
        P("head", None, None),
        P(),
    )
    return jax.shard_map(
        shards, mesh=mesh, in_specs=placed, out_specs=P(("ctx", "head"), None), check_vma=False
    )
```

```python
import functools
import math

import jax
import jax.numpy as jnp
from jax import lax
from jax.experimental import pallas as pl
from jax.experimental.pallas import tpu as pltpu
from jax.sharding import PartitionSpec as P

ATT_DIM = 160
WINDOW = 1024
RING = 4
QB = 256
TB = 1536
SB = 512
LED = WINDOW // QB + 1
FINAL_ROWS = 32

coef_first = 3.4445
coef_second = -4.775
coef_third = 2.0315
epsilon = 1e-06
LOG2E = 1.4426950408889634
CENTRES = (0.0, 0.0, 0.5, 0.8, 0.8)
F32 = jnp.float32
BF16 = jnp.bfloat16
MIB = 1024 * 1024


def params(mib):
    return pltpu.CompilerParams(vmem_limit_bytes=mib * MIB)


def dot(a, b, dims=((1,), (0,))):
    return lax.dot_general(a, b, (dims, ((), ())), preferred_element_type=F32)


def sigmoid(x):
    return 0.5 * jnp.tanh(0.5 * x) + 0.5


def pick_weights(place, sources, put):
    for j in range(3):
        for s in range(RING):

            @pl.when(lax.rem(place + RING - j, RING) == s)
            def _(j=j, s=s):
                put(j, sources[s][...])


def grads_kernel(static, place_ref, x_ref, v_ref, r_ref, *rest):
    n_src = 3 if static else RING
    sources, outs, rest = rest[:n_src], rest[n_src : n_src + 4], rest[n_src + 4 :]
    acc, wt, d_gate, d_up, hidden, scaled = rest[-6:]
    step = pl.program_id(0)
    last = pl.num_programs(0) - 1
    place = place_ref[0]
    width, count = x_ref.shape

    @pl.when(step == 0)
    def _():
        def put(j, w):
            wt[j] = (w * 0.5 if j == 0 else w).T

        if static:
            for j in range(3):
                put(j, sources[j][...])
        else:
            pick_weights(place, sources, put)
        acc[...] = jnp.zeros_like(acc)

    def forward(span):
        x = x_ref[:, span]
        e = (r_ref[:, span] * v_ref[:, span].astype(F32)).astype(BF16)
        scaled[:, span] = e
        half = dot(wt[0], x)
        up = dot(wt[1], x)
        back = dot(wt[2], e)
        both = 1.0 + jnp.tanh(half)
        gated = half * both
        slope = both * (half + half + 1.0 - gated)
        hidden[:, span] = (gated * up).astype(BF16)
        d_up[:, span] = (back * gated).astype(BF16)
        d_gate[:, span] = (back * up * slope).astype(BF16)

    def backward(span):
        nt = ((1,), (1,))
        x = x_ref[:, span]
        acc[0] += dot(x, d_gate[:, span], nt)
        acc[1] += dot(x, d_up[:, span], nt)
        acc[2] += dot(scaled[:, span], hidden[:, span], nt)

    spans = [slice(b, b + SB) for b in range(0, count, SB)]
    for i, span in enumerate(spans):
        forward(span)
        if i:
            backward(spans[i - 1])
    backward(spans[-1])

    @pl.when(step == last)
    def _():
        if static:
            rim = slice(count - WINDOW, count)
            rest[0][:width] = x_ref[:, rim]
            rest[0][width:] = v_ref[:, rim]
        for shift, out in enumerate(outs):
            j = jnp.minimum(lax.rem(place + shift, RING), 2)
            out[...] = (acc[j] * jnp.where(j == 0, 0.5, 1.0)).astype(BF16)


def grads(place, xt, vt, rates, sources, static):
    width, count = xt.shape
    matrix = sources[0].shape
    whole = pl.BlockSpec(matrix, lambda i, p: (0, 0))
    tokens = pl.BlockSpec((width, TB), lambda i, p: (0, i))
    hidden = matrix[1]
    rim = (2 * width, WINDOW)
    return pl.pallas_call(
        functools.partial(grads_kernel, static),
        grid_spec=pltpu.PrefetchScalarGridSpec(
            num_scalar_prefetch=1,
            grid=(count // TB,),
            in_specs=[tokens, tokens, pl.BlockSpec((1, TB), lambda i, p: (0, i))]
            + [whole] * len(sources),
            out_specs=[whole] * 4 + ([pl.BlockSpec(rim, lambda i, p: (0, 0))] if static else []),
            scratch_shapes=[
                pltpu.VMEM((3,) + matrix, F32),
                pltpu.VMEM((3, hidden, width), BF16),
            ]
            + [pltpu.VMEM((hidden, TB), BF16)] * 3
            + [pltpu.VMEM((width, TB), BF16)],
        ),
        out_shape=[jax.ShapeDtypeStruct(matrix, BF16)] * 4
        + ([jax.ShapeDtypeStruct(rim, BF16)] if static else []),
        compiler_params=params(56),
        cost_estimate=pl.CostEstimate(
            flops=12 * width * hidden * count,
            bytes_accessed=4 * width * count,
            transcendentals=hidden * count,
        ),
    )(place, xt, vt, rates, *sources)


def update_kernel(place_ref, step_ref, own, r1, r2, r3, *rest):
    olds, out = rest[:-1], rest[-1]
    place = place_ref[0]
    if len(olds) == 3:
        old = jnp.where(
            place == 0, olds[0][...], jnp.where(place == 1, olds[1][...], olds[2][...])
        )
    else:
        old = olds[0][...]
    g = own[...].astype(F32) + r1[...].astype(F32) + r2[...].astype(F32) + r3[...].astype(F32)
    x = g * lax.rsqrt(jnp.sum(g * g) + epsilon)
    rows = g.shape[0]
    diagonal = lax.broadcasted_iota(jnp.int32, (rows, rows), 0) == lax.broadcasted_iota(
        jnp.int32, (rows, rows), 1
    )
    for c in CENTRES:
        xb = x.astype(BF16)
        e = dot(xb, xb, ((1,), (1,)))
        if c:
            e = e - jnp.where(diagonal, c, 0.0)
        eb = e.astype(BF16)
        mix = (coef_second + 2.0 * c * coef_third) * e + coef_third * dot(eb, eb)
        k = coef_first + coef_second * c + coef_third * c * c
        x = k * x + dot(mix.astype(BF16), xb)
    out[...] = (old.astype(F32) + step_ref[0] * x).astype(BF16)


def update(place, step, pieces, olds, mib):
    matrix = pieces[0].shape
    smem = pl.BlockSpec(memory_space=pltpu.SMEM)
    vmem = pl.BlockSpec(memory_space=pltpu.VMEM)
    return pl.pallas_call(
        update_kernel,
        in_specs=[smem, smem] + [vmem] * (4 + len(olds)),
        out_specs=vmem,
        out_shape=jax.ShapeDtypeStruct(matrix, BF16),
        compiler_params=params(mib),
        cost_estimate=pl.CostEstimate(
            flops=5 * 2 * 5 * matrix[0] * matrix[0] * matrix[0],
            bytes_accessed=16 * matrix[0] * matrix[1],
            transcendentals=0,
        ),
    )(place, step, *pieces, *olds)


def attend_kernel(blocks, kb_first, first_ref, q_ref, k_ref, v_ref, *rest):
    if kb_first is None:
        (out, k_nat) = rest
        rims = ()
    else:
        (rim, _, out, k_nat) = rest
        width = q_ref.shape[0]
        rims = (rim.at[:width], rim.at[width:])
    step = pl.program_id(0)
    heads = q_ref.shape[0] // ATT_DIM
    chunks = WINDOW // QB + 1
    rim_blocks = WINDOW // QB if rims else 0

    @pl.when(step == 0)
    def _():
        if rims:
            for h in range(heads):
                k_nat[h, :WINDOW, :] = rims[0][pl.ds(h * ATT_DIM, ATT_DIM), :].T
        for h in range(heads):
            k_nat[h, rim_blocks * QB :, :] = k_ref[pl.ds(h * ATT_DIM, ATT_DIM), :].T

    later = lax.broadcasted_iota(jnp.int32, (QB, QB), 0) > lax.broadcasted_iota(
        jnp.int32, (QB, QB), 1
    )
    scale = LOG2E / math.sqrt(ATT_DIM)
    low = -1e30

    def values(h, block):
        return v_ref[pl.ds(h * ATT_DIM, ATT_DIM), pl.ds(pl.multiple_of(block * QB, QB), QB)]

    def body(i, fresh):
        for h in range(heads):
            q = q_ref[pl.ds(h * ATT_DIM, ATT_DIM), :]
            s = []
            for c in range(chunks):
                k = k_nat[h, pl.ds(pl.multiple_of((i + c) * QB, QB), QB), :]
                part = dot(k, q)
                if c == 0:
                    part = jnp.where(later, part, low)
                elif c == chunks - 1:
                    part = jnp.where(later, low, part)
                if c < fresh:
                    part = jnp.where(first_ref[0] == 1, low, part)
                s.append(part)
            top = functools.reduce(
                jnp.maximum, [jnp.max(part, axis=0, keepdims=True) for part in s]
            )
            total = jnp.zeros((1, QB), F32)
            result = jnp.zeros((ATT_DIM, QB), F32)
            for c in range(chunks):
                expo = jnp.exp2((s[c] - top) * scale)
                total += jnp.sum(expo, axis=0, keepdims=True)
                if c < fresh:
                    v = rims[1][pl.ds(h * ATT_DIM, ATT_DIM), pl.ds((i + c) * QB, QB)]
                else:
                    v = values(h, i + c - rim_blocks)
                result += dot(v, expo.astype(BF16))
            out[pl.ds(h * ATT_DIM, ATT_DIM), :] = result / total

    if rims:
        for i in range(blocks):

            @pl.when(step == i)
            def _(i=i):
                body(i, max(rim_blocks - i, 0))
    else:
        body(step + LED - (chunks - 1), 0)


def attend_main(qt, kt, vt, first):
    width, count = qt.shape
    skip = LED
    blocks = count // QB - skip
    heads = width // ATT_DIM
    whole = pl.BlockSpec((width, count), lambda i, f: (0, 0))
    return pl.pallas_call(
        functools.partial(attend_kernel, blocks, None),
        grid_spec=pltpu.PrefetchScalarGridSpec(
            num_scalar_prefetch=1,
            grid=(blocks,),
            in_specs=[pl.BlockSpec((width, QB), lambda i, f: (0, i + skip)), whole, whole],
            out_specs=pl.BlockSpec((width, QB), lambda i, f: (0, i + skip)),
            scratch_shapes=[pltpu.VMEM((heads, count, ATT_DIM), BF16)],
        ),
        out_shape=jax.ShapeDtypeStruct((width, count), F32),
        compiler_params=params(56),
        cost_estimate=pl.CostEstimate(
            flops=4 * blocks * QB * (WINDOW + QB) * width,
            bytes_accessed=10 * width * count,
            transcendentals=blocks * QB * (WINDOW + QB) * heads,
        ),
    )(first, qt, kt, vt)


def attend_rim(qt, kt, vt, rim, main, first):
    width = qt.shape[0]
    blocks = LED
    heads = width // ATT_DIM
    whole = pl.BlockSpec((width, LED * QB), lambda i, f: (0, 0))
    return pl.pallas_call(
        functools.partial(attend_kernel, blocks, 0),
        grid_spec=pltpu.PrefetchScalarGridSpec(
            num_scalar_prefetch=1,
            grid=(blocks,),
            in_specs=[pl.BlockSpec((width, QB), lambda i, f: (0, i))] + [whole] * 2
            + [
                pl.BlockSpec(rim.shape, lambda i, f: (0, 0)),
                pl.BlockSpec(memory_space=pl.ANY),
            ],
            out_specs=pl.BlockSpec((width, QB), lambda i, f: (0, i)),
            scratch_shapes=[pltpu.VMEM((heads, WINDOW + LED * QB, ATT_DIM), BF16)],
        ),
        out_shape=jax.ShapeDtypeStruct(main.shape, F32),
        input_output_aliases={5: 0},
        compiler_params=params(56),
        cost_estimate=pl.CostEstimate(
            flops=4 * blocks * QB * (WINDOW + QB) * width,
            bytes_accessed=16 * width * WINDOW,
            transcendentals=blocks * QB * (WINDOW + QB) * heads,
        ),
    )(first, qt, kt, vt, rim, main)


def pack(rows, out, dests):
    n = rows.shape[0] // (2 * dests)
    width = rows.shape[1]
    for d in range(dests):
        begin = 2 * n * d
        out[d] = jnp.concatenate([rows[begin : begin + n], rows[begin + n : begin + 2 * n]], 1)


def apply_kernel(dests, place_ref, part_ref, q_ref, att_ref, *rest):
    sources, out, (wt, w2) = rest[: 2 * RING], rest[2 * RING], rest[2 * RING + 1 :]

    @pl.when(pl.program_id(0) == 0)
    def _():
        def put(j, w):
            if j < 2:
                wt[j] = (w * 0.5 if j == 0 else w).T
            else:
                w2[...] = w

        for part in range(2):

            @pl.when(part_ref[0] == part)
            def _(part=part):
                pick_weights(place_ref[0], sources[part * RING : (part + 1) * RING], put)

    q = q_ref[...]
    half = dot(wt[0], q)
    up = dot(wt[1], q)
    hidden = (half * (1.0 + jnp.tanh(half)) * up).astype(BF16)
    fast = dot(w2[...], hidden)
    pack((fast + att_ref[...]).astype(BF16).T, out, dests)


def apply_mix(place, part, qt, att, early, late, parts_out):
    width, count = qt.shape
    matrix = early[0].shape
    rows = count // parts_out
    dests = 4
    tokens = pl.BlockSpec((width, dests * rows), lambda i, p, g: (0, i))
    return pl.pallas_call(
        functools.partial(apply_kernel, dests),
        grid_spec=pltpu.PrefetchScalarGridSpec(
            num_scalar_prefetch=2,
            grid=(parts_out // dests,),
            in_specs=[tokens, tokens] + [pl.BlockSpec(matrix, lambda i, p, g: (0, 0))] * 8,
            out_specs=pl.BlockSpec((dests, rows // 2, 2 * width), lambda i, p, g: (i, 0, 0)),
            scratch_shapes=[
                pltpu.VMEM((2, matrix[1], width), BF16),
                pltpu.VMEM(matrix, BF16),
            ],
        ),
        out_shape=jax.ShapeDtypeStruct((parts_out, rows // 2, 2 * width), BF16),
        compiler_params=params(56),
        cost_estimate=pl.CostEstimate(
            flops=6 * width * matrix[1] * count,
            bytes_accessed=8 * width * count,
            transcendentals=matrix[1] * count,
        ),
    )(place, part, qt, att, *early, *late)


def gate_kernel(dests, g_ref, out):
    pack(g_ref[...].T, out, dests)


def pack_gate(gt, parts_out):
    width, count = gt.shape
    rows = count // parts_out
    dests = 4
    return pl.pallas_call(
        functools.partial(gate_kernel, dests),
        grid=(parts_out // dests,),
        in_specs=[pl.BlockSpec((width, dests * rows), lambda i: (0, i))],
        out_specs=pl.BlockSpec((dests, rows // 2, 2 * width), lambda i: (i, 0, 0)),
        out_shape=jax.ShapeDtypeStruct((parts_out, rows // 2, 2 * width), BF16),
        compiler_params=params(56),
        cost_estimate=pl.CostEstimate(
            flops=0, bytes_accessed=8 * width * count, transcendentals=0
        ),
    )(gt)


def final_kernel(m_ref, g_ref, gain_ref, out):
    heads, rows, double = m_ref.shape
    width = double // 2
    squares = jnp.zeros((rows, double), F32)
    for h in range(heads):
        m = m_ref[h].astype(F32)
        squares += m * m
    left = lax.broadcasted_iota(jnp.int32, (1, double), 1) < width
    mean = 1.0 / (heads * width)
    early = lax.rsqrt(jnp.sum(squares[:, :width], 1, keepdims=True) * mean + epsilon)
    late = lax.rsqrt(jnp.sum(squares[:, width:], 1, keepdims=True) * mean + epsilon)
    factor = jnp.where(left, early, late)
    for h in range(0, heads, 2):
        pair = []
        for j in (h, h + 1):
            g = g_ref[j].astype(F32)
            scale = factor * gain_ref[j : j + 1]
            pair.append((m_ref[j].astype(F32) * scale * (g * sigmoid(g))).astype(BF16))
        cols = slice(h * width, (h + 2) * width)
        out[0, :, cols] = jnp.concatenate([y[:, :width] for y in pair], 1)
        out[1, :, cols] = jnp.concatenate([y[:, width:] for y in pair], 1)


def final(mixed, gates, gain):
    heads, rows, double = mixed.shape
    block = FINAL_ROWS
    wide = heads * double // 2
    gain = gain.reshape(heads, double // 2)
    tokens = pl.BlockSpec((heads, block, double), lambda i: (0, i, 0))
    result = pl.pallas_call(
        final_kernel,
        grid=(rows // block,),
        in_specs=[tokens, tokens, pl.BlockSpec((heads, double), lambda i: (0, 0))],
        out_specs=pl.BlockSpec((2, block, wide), lambda i: (0, i, 0)),
        out_shape=jax.ShapeDtypeStruct((2, rows, wide), BF16),
        compiler_params=params(48),
        cost_estimate=pl.CostEstimate(
            flops=20 * rows * wide, bytes_accessed=12 * rows * wide, transcendentals=2 * rows * wide
        ),
    )(mixed, gates, jnp.concatenate([gain, gain], 1))
    return result.reshape(2 * rows, wide)


def reduce_moves(part):
    return [[(part, (m - s) % RING, part, m) for m in range(3)] for s in range(1, RING)]


def spread_moves(parts):
    return [[(p, m, p, (m + s) % RING) for p in parts for m in range(3)] for s in range(1, RING)]


def ring_send(array, moves):
    heads = lax.axis_size("head")

    def index(part, place, head):
        return (part * RING + (place + 2 * (head % 2)) % RING) * heads + head

    pairs = [(index(a, b, h), index(c, d, h)) for a, b, c, d in moves for h in range(heads)]
    return lax.ppermute(array, ("ctx", "head"), pairs)


def send(array, pairs):
    return lax.ppermute(array, "ctx", pairs)


def shards(
    query_rows,
    key_rows,
    value_rows,
    gate_rows,
    token_rates,
    step_sizes,
    fast_first,
    fast_third,
    fast_second,
    norm_gain,
):
    ctx = lax.axis_index("ctx")
    heads = lax.axis_size("head")
    place = ((ctx + 2 * (lax.axis_index("head") % 2)) % RING).reshape(1).astype(jnp.int32)
    part = (ctx // RING).reshape(1).astype(jnp.int32)
    first = (ctx == 0).reshape(1).astype(jnp.int32)
    qt, kt, vt, gt = query_rows.T, key_rows.T, value_rows.T, gate_rows.T
    start = [fast_first[0], fast_third[0], fast_second[0].T]
    hold = lax.optimization_barrier

    own, *out = grads(place, kt, vt, token_rates, start, True)
    out, tail = out[:3], out[3]
    pieces = [own] + [ring_send(o, p) for o, p in zip(out, reduce_moves(0))]
    rim_late = send(tail, [(i, i + 1) for i in range(4, 7)])
    att_main = attend_main(qt, kt, vt, first)
    pieces, att_main = hold((pieces, att_main))
    fresh = update(place, step_sizes, pieces, start, 56)
    fresh, gt = hold((fresh, gt))
    crossed = ring_send(fresh, [(0, m, 1, m) for m in range(3)])
    gates = pack_gate(gt, heads)
    held = jnp.where(part[0] == 0, fresh, crossed)
    held, gates, rim_late = hold((held, gates, rim_late))
    gate_tokens = lax.all_to_all(gates, "head", split_axis=0, concat_axis=0)
    early = [held] + [ring_send(held, p) for p in spread_moves((0, 1))]
    early[1], tail = hold((early[1], tail))
    rim_early = send(tail, [(i, i + 1) for i in range(4)])

    own, *out = grads(place, kt, vt, token_rates, early, False)
    pieces = [own] + [ring_send(o, p) for o, p in zip(out, reduce_moves(1))]
    fresh = update(place, step_sizes, pieces, [early[0]], 56)
    fresh, att_main = hold((fresh, att_main))
    late = [fresh] + [ring_send(fresh, p) for p in spread_moves((1,))]
    att = attend_rim(qt, kt, vt, jnp.where(ctx <= RING, rim_early, rim_late), att_main, first)
    att, gate_tokens = hold((att, gate_tokens))
    mixed = apply_mix(place, part, qt, att, early, late, heads)
    mixed_tokens = lax.all_to_all(mixed, "head", split_axis=0, concat_axis=0)
    return final(mixed_tokens, gate_tokens, norm_gain)


def solution(mesh):
    placed = (
        P("ctx", "head"),
        P("ctx", "head"),
        P("ctx", "head"),
        P("ctx", "head"),
        P("head", "ctx"),
        P("head"),
        P("head", None, None),
        P("head", None, None),
        P("head", None, None),
        P(),
    )
    return jax.shard_map(
        shards, mesh=mesh, in_specs=placed, out_specs=P(("ctx", "head"), None), check_vma=False
    )
```
